32 devices in a mesh: dp: 8 (over z, y), mp: 4 (over x, core).
Axes of the slice: x: 2, y: 2, z: 4, core: 2. Of those that a mesh axis runs over, the one named last changes fastest.
Arguments:
- tokens: bfloat16 [8, 2048, 768], P('dp'), may hold values from -6 to 6
- cotangent: bfloat16 [8, 2048, 768], P('dp'), may hold values from -6 to 6
- capacity: int32 [8], replicated, may hold values from 256 to 1024, as said below
- selected: int32 [8, 1024], P('dp'), may hold values from 0 to 2047, as said below
- qkv_master: float32 [3, 768, 768], P(None, 'dp', 'mp'), may hold values from -0.21875 to 0.21875
- out_master: float32 [768, 768], P('mp', 'dp'), may hold values from -0.75 to 0.75
- up_master: float32 [768, 3072], P('dp', 'mp'), may hold values from -0.21875 to 0.21875
- down_master: float32 [3072, 768], P('mp', 'dp'), may hold values from -0.109375 to 0.109375
- vec_master: float32 [3, 768], P(None, 'dp')
- qkv_first: float32 [3, 768, 768], P(None, 'dp', 'mp'), may hold values from -48 to 48
- out_first: float32 [768, 768], P('mp', 'dp'), may hold values from -6 to 6
- up_first: float32 [768, 3072], P('dp', 'mp'), may hold values from -6 to 6
- down_first: float32 [3072, 768], P('mp', 'dp'), may hold values from -16 to 16
- vec_first: float32 [3, 768], P(None, 'dp')
- qkv_second: float32 [3, 768, 768], P(None, 'dp', 'mp'), may hold values from 127.7952 to 2064.384
- out_second: float32 [768, 768], P('mp', 'dp'), may hold values from 5.111808 to 82.57536
- up_second: float32 [768, 3072], P('dp', 'mp'), may hold values from 1.8402508 to 29.727129
- down_second: float32 [3072, 768], P('mp', 'dp'), may hold values from 14.057472 to 227.08224
- vec_second: float32 [3, 768], P(None, 'dp')
Outputs:
- block_out: bfloat16 [8, 2048, 768], P('dp')
- input_grad: float32 [8, 2048, 768], P('dp')
- qkv_new: float32 [3, 768, 768], P(None, 'dp', 'mp')
- out_new: float32 [768, 768], P('mp', 'dp')
- up_new: float32 [768, 3072], P('dp', 'mp')
- down_new: float32 [3072, 768], P('mp', 'dp')
- vec_new: float32 [3, 768], P(None, 'dp')
- qkv_first_new: float32 [3, 768, 768], P(None, 'dp', 'mp')
- out_first_new: float32 [768, 768], P('mp', 'dp')
- up_first_new: float32 [768, 3072], P('dp', 'mp')
- down_first_new: float32 [3072, 768], P('mp', 'dp')
- vec_first_new: float32 [3, 768], P(None, 'dp')
- qkv_second_new: float32 [3, 768, 768], P(None, 'dp', 'mp')
- out_second_new: float32 [768, 768], P('mp', 'dp')
- up_second_new: float32 [768, 3072], P('dp', 'mp')
- down_second_new: float32 [3072, 768], P('mp', 'dp')
- vec_second_new: float32 [3, 768], P(None, 'dp')
The draws below stay inside these ranges and needn't reach their ends.
Inputs may be any that keep to these rules, and one draw needn't show every extreme that they name: Every sequence's capacity is 1024, 512 or 256; the sequences come in 4 batches of consecutive sequences that share one capacity, and each of the three values is used by some batch. Each row holds distinct positions: its first capacity[s] entries are the selected positions in ascending order, the rest are other positions in ascending order.
All inputs are finite; a program needn't handle non-finite values.
Results may differ from the reference program's by a relative error of at most 0.012.
Values may be sent and summed in bfloat16 or wider, within the bound.
A program may use at most 128 MiB of HBM per device.

```python
import math
import jax
import jax.numpy as jnp
from jax import lax

MODEL_DIM = 768
HEADS = 12
HEAD_DIM = 64
FFN_DIM = 3072
SEQ_LEN = 2048
BATCHES = 4
STEP = 10
SEQS = 8


def routing_tables(key):
    level_extra = jax.random.randint(jax.random.fold_in(key, 11), (BATCHES - 3,), 0, 3).astype(jnp.int32)
    levels = jnp.concatenate([jnp.arange(3, dtype=jnp.int32), level_extra])
    levels = jax.random.permutation(jax.random.fold_in(key, 12), levels)
    batch_ids = jnp.arange(SEQS, dtype=jnp.int32) * BATCHES // SEQS
    shifts = levels[batch_ids]
    counts = (SEQ_LEN // 2 // jnp.left_shift(jnp.ones_like(shifts), shifts)).astype(jnp.int32)
    seq_keys = jax.random.split(jax.random.fold_in(key, 13), SEQS)

    def shuffle_one(one_key):
        return jax.random.permutation(one_key, SEQ_LEN)
    orders = jax.vmap(shuffle_one)(seq_keys).astype(jnp.int32)
    ranks = jnp.argsort(orders, axis=-1, stable=True).astype(jnp.int32)
    positions = jnp.arange(SEQ_LEN, dtype=jnp.int32)[None, :]
    sort_keys = jnp.where(ranks < counts[:, None], positions, positions + SEQ_LEN)
    chosen = jnp.argsort(sort_keys, axis=-1, stable=True)[:, :SEQ_LEN // 2].astype(jnp.int32)
    return (counts, chosen)


def draw_capacity(key, part):
    return routing_tables(key)[0]


def draw_selected(key, part):
    return routing_tables(key)[1]


def vector_scales():
    return jnp.array([1.0, 0.35, 0.35], jnp.float32)[:, None] * (0.3 * SEQS * SEQ_LEN) ** 0.5


def draw_vec_master(key, part):
    gain_part = 1.0 + 0.25 * jax.random.uniform(jax.random.fold_in(key, 21), (2, MODEL_DIM), minval=-1.0, maxval=1.0)
    router_part = jax.random.normal(jax.random.fold_in(key, 22), (1, MODEL_DIM))
    return jnp.concatenate([gain_part, router_part], axis=0).astype(jnp.float32)


def draw_vec_first(key, part):
    return (0.11 * vector_scales() * jax.random.normal(key, (3, MODEL_DIM))).astype(jnp.float32)


def draw_vec_second(key, part):
    factor = jnp.exp(jax.random.uniform(key, (3, MODEL_DIM), minval=0.0, maxval=math.log(4.0)))
    return (0.0526 * vector_scales() * vector_scales() * factor).astype(jnp.float32)


def shard_levels(key, extent, shards, least, largest):
    def one(dim, shards_of):
        heights = jax.random.uniform(jax.random.fold_in(jax.random.fold_in(key, 6), dim), (shards_of,), jnp.float32, least / len(shards), largest / len(shards))
        return jnp.repeat(jnp.exp(heights), extent[dim] // shards_of).reshape((-1,) + (1,) * (len(extent) - dim - 1))

    level = one(*shards[0])
    for cut in shards[1:]:
        level = level * one(*cut)
    return level


def normal_values(own_key, extent, deviation, limit, cuts=(), kind=jnp.bfloat16):
    drawn = deviation * jax.random.normal(own_key, extent, jnp.float32)
    if cuts:
        drawn = drawn * shard_levels(own_key, extent, cuts, -0.22, 0.18)
    return jnp.clip(drawn, -limit, limit).astype(kind)


def setup_inputs(seed: int = 0) -> dict:
    splits = jax.random.split(jax.random.key(seed), 20)
    tokens = normal_values(splits[0], (SEQS, SEQ_LEN, MODEL_DIM), 1.0, 6.0, ((0, 8),))
    cotangent = normal_values(splits[1], (SEQS, SEQ_LEN, MODEL_DIM), 1.0, 6.0, ((0, 8),))
    capacity = draw_capacity(jax.random.fold_in(splits[19], 71), 0)
    selected = draw_selected(jax.random.fold_in(splits[19], 71), 0)
    qkv_master = normal_values(splits[4], (3, MODEL_DIM, MODEL_DIM), MODEL_DIM ** -0.5, 0.21875, ((1, 8), (2, 4)), jnp.float32)
    out_master = normal_values(splits[5], (MODEL_DIM, MODEL_DIM), HEAD_DIM ** -0.5, 0.75, ((0, 4), (1, 8)), jnp.float32)
    up_master = normal_values(splits[6], (MODEL_DIM, FFN_DIM), MODEL_DIM ** -0.5, 0.21875, ((0, 8), (1, 4)), jnp.float32)
    down_master = normal_values(splits[7], (FFN_DIM, MODEL_DIM), FFN_DIM ** -0.5, 0.109375, ((0, 4), (1, 8)), jnp.float32)
    vec_master = draw_vec_master(jax.random.fold_in(splits[19], 71), 0)
    qkv_first = normal_values(splits[9], (3, MODEL_DIM, MODEL_DIM), (0.11 * (0.3 * SEQS * SEQ_LEN) ** 0.5), 48.0, ((1, 8), (2, 4)), jnp.float32)
    out_first = normal_values(splits[10], (MODEL_DIM, MODEL_DIM), (0.022 * (0.3 * SEQS * SEQ_LEN) ** 0.5), 6.0, ((0, 4), (1, 8)), jnp.float32)
    up_first = normal_values(splits[11], (MODEL_DIM, FFN_DIM), (0.013 * (0.3 * SEQS * SEQ_LEN) ** 0.5), 6.0, ((0, 8), (1, 4)), jnp.float32)
    down_first = normal_values(splits[12], (FFN_DIM, MODEL_DIM), (0.036 * (0.3 * SEQS * SEQ_LEN) ** 0.5), 16.0, ((0, 4), (1, 8)), jnp.float32)
    vec_first = draw_vec_first(jax.random.fold_in(splits[19], 71), 0)
    qkv_second = jnp.clip(jnp.exp(math.log(2064.384) - 2.7821582 * jax.random.uniform(splits[14], (3, MODEL_DIM, MODEL_DIM), jnp.float32) ** shard_levels(splits[14], (3, MODEL_DIM, MODEL_DIM), ((1, 8), (2, 4)), -0.2, 0.2)), 127.7952, 2064.384)
    out_second = jnp.clip(jnp.exp(math.log(82.57536) - 2.7821582 * jax.random.uniform(splits[15], (MODEL_DIM, MODEL_DIM), jnp.float32) ** shard_levels(splits[15], (MODEL_DIM, MODEL_DIM), ((0, 4), (1, 8)), -0.2, 0.2)), 5.111808, 82.57536)
    up_second = jnp.clip(jnp.exp(math.log(29.727129) - 2.7821582 * jax.random.uniform(splits[16], (MODEL_DIM, FFN_DIM), jnp.float32) ** shard_levels(splits[16], (MODEL_DIM, FFN_DIM), ((0, 8), (1, 4)), -0.2, 0.2)), 1.8402508, 29.727129)
    down_second = jnp.clip(jnp.exp(math.log(227.08224) - 2.7821582 * jax.random.uniform(splits[17], (FFN_DIM, MODEL_DIM), jnp.float32) ** shard_levels(splits[17], (FFN_DIM, MODEL_DIM), ((0, 4), (1, 8)), -0.2, 0.2)), 14.057472, 227.08224)
    vec_second = draw_vec_second(jax.random.fold_in(splits[19], 71), 0)
    return {"tokens": tokens, "cotangent": cotangent, "capacity": capacity, "selected": selected, "qkv_master": qkv_master, "out_master": out_master, "up_master": up_master, "down_master": down_master, "vec_master": vec_master, "qkv_first": qkv_first, "out_first": out_first, "up_first": up_first, "down_first": down_first, "vec_first": vec_first, "qkv_second": qkv_second, "out_second": out_second, "up_second": up_second, "down_second": down_second, "vec_second": vec_second}


NORM_EPS = 1e-05
MASKED_SCORE = -1000000000.0
MOMENT_DECAY = 0.9
SQUARE_DECAY = 0.95
ADAM_EPS = 1e-08
WEIGHT_DECAY = 0.1
RATE_MATRIX = 0.06
RATE_VECTOR = 0.2
PRECISE = lax.Precision.HIGHEST

@jax.custom_vjp
def low(v):
    return lax.optimization_barrier(v.astype(jnp.bfloat16)).astype(jnp.float32)

@jax.custom_vjp
def low_back(v):
    return v

def low_keep(v):
    return (low(v), None)

def low_pass(kept, grad):
    return (grad,)

def back_keep(v):
    return (v, None)

def back_low(kept, grad):
    return (low(grad),)
low.defvjp(low_keep, low_pass)
low_back.defvjp(back_keep, back_low)

def rms_scaled(values, gain_row):
    return values * lax.rsqrt(lax.optimization_barrier(jnp.mean(values * values, axis=-1, keepdims=True)) + NORM_EPS) * gain_row

def gelu_tanh(values):
    return 0.5 * values * (1.0 + jnp.tanh(0.7978845608028654 * (values + 0.044715 * values * values * values)))

def sequence_forward(weights, one_sequence, chosen, live_count):
    w_qkv, w_out, w_up, w_down, vectors = weights
    slot_count = chosen.shape[0]
    slot_ids = jnp.arange(slot_count, dtype=jnp.int32)
    live_mask = slot_ids < live_count
    row_data = one_sequence[chosen]
    normed_low = low(rms_scaled(row_data, vectors[0]))
    projected = jnp.einsum('cd,tde->tce', normed_low, w_qkv, precision=PRECISE)
    projected = low_back(low(projected))
    head_split = projected.reshape(3, slot_count, HEADS, HEAD_DIM)
    scores = jnp.einsum('qhd,khd->hqk', head_split[0], head_split[1], precision=PRECISE) * HEAD_DIM ** (-0.5)
    scores = low_back(scores)
    allowed = (slot_ids[None, :] <= slot_ids[:, None]) & live_mask[None, :]
    scores = jnp.where(allowed[None], scores, MASKED_SCORE)
    row_max = lax.optimization_barrier(jnp.max(scores, axis=-1, keepdims=True))
    exp_terms = jnp.exp(scores - row_max)
    prob_rows = exp_terms / lax.optimization_barrier(jnp.sum(exp_terms, axis=-1, keepdims=True))
    mixed_heads = jnp.einsum('hqk,khd->qhd', low(prob_rows), head_split[2], precision=PRECISE)
    mixed_heads = low_back(low(mixed_heads.reshape(slot_count, HEADS * HEAD_DIM)))
    attended = low_back(jnp.dot(mixed_heads, w_out, precision=PRECISE))
    summed = low_back(low(row_data + attended))
    inner_low = low(rms_scaled(summed, vectors[1]))
    up_proj = low_back(jnp.dot(inner_low, w_up, precision=PRECISE))
    activated = low(gelu_tanh(up_proj))
    branch = low_back(low(jnp.dot(activated, w_down, precision=PRECISE)))
    gate_value = jax.nn.sigmoid(jnp.dot(row_data, vectors[2], precision=PRECISE) * MODEL_DIM ** (-0.5))
    updated = row_data + gate_value[:, None] * (attended + branch)
    target = jnp.where(live_mask, chosen, one_sequence.shape[0]).astype(jnp.int32)
    return one_sequence.at[target].set(updated, mode='drop')

def adam_update(master, first_moment, second_moment, gradient, step_rate, decay_rate):
    first_new = MOMENT_DECAY * first_moment + (1.0 - MOMENT_DECAY) * gradient
    second_new = SQUARE_DECAY * second_moment + (1.0 - SQUARE_DECAY) * gradient * gradient
    first_hat = first_new / (1.0 - MOMENT_DECAY ** STEP)
    second_hat = second_new / (1.0 - SQUARE_DECAY ** STEP)
    master_new = master - step_rate * (first_hat / (jnp.sqrt(second_hat) + ADAM_EPS) + decay_rate * master)
    return (master_new, first_new, second_new)

def reference(tokens, cotangent, capacity, selected, qkv_master, out_master, up_master, down_master, vec_master, qkv_first, out_first, up_first, down_first, vec_first, qkv_second, out_second, up_second, down_second, vec_second):
    masters = (qkv_master, out_master, up_master, down_master, vec_master)
    weights = tuple((master.astype(jnp.bfloat16).astype(jnp.float32) for master in masters))

    def forward(weight_set, inputs):

        def one_step(seq_items):
            return sequence_forward(weight_set, seq_items[0], seq_items[1], seq_items[2])
        return lax.map(jax.checkpoint(one_step), (inputs, selected, capacity))
    outputs, pullback = jax.vjp(forward, weights, tokens.astype(jnp.float32))
    weight_grads, token_grads = pullback(cotangent.astype(jnp.float32))
    firsts = (qkv_first, out_first, up_first, down_first, vec_first)
    seconds = (qkv_second, out_second, up_second, down_second, vec_second)
    rates = (RATE_MATRIX, RATE_MATRIX, RATE_MATRIX, RATE_MATRIX, RATE_VECTOR)
    decays = (WEIGHT_DECAY, WEIGHT_DECAY, WEIGHT_DECAY, WEIGHT_DECAY, 0.0)
    results = [adam_update(masters[number], firsts[number], seconds[number], weight_grads[number], rates[number], decays[number]) for number in range(5)]
    return (outputs.astype(jnp.bfloat16), token_grads, results[0][0], results[1][0], results[2][0], results[3][0], results[4][0], results[0][1], results[1][1], results[2][1], results[3][1], results[4][1], results[0][2], results[1][2], results[2][2], results[3][2], results[4][2])
```

```python
import functools

import jax
import jax.numpy as jnp
from jax import lax
from jax.experimental import pallas as pl
from jax.experimental.pallas import tpu as pltpu
from jax.sharding import PartitionSpec as P

HEAD_DIM = 64
STEP = 10
NORM_EPS = 1e-05
MASKED_SCORE = -1000000000.0
MOMENT_DECAY = 0.9
SQUARE_DECAY = 0.95
ADAM_EPS = 1e-08
WEIGHT_DECAY = 0.1
RATE_MATRIX = 0.06
RATE_VECTOR = 0.2

LOW = jnp.bfloat16
FULL = jnp.float32
MESH = pl.DeviceIdType.MESH
BLOCKS = 4
VMEM_BYTES = 58 * 2**20


def nn(a, b):
    return lax.dot_general(a, b, (((1,), (0,)), ((), ())), preferred_element_type=FULL)


def nt(a, b):
    return lax.dot_general(a, b, (((1,), (1,)), ((), ())), preferred_element_type=FULL)


def tn(a, b):
    return lax.dot_general(a, b, (((0,), (0,)), ((), ())), preferred_element_type=FULL)


def mean_square_inverse(values):
    return lax.rsqrt(jnp.mean(values * values, axis=-1, keepdims=True) + NORM_EPS)


def gate_of(rows, router_row):
    width = rows.shape[-1]
    logit = jnp.sum(rows * router_row, axis=-1, keepdims=True) * width ** (-0.5)
    return jax.nn.sigmoid(logit)


def greet(partners):
    barrier = pltpu.get_barrier_semaphore()
    for partner in partners:
        pl.semaphore_signal(barrier, inc=1, device_id=partner, device_id_type=MESH)
    pl.semaphore_wait(barrier, len(partners))


def remote(src, dst, send_sem, recv_sem, device):
    return pltpu.make_async_remote_copy(
        src_ref=src,
        dst_ref=dst,
        send_sem=send_sem,
        recv_sem=recv_sem,
        device_id=device,
        device_id_type=MESH,
    )


def places(groups):
    me = lax.axis_index("dp")
    part = lax.axis_index("mp")
    line = groups // 2
    return me, part, line, me // 2, me % 2


class Exchange:
    def __init__(self, parts, near, pair, far, total, sems):
        self.parts, self.near, self.pair, self.far, self.total = parts, near, pair, far, total
        self.sems = sems
        self.me, self.part = lax.axis_index("dp"), lax.axis_index("mp")
        self.half = self.part % 2
        self.near_device = (self.me, self.part + 1 - 2 * self.half)
        self.far_device = (self.me, (self.part + 2) % 4)

    def copy(self, which, block, src, dst):
        device = self.far_device if which == 1 else self.near_device
        return remote(src, dst, self.sems.at[0, which, block], self.sems.at[1, which, block], device)

    def out(self, which, block):
        if which == 0:
            return self.copy(0, block, self.parts.at[block, 1 - self.half], self.near.at[block])
        if which == 1:
            return self.copy(1, block, self.pair.at[block], self.far.at[block])
        spot = self.total.at[block, self.half]
        return self.copy(2, block, spot, spot)

    def into(self, which, block):
        spot = (self.near.at[block], self.far.at[block], self.total.at[block, 1 - self.half])[which]
        return self.copy(which, block, spot, spot)

    def put(self, block, value):
        rows, width = value.shape
        self.parts[block] = value.astype(LOW).reshape(2, rows // 2, width)
        self.send(block)

    def send(self, block):
        self.out(0, block).start()

    def cross(self, block):
        self.into(0, block).wait_recv()
        self.pair[block] = (
            self.parts[block, self.half].astype(FULL) + self.near[block].astype(FULL)
        ).astype(LOW)
        self.out(1, block).start()

    def finish(self, block):
        self.into(1, block).wait_recv()
        self.total[block, self.half] = (
            self.pair[block].astype(FULL) + self.far[block].astype(FULL)
        ).astype(LOW)
        self.out(2, block).start()

    def arrived(self, block):
        self.into(2, block).wait_recv()

    def drain(self, block):
        for which in range(3):
            self.out(which, block).wait_send()


def head_lanes(width, head):
    lanes = lax.broadcasted_iota(jnp.int32, (1, width), 1)
    return (lanes // HEAD_DIM == head).astype(FULL).astype(LOW)


def first_kernel(groups, joined, *refs):
    if joined:
        (count_ref, sel_ref, tok_ref, cot_ref, shard_ref, vec_ref), refs = refs[:6], refs[6:]
        (wg, gains, x_ref, dy_ref, qkv_ref, o_ref), refs = refs[:6], refs[6:]
        vg, mixed, send_z, recv_z, send_y, recv_y, send_f, recv_f = refs
    else:
        (count_ref, sel_ref, tok_ref, cot_ref, wg, gains), refs = refs[:6], refs[6:]
        (x_ref, dy_ref, qkv_ref, o_ref), refs = refs[:4], refs[4:]
        (mixed,) = refs
    slots, width = x_ref.shape
    seq_len = tok_ref.shape[0]
    local_width = o_ref.shape[1]
    heads = local_width // HEAD_DIM
    count = count_ref[0]

    if joined:
        me, part, line, place, side = places(groups)
        other = (me + 1 - 2 * side, part)
        peers = [lax.rem(place + j, line) * 2 + side for j in range(1, line)]
        sources = [lax.rem(place + line - j, line) * 2 + side for j in range(1, line)]
        greet([other] + [(peer, part) for peer in peers])

        def slot(k, d):
            return vg.at[d] if k == 3 else wg.at[k, d]

        def source(k):
            return vec_ref if k == 3 else shard_ref.at[k]

        def to_line(k, j):
            return remote(
                source(k), slot(k, me), send_z.at[k, j], recv_z.at[k, j], (peers[j], part)
            )

        def from_line(k, j):
            spot = slot(k, sources[j])
            return remote(spot, spot, send_z.at[k, j], recv_z.at[k, j], (peers[j], part))

        def to_pair(k):
            return remote(source(k), slot(k, me), send_y.at[k], recv_y.at[k], other)

        def from_pair(k):
            spot = slot(k, me + 1 - 2 * side)
            return remote(spot, spot, send_y.at[k], recv_y.at[k], other)

        def forward(k, j):
            spot = slot(k, sources[j])
            return remote(spot, spot, send_f.at[k, j], recv_f.at[k, j], other)

        def forwarded(k, j):
            spot = slot(k, sources[j] + 1 - 2 * side)
            return remote(spot, spot, send_f.at[k, j], recv_f.at[k, j], other)

        def begin(k):
            for j in range(line - 1):
                to_line(k, j).start()
            to_pair(k).start()

        def relay(k):
            for j in range(line - 1):
                from_line(k, j).wait_recv()
                forward(k, j).start()

        def arrive(k):
            from_pair(k).wait_recv()
            for j in range(line - 1):
                forwarded(k, j).wait_recv()

        def drain(k):
            to_pair(k).wait_send()
            for j in range(line - 1):
                to_line(k, j).wait_send()
                forward(k, j).wait_send()

        begin(3)
        begin(0)
        for k in range(3):
            wg[k, me] = shard_ref[k]
        vg[me] = vec_ref[...]

    block = slots // 2

    def pick(number, table_ref, dead_zero, out_ref):
        rows = pl.ds(pl.multiple_of(number * block, block), block)
        spots = lax.broadcasted_iota(jnp.int32, (block, seq_len), 1)
        hot = (spots == sel_ref[rows, :]).astype(FULL).astype(LOW)
        got = nn(hot, table_ref[...])
        if dead_zero:
            ids = number * block + lax.broadcasted_iota(jnp.int32, (block, 1), 0)
            got = jnp.where(ids < count, got, 0.0)
        out_ref[rows, :] = got.astype(LOW)

    @pl.loop(0, 2)
    def _(number):
        pick(number, tok_ref, False, x_ref)

    if joined:
        relay(3)
        relay(0)
        begin(1)

    @pl.loop(0, 2)
    def _(number):
        pick(number, cot_ref, True, dy_ref)

    if joined:
        arrive(3)
        arrive(0)
        share = width // groups
        rows = [vg[d].astype(FULL)[:, :share] for d in range(groups)]
        gains[...] = jnp.concatenate(rows, axis=1)[: gains.shape[0]]

    first_gain = gains[0:1, :]
    w_first = wg[0].reshape(width, wg.shape[-1])
    quarter = slots // BLOCKS

    for t in range(3):
        w_t = w_first[:, t * local_width : (t + 1) * local_width]
        for number in range(BLOCKS):
            rows = slice(number * quarter, (number + 1) * quarter)
            x_rows = x_ref[rows, :].astype(FULL)
            normed = (x_rows * mean_square_inverse(x_rows) * first_gain).astype(LOW)
            qkv_ref[t, rows, :] = nn(normed, w_t).astype(LOW)

    if joined:
        relay(1)
        begin(2)

    mixed[...] = jnp.zeros_like(mixed)

    @pl.loop(0, heads)
    def _(head):
        lanes = head_lanes(local_width, head)
        for number in range(BLOCKS):
            start, stop = number * quarter, (number + 1) * quarter
            query = qkv_ref[0, start:stop, :] * (lanes * HEAD_DIM ** (-0.5))
            scores = nt(query, qkv_ref[1, :stop, :])
            own = start + lax.broadcasted_iota(jnp.int32, (quarter, 1), 0)
            last = jnp.minimum(own, count - 1)
            keys = lax.broadcasted_iota(jnp.int32, (quarter, stop), 1)
            scores = jnp.where(keys <= last, scores, MASKED_SCORE)
            terms = jnp.exp(scores - jnp.max(scores, axis=-1, keepdims=True))
            inverse = 1.0 / jnp.sum(terms, axis=-1, keepdims=True)
            probs = (terms * inverse).astype(LOW)
            mixed[start:stop, :] += nn(probs, qkv_ref[2, :stop, :] * lanes)

    o_ref[...] = mixed[...].astype(LOW)

    if joined:
        relay(2)
        arrive(1)
        arrive(2)
        for k in range(4):
            drain(k)


def second_kernel(*refs):
    (o_ref, x_ref, dy_ref, w_ref, gains), refs = refs[:5], refs[5:]
    (a_ref, m_ref, dz_ref, do_ref, du_ref, dd_ref, dwo_ref, dg_ref), refs = refs[:8], refs[8:]
    a_parts, a_near, a_pair, a_far, h_parts, h_near, h_pair, h_far, h_total = refs[:9]
    up_acc, down_acc, out_acc, a_sems, h_sems = refs[9:]
    width = x_ref.shape[1]
    local_width = o_ref.shape[1]
    rows_of = x_ref.shape[0] // BLOCKS
    first = Exchange(a_parts, a_near, a_pair, a_far, a_ref, a_sems)
    second = Exchange(h_parts, h_near, h_pair, h_far, h_total, h_sems)
    greet([first.near_device, first.far_device])
    w_out = w_ref[0, :, 3 * local_width : 4 * local_width]
    gain_row, router_row = gains[1:2, :], gains[2:3, :]

    def rows_at(number):
        return pl.ds(pl.multiple_of(number * rows_of, rows_of), rows_of)

    @pl.loop(0, BLOCKS)
    def _(number):
        first.put(number, nt(o_ref[rows_at(number), :], w_out))

    @pl.loop(0, BLOCKS)
    def _(number):
        first.cross(number)

    first.finish(0)
    up_acc[...] = jnp.zeros_like(up_acc)
    down_acc[...] = jnp.zeros_like(down_acc)
    out_acc[...] = jnp.zeros_like(out_acc)
    dg_ref[...] = jnp.zeros_like(dg_ref)

    def summed(number):
        x_rows = x_ref[rows_at(number), :].astype(FULL)
        attended = a_ref[number].reshape(rows_of, width).astype(FULL)
        summed_rows = (x_rows + attended).astype(LOW).astype(FULL)
        inverse = mean_square_inverse(summed_rows)
        return x_rows, summed_rows * inverse, inverse

    @pl.loop(0, BLOCKS)
    def _(number):
        rows = rows_at(number)
        first.arrived(number)
        x_rows, normed, inverse = summed(number)
        inner = (normed * gain_row).astype(LOW)
        up = nn(inner, w_ref[1])
        square = up * up
        bent = jnp.tanh(0.7978845608028654 * (up + 0.044715 * square * up))
        half = 0.5 * (1.0 + bent)
        active = (up * half).astype(LOW)
        slope = half + 0.5 * up * (1.0 - bent * bent) * (
            0.7978845608028654 * (1.0 + 3.0 * 0.044715 * square)
        )
        m_ref[rows, :] = nt(active, w_ref[2]).astype(LOW)

        @pl.when(number < BLOCKS - 1)
        def _():
            first.finish(number + 1)

        @pl.when(number > 0)
        def _():
            second.cross(number - 1)

        gate = gate_of(x_rows, router_row)
        branch = (gate * dy_ref[rows, :].astype(FULL)).astype(LOW)
        up_low = (nn(branch, w_ref[2]) * slope).astype(LOW)
        second.put(number, nt(up_low, w_ref[1]))
        down_acc[...] += tn(branch, active)
        up_acc[...] += tn(inner, up_low)

    second.cross(BLOCKS - 1)
    second.finish(0)
    du_ref[...] = up_acc[...].astype(LOW)
    dd_ref[...] = down_acc[...].astype(LOW)

    @pl.loop(0, BLOCKS)
    def _(number):
        rows = rows_at(number)

        @pl.when(number < BLOCKS - 1)
        def _():
            second.finish(number + 1)

        second.arrived(number)
        x_rows, normed, inverse = summed(number)
        grad = h_total[number].reshape(rows_of, width).astype(FULL)
        dg_ref[0:1, :] += jnp.sum(grad * normed, axis=0, keepdims=True)
        scaled = grad * gain_row
        back = inverse * (scaled - normed * jnp.mean(scaled * normed, axis=-1, keepdims=True))
        back_low = back.astype(LOW)
        dz_ref[rows, :] = back_low
        gate = gate_of(x_rows, router_row)
        attn = (gate * dy_ref[rows, :].astype(FULL) + back_low.astype(FULL)).astype(LOW)
        do_ref[rows, :] = nn(attn, w_out).astype(LOW)
        out_acc[...] += tn(attn, o_ref[rows, :])

    dwo_ref[...] = out_acc[...].astype(LOW)

    @pl.loop(0, BLOCKS)
    def _(number):
        first.drain(number)
        second.drain(number)


def third_kernel(groups, joined, *refs):
    (count_ref, x_ref, dy_ref, a_ref, m_ref, dz_ref, do_ref, qkv_ref, w_ref), refs = refs[:9], refs[9:]
    (du_ref, dd_ref, dwo_ref, dg_ref, gains), refs = refs[:5], refs[5:]
    (y_ref, dx_ref, gsum_ref, vsum_ref), refs = refs[:4], refs[4:]
    m_near, m_pair, m_far, m_total, d_parts, d_near, d_pair, d_far, d_total = refs[:9]
    h_ref, dqkv, dqkv_low, vacc, m_sems, d_sems = refs[9:15]
    refs = refs[15:]
    slots, width = x_ref.shape
    local_width = do_ref.shape[1]
    heads = local_width // HEAD_DIM
    rows_of = slots // BLOCKS
    count = count_ref[0]
    branch = Exchange(m_ref, m_near, m_pair, m_far, m_total, m_sems)
    inputs = Exchange(d_parts, d_near, d_pair, d_far, d_total, d_sems)
    partners = [branch.near_device, branch.far_device]
    if joined:
        g0, ry, pairs, rz, vr, send_y, recv_y, send_z, recv_z, send_v, recv_v = refs
        me, part, line, place, side = places(groups)
        other = (me + 1 - 2 * side, part)
        peers = [lax.rem(place + j, line) for j in range(1, line)]
        everyone = [(lax.rem(me + j, groups), part) for j in range(1, groups)]
        greet(partners + everyone)
        grads = (g0, du_ref, dd_ref)

        def to_pair(k, z):
            spot = z * 2 + 1 - side
            return remote(grads[k].at[spot], ry.at[k, z], send_y.at[k, z], recv_y.at[k, z], other)

        def to_line(k, j):
            return remote(
                pairs.at[k, peers[j]],
                rz.at[k, j],
                send_z.at[k, j],
                recv_z.at[k, j],
                (peers[j] * 2 + side, part),
            )

        def begin(k):
            for z in range(line):
                to_pair(k, z).start()

        def relay(k):
            for z in range(line):
                to_pair(k, z).wait_recv()
                pairs[k, z] = (
                    grads[k][z * 2 + side].astype(FULL) + ry[k, z].astype(FULL)
                ).astype(LOW)
            for j in range(line - 1):
                to_line(k, j).start()

        def arrive(k):
            total = pairs[k, place].astype(FULL)
            for j in range(line - 1):
                to_line(k, j).wait_recv()
                total = total + rz[k, j].astype(FULL)
            gsum_ref[k] = total

        def to_all(j):
            return remote(vacc, vr.at[j], send_v.at[j], recv_v.at[j], everyone[j])

        begin(1)
        begin(2)
    else:
        greet(partners)

    branch.send(0)
    dqkv[...] = jnp.zeros_like(dqkv)

    @pl.loop(0, heads)
    def _(head):
        lanes = head_lanes(local_width, head)
        for number in range(BLOCKS):
            start, stop = number * rows_of, (number + 1) * rows_of
            query = qkv_ref[0, start:stop, :] * (lanes * HEAD_DIM ** (-0.5))
            mixed_grad = do_ref[start:stop, :] * lanes
            scores = nt(qkv_ref[1, :stop, :], query)
            own = start + lax.broadcasted_iota(jnp.int32, (1, rows_of), 1)
            last = jnp.minimum(own, count - 1)
            keys = lax.broadcasted_iota(jnp.int32, (stop, rows_of), 0)
            scores = jnp.where(keys <= last, scores, MASKED_SCORE)
            terms = jnp.exp(scores - jnp.max(scores, axis=0, keepdims=True))
            inverse = 1.0 / jnp.sum(terms, axis=0, keepdims=True)
            probs = terms * inverse
            prob_grad = nt(qkv_ref[2, :stop, :], mixed_grad)
            dots = jnp.sum(prob_grad * probs, axis=0, keepdims=True)
            score_grad = (probs * (prob_grad - dots)).astype(LOW)
            dqkv[2, :stop, :] += nn(probs.astype(LOW), mixed_grad)
            dqkv[1, :stop, :] += nn(score_grad, query)
            dqkv[0, start:stop, :] += tn(score_grad, qkv_ref[1, :stop, :] * lanes)

        @pl.when(head == 0)
        def _():
            branch.cross(0)
            if joined:
                relay(1)

        @pl.when(head == 1)
        def _():
            if joined:
                relay(2)

    dqkv_low[0] = (dqkv[0] * HEAD_DIM ** (-0.5)).astype(LOW)
    dqkv_low[1] = dqkv[1].astype(LOW)
    dqkv_low[2] = dqkv[2].astype(LOW)
    first_gain, router_row = gains[0:1, :], gains[2:3, :]

    for number in range(BLOCKS):
        rows = slice(number * rows_of, (number + 1) * rows_of)
        total = jnp.zeros((rows_of, width), FULL)
        for t in range(3):
            w_t = w_ref[:, t * local_width : (t + 1) * local_width]
            total += nt(dqkv_low[t, rows, :], w_t)
        inputs.put(number, total)

    for number in range(BLOCKS):
        inputs.cross(number)
    branch.finish(0)

    for number in range(BLOCKS):
        rows = slice(number * rows_of, (number + 1) * rows_of)
        x_rows = x_ref[rows, :].astype(FULL)
        h_ref[rows, :] = (x_rows * mean_square_inverse(x_rows) * first_gain).astype(LOW)
    parts = [tn(h_ref[...], dqkv_low[t]) for t in range(3)]
    parts.append(dwo_ref[...].astype(FULL))
    merged = jnp.concatenate(parts, axis=1)
    if joined:
        g0[...] = merged.astype(LOW).reshape(g0.shape)
        begin(0)
    else:
        gsum_ref[0] = merged
        gsum_ref[1] = du_ref[...].astype(FULL)
        gsum_ref[2] = dd_ref[...].astype(FULL)

    vacc[...] = jnp.zeros_like(vacc)
    vacc[1:2, :] = dg_ref[0:1, :]
    branch.arrived(0)
    if joined:
        relay(0)
    inputs.finish(0)

    for number in range(BLOCKS):
        rows = slice(number * rows_of, (number + 1) * rows_of)
        if number + 1 < BLOCKS:
            inputs.finish(number + 1)
        x_rows = x_ref[rows, :].astype(FULL)
        dy_rows = dy_ref[rows, :].astype(FULL)
        half, inner = number // (BLOCKS // 2), number % (BLOCKS // 2)
        m_rows = m_total[0, half, inner * rows_of : (inner + 1) * rows_of, :].astype(FULL)
        added = a_ref[rows, :].astype(FULL) + m_rows
        gate = gate_of(x_rows, router_row)
        y_ref[rows, :] = (x_rows + gate * added).astype(LOW)
        gate_grad = jnp.sum(dy_rows * added, axis=-1, keepdims=True)
        logit_grad = gate_grad * gate * (1.0 - gate) * width ** (-0.5)
        inverse = mean_square_inverse(x_rows)
        normed = x_rows * inverse
        inputs.arrived(number)
        grad = d_total[number].reshape(rows_of, width).astype(FULL)
        vacc[0:1, :] += jnp.sum(grad * normed, axis=0, keepdims=True)
        vacc[2:3, :] += jnp.sum(logit_grad * x_rows, axis=0, keepdims=True)
        scaled = grad * first_gain
        back = inverse * (scaled - normed * jnp.mean(scaled * normed, axis=-1, keepdims=True))
        dx_ref[rows, :] = (
            dy_rows + dz_ref[rows, :].astype(FULL) + back + logit_grad * router_row
        ).astype(LOW)

    if joined:
        for j in range(groups - 1):
            to_all(j).start()
        for k in (1, 2, 0):
            arrive(k)
        total = vacc[...]
        for j in range(groups - 1):
            to_all(j).wait_recv()
            total = total + vr[j]
        vsum_ref[...] = total
        for k in range(3):
            for z in range(line):
                to_pair(k, z).wait_send()
            for j in range(line - 1):
                to_line(k, j).wait_send()
        for j in range(groups - 1):
            to_all(j).wait_send()
    else:
        vsum_ref[...] = vacc[...]

    branch.drain(0)
    for number in range(BLOCKS):
        inputs.drain(number)


def place_kernel(count_ref, sel_ref, tok_ref, cot_ref, y_ref, dx_ref, out_ref, grad_ref):
    rows, width = tok_ref.shape
    slots = y_ref.shape[0]
    spots = pl.program_id(0) * rows + lax.broadcasted_iota(jnp.int32, (rows, slots), 0)
    ids = lax.broadcasted_iota(jnp.int32, (1, slots), 1)
    chosen = jnp.where(ids < count_ref[0], sel_ref[...], -1)
    hot = (spots == chosen).astype(FULL)
    hit = jnp.max(hot, axis=-1, keepdims=True) > 0.5
    hot = hot.astype(LOW)
    out_ref[...] = jnp.where(hit, nn(hot, y_ref[...]), tok_ref[...].astype(FULL)).astype(LOW)
    grad_ref[...] = jnp.where(hit, nn(hot, dx_ref[...]), cot_ref[...].astype(FULL))


def adam_update(master, first_moment, second_moment, gradient, step_rate, decay_rate):
    first_new = MOMENT_DECAY * first_moment + (1.0 - MOMENT_DECAY) * gradient
    second_new = SQUARE_DECAY * second_moment + (1.0 - SQUARE_DECAY) * gradient * gradient
    first_hat = first_new / (1.0 - MOMENT_DECAY**STEP)
    second_hat = second_new / (1.0 - SQUARE_DECAY**STEP)
    master_new = master - step_rate * (
        first_hat / (jnp.sqrt(second_hat) + ADAM_EPS) + decay_rate * master
    )
    return (master_new, first_new, second_new)


def shape(dims, kind):
    return jax.ShapeDtypeStruct(dims, kind)


IN_VMEM = pl.BlockSpec(memory_space=pltpu.VMEM)
IN_SMEM = pl.BlockSpec(memory_space=pltpu.SMEM)
DMA = pltpu.SemaphoreType.DMA


def params(number=None):
    if number is None:
        return pltpu.CompilerParams(vmem_limit_bytes=VMEM_BYTES)
    return pltpu.CompilerParams(
        vmem_limit_bytes=VMEM_BYTES, collective_id=number, has_side_effects=True
    )


def local(
    tokens,
    cotangent,
    capacity,
    selected,
    qkv_master,
    out_master,
    up_master,
    down_master,
    vec_master,
    qkv_first,
    out_first,
    up_first,
    down_first,
    vec_first,
    qkv_second,
    out_second,
    up_second,
    down_second,
    vec_second,
):
    groups = lax.axis_size("dp")
    me = lax.axis_index("dp")
    share, local_width = qkv_master.shape[1:]
    hidden = up_master.shape[1]
    width = tokens.shape[2]
    seq_len = tokens.shape[1]
    slots = selected.shape[1]
    joined = share % 16 == 0 and groups % 2 == 0
    count = lax.dynamic_slice_in_dim(capacity, me, 1)
    sel_column = selected.reshape(slots, 1)
    token_rows, cot_rows = tokens[0], cotangent[0]
    line = groups // 2

    first_shard = jnp.concatenate(
        [qkv_master[0], qkv_master[1], qkv_master[2], out_master.T], axis=1
    )
    shard = jnp.stack([first_shard, up_master, down_master.T]).astype(LOW)

    row_outs = [
        shape((slots, width), LOW),
        shape((slots, width), LOW),
        shape((3, slots, local_width), LOW),
        shape((slots, local_width), LOW),
    ]
    if joined:
        vec_pad = jnp.pad(vec_master.astype(LOW), ((0, 13), (0, 128 - share)))
        w_all, gains, x_rows, dy_rows, qkv_rows, mixed = pl.pallas_call(
            functools.partial(first_kernel, groups, True),
            out_shape=[
                shape((3, groups, share, width), LOW),
                shape((8, width), FULL),
            ]
            + row_outs,
            in_specs=[IN_SMEM] + [IN_VMEM] * 5,
            out_specs=[IN_VMEM] * 6,
            scratch_shapes=[
                pltpu.VMEM((groups, 16, 128), LOW),
                pltpu.VMEM((slots, local_width), FULL),
                DMA((4, line - 1)),
                DMA((4, line - 1)),
                DMA((4,)),
                DMA((4,)),
                DMA((4, line - 1)),
                DMA((4, line - 1)),
            ],
            compiler_params=params(0),
            name="first",
        )(count, sel_column, token_rows, cot_rows, shard, vec_pad)
        w_all = w_all.reshape(3, width, width)
    else:
        w_all = lax.all_gather(shard, "dp", axis=1, tiled=True)
        gains = lax.all_gather(vec_master.astype(LOW), "dp", axis=1, tiled=True)
        gains = jnp.pad(gains.astype(FULL), ((0, 5), (0, 0)))
        x_rows, dy_rows, qkv_rows, mixed = pl.pallas_call(
            functools.partial(first_kernel, groups, False),
            out_shape=row_outs,
            in_specs=[IN_SMEM] + [IN_VMEM] * 5,
            out_specs=[IN_VMEM] * 4,
            scratch_shapes=[pltpu.VMEM((slots, local_width), FULL)],
            compiler_params=params(),
            name="first",
        )(count, sel_column, token_rows, cot_rows, w_all, gains)

    quarter = slots // BLOCKS
    half_block = (BLOCKS, quarter // 2, width)
    both_halves = (BLOCKS, 2, quarter // 2, width)
    attended, m_part, dz_rows, mixed_grad, du, dd, dwo, dgain = pl.pallas_call(
        second_kernel,
        out_shape=[
            shape(both_halves, LOW),
            shape((slots, width), LOW),
            shape((slots, width), LOW),
            shape((slots, local_width), LOW),
            shape((width, hidden), LOW),
            shape((width, hidden), LOW),
            shape((width, local_width), LOW),
            shape((8, width), FULL),
        ],
        in_specs=[IN_VMEM] * 5,
        out_specs=[IN_VMEM] * 8,
        scratch_shapes=[
            pltpu.VMEM(both_halves, LOW),
            pltpu.VMEM(half_block, LOW),
            pltpu.VMEM(half_block, LOW),
            pltpu.VMEM(half_block, LOW),
            pltpu.VMEM(both_halves, LOW),
            pltpu.VMEM(half_block, LOW),
            pltpu.VMEM(half_block, LOW),
            pltpu.VMEM(half_block, LOW),
            pltpu.VMEM(both_halves, LOW),
            pltpu.VMEM((width, hidden), FULL),
            pltpu.VMEM((width, hidden), FULL),
            pltpu.VMEM((width, local_width), FULL),
            DMA((2, 3, BLOCKS)),
            DMA((2, 3, BLOCKS)),
        ],
        compiler_params=params(1),
        name="second",
    )(mixed, x_rows, dy_rows, w_all, gains)

    whole_half = (1, slots // 2, width)
    whole_both = (1, 2, slots // 2, width)
    if joined:
        du, dd = (g.reshape(groups, share, hidden) for g in (du, dd))
        grad_out = shape((3, share, width), FULL)
        more_scratch = [
            pltpu.VMEM((groups, share, width), LOW),
            pltpu.VMEM((3, line, share, width), LOW),
            pltpu.VMEM((3, line, share, width), LOW),
            pltpu.VMEM((3, line - 1, share, width), LOW),
            pltpu.VMEM((groups - 1, 8, width), FULL),
            DMA((3, line)),
            DMA((3, line)),
            DMA((3, line - 1)),
            DMA((3, line - 1)),
            DMA((groups - 1,)),
            DMA((groups - 1,)),
        ]
    else:
        grad_out = shape((3, width, width), FULL)
        more_scratch = []
    y_rows, dx_rows, grad_sum, vec_sum = pl.pallas_call(
        functools.partial(third_kernel, groups, joined),
        out_shape=[
            shape((slots, width), LOW),
            shape((slots, width), LOW),
            grad_out,
            shape((8, width), FULL),
        ],
        in_specs=[IN_SMEM] + [IN_VMEM] * 13,
        out_specs=[IN_VMEM] * 4,
        scratch_shapes=[
            pltpu.VMEM(whole_half, LOW),
            pltpu.VMEM(whole_half, LOW),
            pltpu.VMEM(whole_half, LOW),
            pltpu.VMEM(whole_both, LOW),
            pltpu.VMEM(both_halves, LOW),
            pltpu.VMEM(half_block, LOW),
            pltpu.VMEM(half_block, LOW),
            pltpu.VMEM(half_block, LOW),
            pltpu.VMEM(both_halves, LOW),
            pltpu.VMEM((slots, width), LOW),
            pltpu.VMEM((3, slots, local_width), FULL),
            pltpu.VMEM((3, slots, local_width), LOW),
            pltpu.VMEM((8, width), FULL),
            DMA((2, 3, 1)),
            DMA((2, 3, BLOCKS)),
        ]
        + more_scratch,
        compiler_params=params(2),
        name="third",
    )(
        count,
        x_rows,
        dy_rows,
        attended.reshape(slots, width),
        m_part.reshape(whole_both),
        dz_rows,
        mixed_grad,
        qkv_rows,
        w_all[0],
        du,
        dd,
        dwo,
        dgain,
        gains,
    )

    spot_rows = min(256, seq_len)
    by_spot = pl.BlockSpec((spot_rows, width), lambda i: (i, 0))
    block_out, input_grad = pl.pallas_call(
        place_kernel,
        grid=(seq_len // spot_rows,),
        out_shape=[shape((seq_len, width), LOW), shape((seq_len, width), FULL)],
        in_specs=[
            IN_SMEM,
            pl.BlockSpec((1, slots), lambda i: (0, 0)),
            by_spot,
            by_spot,
            pl.BlockSpec((slots, width), lambda i: (0, 0)),
            pl.BlockSpec((slots, width), lambda i: (0, 0)),
        ],
        out_specs=[by_spot, by_spot],
        compiler_params=params(),
        name="place",
    )(count, selected, token_rows, cot_rows, y_rows, dx_rows)

    if joined:
        vec_grad = lax.dynamic_slice_in_dim(vec_sum[:3], me * share, share, 1)
    else:
        grad_sum = lax.psum_scatter(grad_sum, "dp", scatter_dimension=1, tiled=True)
        vec_grad = lax.psum_scatter(vec_sum[:3], "dp", scatter_dimension=1, tiled=True)
    first_sum = grad_sum[0]
    qkv_sum = jnp.stack(
        [first_sum[:, t * local_width : (t + 1) * local_width] for t in range(3)]
    )
    out_sum = first_sum[:, 3 * local_width :].T
    qkv_res = adam_update(qkv_master, qkv_first, qkv_second, qkv_sum, RATE_MATRIX, WEIGHT_DECAY)
    out_res = adam_update(out_master, out_first, out_second, out_sum, RATE_MATRIX, WEIGHT_DECAY)
    up_res = adam_update(up_master, up_first, up_second, grad_sum[1], RATE_MATRIX, WEIGHT_DECAY)
    down_res = adam_update(
        down_master, down_first, down_second, grad_sum[2].T, RATE_MATRIX, WEIGHT_DECAY
    )
    vec_res = adam_update(vec_master, vec_first, vec_second, vec_grad, RATE_VECTOR, 0.0)
    results = (qkv_res, out_res, up_res, down_res, vec_res)
    return (
        block_out[None],
        input_grad[None],
        *(res[0] for res in results),
        *(res[1] for res in results),
        *(res[2] for res in results),
    )


def solution(mesh):
    weights = (
        P(None, "dp", "mp"),
        P("mp", "dp"),
        P("dp", "mp"),
        P("mp", "dp"),
        P(None, "dp"),
    )
    rows = (P("dp", None, None), P("dp", None, None))
    return jax.shard_map(
        local,
        mesh=mesh,
        in_specs=(*rows, P(), P("dp", None), *weights * 3),
        out_specs=(*rows, *weights * 3),
        check_vma=False,
    )
```

```python
import functools

import jax
import jax.numpy as jnp
from jax import lax
from jax.experimental import pallas as pl
from jax.experimental.pallas import tpu as pltpu
from jax.sharding import PartitionSpec as P

HEAD_DIM = 64
STEP = 10
NORM_EPS = 1e-05
MASKED_SCORE = -1000000000.0
MOMENT_DECAY = 0.9
SQUARE_DECAY = 0.95
ADAM_EPS = 1e-08
WEIGHT_DECAY = 0.1
RATE_MATRIX = 0.06
RATE_VECTOR = 0.2

LOW = jnp.bfloat16
FULL = jnp.float32
MESH = pl.DeviceIdType.MESH
BLOCKS = 4
VMEM_BYTES = 58 * 2**20


def nn(a, b):
    return lax.dot_general(a, b, (((1,), (0,)), ((), ())), preferred_element_type=FULL)


def nt(a, b):
    return lax.dot_general(a, b, (((1,), (1,)), ((), ())), preferred_element_type=FULL)


def tn(a, b):
    return lax.dot_general(a, b, (((0,), (0,)), ((), ())), preferred_element_type=FULL)


def mean_square_inverse(values):
    return lax.rsqrt(jnp.mean(values * values, axis=-1, keepdims=True) + NORM_EPS)


def gate_of(rows, router_row):
    width = rows.shape[-1]
    logit = jnp.sum(rows * router_row, axis=-1, keepdims=True) * width ** (-0.5)
    return jax.nn.sigmoid(logit)


def greet(partners):
    barrier = pltpu.get_barrier_semaphore()
    for partner in partners:
        pl.semaphore_signal(barrier, inc=1, device_id=partner, device_id_type=MESH)
    pl.semaphore_wait(barrier, len(partners))


def remote(src, dst, send_sem, recv_sem, device):
    return pltpu.make_async_remote_copy(
        src_ref=src,
        dst_ref=dst,
        send_sem=send_sem,
        recv_sem=recv_sem,
        device_id=device,
        device_id_type=MESH,
    )


class Exchange:
    def __init__(self, parts, near, pair, far, total, sems):
        self.parts, self.near, self.pair, self.far, self.total = parts, near, pair, far, total
        self.sems = sems
        self.me, self.part = lax.axis_index("dp"), lax.axis_index("mp")
        self.half = self.part % 2
        self.near_device = (self.me, self.part + 1 - 2 * self.half)
        self.far_device = (self.me, (self.part + 2) % 4)

    def copy(self, which, block, src, dst):
        device = self.far_device if which == 1 else self.near_device
        return remote(src, dst, self.sems.at[0, which, block], self.sems.at[1, which, block], device)

    def out(self, which, block):
        if which == 0:
            return self.copy(0, block, self.parts.at[block, 1 - self.half], self.near.at[block])
        if which == 1:
            return self.copy(1, block, self.pair.at[block], self.far.at[block])
        spot = self.total.at[block, self.half]
        return self.copy(2, block, spot, spot)

    def into(self, which, block):
        spot = (self.near.at[block], self.far.at[block], self.total.at[block, 1 - self.half])[which]
        return self.copy(which, block, spot, spot)

    def put(self, block, value):
        rows, width = value.shape
        self.parts[block] = value.astype(LOW).reshape(2, rows // 2, width)
        self.send(block)

    def send(self, block):
        self.out(0, block).start()

    def cross(self, block):
        self.into(0, block).wait_recv()
        self.pair[block] = (
            self.parts[block, self.half].astype(FULL) + self.near[block].astype(FULL)
        ).astype(LOW)
        self.out(1, block).start()

    def finish(self, block):
        self.into(1, block).wait_recv()
        self.total[block, self.half] = (
            self.pair[block].astype(FULL) + self.far[block].astype(FULL)
        ).astype(LOW)
        self.out(2, block).start()

    def arrived(self, block):
        self.into(2, block).wait_recv()

    def drain(self, block):
        for which in range(3):
            self.out(which, block).wait_send()


def head_lanes(width, head):
    lanes = lax.broadcasted_iota(jnp.int32, (1, width), 1)
    return (lanes // HEAD_DIM == head).astype(FULL).astype(LOW)


def main_kernel(groups, joined, *refs):
    (cap_ref, sel_ref, tok_any, cot_any), refs = refs[:4], refs[4:]
    if joined:
        (shard_ref, vec_ref), refs = refs[:2], refs[2:]
    else:
        (wg, gains), refs = refs[:2], refs[2:]
    (m_total, d_total, gsum_ref, vsum_ref), refs = refs[:4], refs[4:]
    (table, table_sems, x_ref, dy_ref, qkv_ref, o_ref, w4), refs = refs[:7], refs[7:]
    (parts, near, pair, far, a_total, a_sems, d_sems), refs = refs[:7], refs[7:]
    (h_parts, h_near, h_pair, h_far, h_total, h_sems), refs = refs[:6], refs[6:]
    (m_parts, m_near, m_pair, m_far, m_sems), refs = refs[:5], refs[5:]
    (slope_ref, dz_ref, do_ref, out_acc, dkv, dlow, vacc), refs = refs[:7], refs[7:]

    slots, width = x_ref.shape
    seq_len = tok_any.shape[0]
    local_width = o_ref.shape[1]
    heads = local_width // HEAD_DIM
    size = slots // BLOCKS
    me, part = lax.axis_index("dp"), lax.axis_index("mp")
    count = cap_ref[me]
    downward = tuple(reversed(range(BLOCKS)))

    def rows_at(number):
        return slice(number * size, (number + 1) * size)

    def table_copy(which, source):
        return pltpu.make_async_copy(source, table.at[which], table_sems.at[which])

    table_copy(0, tok_any).start()
    table_copy(1, cot_any).start()

    heads_sum = Exchange(parts, near, pair, far, a_total, a_sems)
    hidden_sum = Exchange(h_parts, h_near, h_pair, h_far, h_total, h_sems)
    branch_sum = Exchange(m_parts, m_near, m_pair, m_far, m_total, m_sems)
    input_sum = Exchange(parts, near, pair, far, d_total, d_sems)
    partners = [heads_sum.near_device, heads_sum.far_device]

    if joined:
        (wg, gains, vg, send_r, recv_r, send_l, recv_l, send_f, recv_f), refs = refs[:9], refs[9:]
        (grads, ry, pairs, rz, vpad, vr), refs = refs[:6], refs[6:]
        send_y, recv_y, send_z, recv_z, send_v, recv_v = refs
        line, place, side = groups // 2, me // 2, me % 2
        other = (me + 1 - 2 * side, part)
        everyone = [(lax.rem(me + j, groups), part) for j in range(1, groups)]
        greet(partners + everyone)

        def slot(k, d):
            return vg.at[d] if k == 3 else wg.at[k, d]

        def held(k, z, own):
            if own:
                return vec_ref if k == 3 else shard_ref.at[k]
            return slot(k, z * 2 + side)

        def chain(k, step, right):
            z = place - step + 1 if right else place + step - 1
            sems = (send_r, recv_r) if right else (send_l, recv_l)
            target = (me + 2 if right else me - 2, part)
            return remote(
                held(k, z, step == 1),
                slot(k, z * 2 + side),
                sems[0].at[k, step - 1],
                sems[1].at[k, step - 1],
                target,
            )

        def chain_in(k, step, right):
            z = place - step if right else place + step
            sems = (send_r, recv_r) if right else (send_l, recv_l)
            spot = slot(k, z * 2 + side)
            return remote(spot, spot, sems[0].at[k, step - 1], sems[1].at[k, step - 1], other)

        def can_send(step, right):
            if right:
                return (place + 1 < line) & (place - step + 1 >= 0)
            return (place >= 1) & (place + step - 1 < line)

        def across(k, z, own=False):
            return remote(
                held(k, z, own), slot(k, z * 2 + side), send_f.at[k, z], recv_f.at[k, z], other
            )

        def across_in(k, z):
            spot = slot(k, z * 2 + 1 - side)
            return remote(spot, spot, send_f.at[k, z], recv_f.at[k, z], other)

        def begin(k):
            for right in (True, False):

                @pl.when(can_send(1, right))
                def _():
                    chain(k, 1, right).start()

            across(k, place, True).start()

        def pump(k, step):
            for right in (True, False):
                z = place - step if right else place + step

                @pl.when((z >= 0) & (z < line))
                def _():
                    chain_in(k, step, right).wait_recv()
                    across(k, z).start()

                if step + 1 < line:

                    @pl.when(can_send(step + 1, right))
                    def _():
                        chain(k, step + 1, right).start()

        def arrive(k):
            for z in range(line):
                across_in(k, z).wait_recv()

        def drain_weights(k):
            for right in (True, False):
                for step in range(1, line):

                    @pl.when(can_send(step, right))
                    def _():
                        chain(k, step, right).wait_send()

            for z in range(line):
                across(k, z).wait_send()

        def to_pair(k, z):
            spot = z * 2 + 1 - side
            return remote(grads.at[k, spot], ry.at[k, z], send_y.at[k, z], recv_y.at[k, z], other)

        def to_line(k, j):
            z = lax.rem(place + j, line)
            return remote(
                pairs.at[k, z],
                rz.at[k, j - 1],
                send_z.at[k, j - 1],
                recv_z.at[k, j - 1],
                (z * 2 + side, part),
            )

        def give(k, value):
            grads[k] = value.astype(LOW).reshape(groups, width // groups, width)
            for z in range(line):
                to_pair(k, z).start()

        def relay(k):
            for z in range(line):
                to_pair(k, z).wait_recv()
                pairs[k, z] = (
                    grads[k, z * 2 + side].astype(FULL) + ry[k, z].astype(FULL)
                ).astype(LOW)
            for j in range(1, line):
                to_line(k, j).start()

        def collect(k):
            total = pairs[k, place].astype(FULL)
            for j in range(1, line):
                to_line(k, j).wait_recv()
                total = total + rz[k, j - 1].astype(FULL)
            gsum_ref[k] = total

        def to_all(j):
            target = lax.rem(me + j, groups)
            return remote(
                vpad.at[target], vr.at[j - 1], send_v.at[j - 1], recv_v.at[j - 1], (target, part)
            )

        begin(3)
        begin(0)
        for k in range(3):
            wg[k, me] = shard_ref[k]
        vg[me] = vec_ref[...]
        steps = [(k, step) for k in (0, 1, 2) for step in range(1, line)]
    else:
        greet(partners)
        steps = []

        def give(k, value):
            gsum_ref[k] = value

    def advance(number):
        for _ in range(number):
            if steps:
                k, step = steps.pop(0)
                pump(k, step)
                if k == 0:
                    pump(3, step)
                if step == line - 2 and k < 2:
                    begin(k + 1)

    def pick(number, which, dead_zero, out_ref):
        block = 2 * size
        rows = slice(number * block, (number + 1) * block)
        spots = lax.broadcasted_iota(jnp.int32, (block, seq_len), 1)
        hot = (spots == sel_ref[rows, :]).astype(FULL).astype(LOW)
        got = nn(hot, table[which])
        if dead_zero:
            ids = number * block + lax.broadcasted_iota(jnp.int32, (block, 1), 0)
            got = jnp.where(ids < count, got, 0.0)
        out_ref[rows, :] = got.astype(LOW)

    table_copy(0, tok_any).wait()
    pick(0, 0, False, x_ref)
    pick(1, 0, False, x_ref)
    advance(1)
    table_copy(1, cot_any).wait()
    pick(0, 1, True, dy_ref)
    pick(1, 1, True, dy_ref)
    advance(2)

    if joined:
        arrive(3)
        arrive(0)
        share = width // groups
        rows = [vg[d].astype(FULL)[:, :share] for d in range(groups)]
        gains[...] = jnp.concatenate(rows, axis=1)[: gains.shape[0]]

    first_gain, gain_row, router_row = gains[0:1, :], gains[1:2, :], gains[2:3, :]

    def weight(k):
        return wg[k].reshape(width, wg.shape[-1])

    w_first = weight(0)
    for t in range(4):
        w4[t] = w_first[:, t * local_width : (t + 1) * local_width]

    def first_norm(number):
        x_rows = x_ref[rows_at(number), :].astype(FULL)
        inverse = mean_square_inverse(x_rows)
        return x_rows, x_rows * inverse, inverse

    for number in downward:
        normed = (first_norm(number)[1] * first_gain).astype(LOW)
        for t in range(3):
            qkv_ref[t, rows_at(number), :] = nn(normed, w4[t]).astype(LOW)
    advance(1)

    all_lanes = [head_lanes(local_width, head) for head in range(heads)]

    for number in downward:
        start, stop = number * size, (number + 1) * size
        own = start + lax.broadcasted_iota(jnp.int32, (size, 1), 0)
        keys = lax.broadcasted_iota(jnp.int32, (size, stop), 1)
        allowed = keys <= jnp.minimum(own, count - 1)
        mixed = jnp.zeros((size, local_width), FULL)
        for lanes in all_lanes:
            query = qkv_ref[0, start:stop, :] * (lanes * HEAD_DIM ** (-0.5))
            scores = nt(query, qkv_ref[1, :stop, :])
            scores = jnp.where(allowed, scores, MASKED_SCORE)
            terms = jnp.exp(scores - jnp.max(scores, axis=-1, keepdims=True))
            inverse = 1.0 / jnp.sum(terms, axis=-1, keepdims=True)
            probs = (terms * inverse).astype(LOW)
            mixed = mixed + nn(probs, qkv_ref[2, :stop, :] * lanes)
        mixed = mixed.astype(LOW)
        o_ref[start:stop, :] = mixed
        heads_sum.put(number, nt(mixed, w4[3]))
        if number + 1 < BLOCKS:
            heads_sum.cross(number + 1)
        advance(1)
    heads_sum.cross(0)

    def summed(number):
        attended = a_total[number].reshape(size, width).astype(FULL)
        x_rows = x_ref[rows_at(number), :].astype(FULL)
        summed_rows = (x_rows + attended).astype(LOW).astype(FULL)
        inverse = mean_square_inverse(summed_rows)
        return summed_rows * inverse, inverse

    def kept(which, number):
        return which // 2, slice((which % 2) * slots + number * size, (which % 2) * slots + (number + 1) * size)

    def kept_all(which):
        return table[which // 2, (which % 2) * slots : (which % 2 + 1) * slots, :]

    heads_sum.finish(BLOCKS - 1)
    advance(2)
    if joined:
        arrive(1)
    for number in downward:
        if number > 0:
            heads_sum.finish(number - 1)
        heads_sum.arrived(number)
        inner = (summed(number)[0] * gain_row).astype(LOW)
        up = nn(inner, weight(1))
        square = up * up
        bent = jnp.tanh(0.7978845608028654 * (up + 0.044715 * square * up))
        half = 0.5 * (1.0 + bent)
        which, spot = kept(0, number)
        table[which, spot, :] = (up * half).astype(LOW)
        which, spot = kept(1, number)
        table[which, spot, :] = inner
        slope_ref[rows_at(number), :] = half + 0.5 * up * (1.0 - bent * bent) * (
            0.7978845608028654 * (1.0 + 3.0 * 0.044715 * square)
        )
        advance(1)
    advance(len(steps))

    if joined:
        arrive(2)
    for number in downward:
        rows = rows_at(number)
        gate = gate_of(x_ref[rows, :].astype(FULL), router_row)
        branch = (gate * dy_ref[rows, :].astype(FULL)).astype(LOW)
        up_low = (nn(branch, weight(2)) * slope_ref[rows, :]).astype(LOW)
        hidden_sum.put(number, nt(up_low, weight(1)))
        which, spot = kept(2, number)
        table[which, spot, :] = branch
        which, spot = kept(3, number)
        table[which, spot, :] = up_low
        if number + 1 < BLOCKS:
            hidden_sum.cross(number + 1)
        which, spot = kept(0, number)
        branch_sum.put(number, nt(table[which, spot, :], weight(2)))
    hidden_sum.cross(0)
    give(2, tn(kept_all(2), kept_all(0)))
    give(1, tn(kept_all(1), kept_all(3)))

    out_acc[...] = jnp.zeros_like(out_acc)
    dkv[...] = jnp.zeros_like(dkv)
    vacc[...] = jnp.zeros_like(vacc)
    hidden_sum.finish(BLOCKS - 1)

    for number in downward:
        rows = rows_at(number)
        start, stop = number * size, (number + 1) * size
        if number > 0:
            hidden_sum.finish(number - 1)
        hidden_sum.arrived(number)
        normed, inverse = summed(number)
        grad = h_total[number].reshape(size, width).astype(FULL)
        vacc[1:2, :] += jnp.sum(grad * normed, axis=0, keepdims=True)
        scaled = grad * gain_row
        back = inverse * (scaled - normed * jnp.mean(scaled * normed, axis=-1, keepdims=True))
        back_low = back.astype(LOW)
        dz_ref[rows, :] = back_low
        gate = gate_of(x_ref[rows, :].astype(FULL), router_row)
        attn = (gate * dy_ref[rows, :].astype(FULL) + back_low.astype(FULL)).astype(LOW)
        do_rows = nn(attn, w4[3]).astype(LOW)
        out_acc[...] += tn(attn, o_ref[rows, :])
        if number + 1 < BLOCKS:
            input_sum.cross(number + 1)

        own = start + lax.broadcasted_iota(jnp.int32, (1, size), 1)
        keys = lax.broadcasted_iota(jnp.int32, (stop, size), 0)
        allowed = keys <= jnp.minimum(own, count - 1)
        dq = jnp.zeros((size, local_width), FULL)
        for lanes in all_lanes:
            query = qkv_ref[0, start:stop, :] * (lanes * HEAD_DIM ** (-0.5))
            mixed_grad = do_rows * lanes
            scores = nt(qkv_ref[1, :stop, :], query)
            scores = jnp.where(allowed, scores, MASKED_SCORE)
            terms = jnp.exp(scores - jnp.max(scores, axis=0, keepdims=True))
            total = 1.0 / jnp.sum(terms, axis=0, keepdims=True)
            probs = terms * total
            prob_grad = nt(qkv_ref[2, :stop, :], mixed_grad)
            dots = jnp.sum(prob_grad * probs, axis=0, keepdims=True)
            score_grad = (probs * (prob_grad - dots)).astype(LOW)
            dkv[1, :stop, :] += nn(probs.astype(LOW), mixed_grad)
            dkv[0, :stop, :] += nn(score_grad, query)
            dq = dq + tn(score_grad, qkv_ref[1, :stop, :] * lanes)
        dlow[0, rows, :] = (dq * HEAD_DIM ** (-0.5)).astype(LOW)
        dlow[1, rows, :] = dkv[0, rows, :].astype(LOW)
        dlow[2, rows, :] = dkv[1, rows, :].astype(LOW)
        part_sum = nt(dlow[0, rows, :], w4[0])
        part_sum += nt(dlow[1, rows, :], w4[1])
        part_sum += nt(dlow[2, rows, :], w4[2])
        heads_sum.drain(number)
        input_sum.put(number, part_sum)
        branch_sum.cross(number)
        if joined and number == BLOCKS - 2:
            relay(2)
    input_sum.cross(0)

    for number in range(BLOCKS):
        which, spot = kept(0, number)
        table[which, spot, :] = (first_norm(number)[1] * first_gain).astype(LOW)
    blocks = [tn(kept_all(0), dlow[t]) for t in range(3)]
    blocks.append(out_acc[...])
    give(0, jnp.concatenate(blocks, axis=1))
    if joined:
        relay(1)

    branch_sum.finish(BLOCKS - 1)
    input_sum.finish(BLOCKS - 1)
    for number in downward:
        rows = rows_at(number)
        if number > 0:
            branch_sum.finish(number - 1)
            input_sum.finish(number - 1)
        elif joined:
            relay(0)
        branch_sum.arrived(number)
        x_rows, normed, inverse = first_norm(number)
        dy_rows = dy_ref[rows, :].astype(FULL)
        added = a_total[number].reshape(size, width).astype(FULL)
        added = added + m_total[number].reshape(size, width).astype(FULL)
        gate = gate_of(x_rows, router_row)
        gate_grad = jnp.sum(dy_rows * added, axis=-1, keepdims=True)
        logit_grad = gate_grad * gate * (1.0 - gate) * width ** (-0.5)
        branch_sum.drain(number)
        m_total[number] = (x_rows + gate * added).astype(LOW).reshape(2, size // 2, width)
        input_sum.arrived(number)
        grad = d_total[number].reshape(size, width).astype(FULL)
        vacc[0:1, :] += jnp.sum(grad * normed, axis=0, keepdims=True)
        vacc[2:3, :] += jnp.sum(logit_grad * x_rows, axis=0, keepdims=True)
        scaled = grad * first_gain
        back = inverse * (scaled - normed * jnp.mean(scaled * normed, axis=-1, keepdims=True))
        dx_rows = dy_rows + dz_ref[rows, :].astype(FULL) + back + logit_grad * router_row
        input_sum.drain(number)
        d_total[number] = dx_rows.astype(LOW).reshape(2, size // 2, width)

    if joined:
        share = width // groups
        for d in range(groups):
            vpad[d, :, :share] = vacc[:, d * share : (d + 1) * share]
        for j in range(1, groups):
            to_all(j).start()
        for k in (2, 1, 0):
            collect(k)
        total = vpad[me]
        for j in range(1, groups):
            to_all(j).wait_recv()
            total = total + vr[j - 1]
        vsum_ref[...] = total
        for k in range(3):
            drain_weights(k)
            for z in range(line):
                to_pair(k, z).wait_send()
            for j in range(1, line):
                to_line(k, j).wait_send()
        drain_weights(3)
        for j in range(1, groups):
            to_all(j).wait_send()
    else:
        vsum_ref[...] = vacc[...]
    for number in range(BLOCKS):
        hidden_sum.drain(number)


def place_kernel(count_ref, sel_ref, tok_ref, cot_ref, y_ref, dx_ref, out_ref, grad_ref):
    rows, width = tok_ref.shape
    slots = y_ref.shape[0]
    spots = pl.program_id(0) * rows + lax.broadcasted_iota(jnp.int32, (rows, slots), 0)
    ids = lax.broadcasted_iota(jnp.int32, (1, slots), 1)
    chosen = jnp.where(ids < count_ref[0], sel_ref[...], -1)
    hot = (spots == chosen).astype(FULL)
    hit = jnp.max(hot, axis=-1, keepdims=True) > 0.5
    hot = hot.astype(LOW)
    out_ref[...] = jnp.where(hit, nn(hot, y_ref[...]), tok_ref[...].astype(FULL)).astype(LOW)
    grad_ref[...] = jnp.where(hit, nn(hot, dx_ref[...]), cot_ref[...].astype(FULL))


def adam_update(master, first_moment, second_moment, gradient, step_rate, decay_rate):
    first_new = MOMENT_DECAY * first_moment + (1.0 - MOMENT_DECAY) * gradient
    second_new = SQUARE_DECAY * second_moment + (1.0 - SQUARE_DECAY) * gradient * gradient
    first_hat = first_new / (1.0 - MOMENT_DECAY**STEP)
    second_hat = second_new / (1.0 - SQUARE_DECAY**STEP)
    master_new = master - step_rate * (
        first_hat / (jnp.sqrt(second_hat) + ADAM_EPS) + decay_rate * master
    )
    return (master_new, first_new, second_new)


def shape(dims, kind):
    return jax.ShapeDtypeStruct(dims, kind)


IN_VMEM = pl.BlockSpec(memory_space=pltpu.VMEM)
IN_SMEM = pl.BlockSpec(memory_space=pltpu.SMEM)
IN_ANY = pl.BlockSpec(memory_space=pl.ANY)
DMA = pltpu.SemaphoreType.DMA


def params(number=None):
    if number is None:
        return pltpu.CompilerParams(vmem_limit_bytes=VMEM_BYTES)
    return pltpu.CompilerParams(
        vmem_limit_bytes=VMEM_BYTES, collective_id=number, has_side_effects=True
    )


def local(
    tokens,
    cotangent,
    capacity,
    selected,
    qkv_master,
    out_master,
    up_master,
    down_master,
    vec_master,
    qkv_first,
    out_first,
    up_first,
    down_first,
    vec_first,
    qkv_second,
    out_second,
    up_second,
    down_second,
    vec_second,
):
    groups = lax.axis_size("dp")
    me = lax.axis_index("dp")
    share, local_width = qkv_master.shape[1:]
    hidden = up_master.shape[1]
    width = tokens.shape[2]
    seq_len = tokens.shape[1]
    slots = selected.shape[1]
    joined = share % 16 == 0 and groups % 2 == 0
    count = lax.dynamic_slice_in_dim(capacity, me, 1)
    sel_column = selected.reshape(slots, 1)
    token_rows, cot_rows = tokens[0], cotangent[0]
    line = groups // 2

    first_shard = jnp.concatenate(
        [qkv_master[0], qkv_master[1], qkv_master[2], out_master.T], axis=1
    )
    shard = jnp.stack([first_shard, up_master, down_master.T]).astype(LOW)

    quarter = slots // BLOCKS
    half_block = pltpu.VMEM((BLOCKS, quarter // 2, width), LOW)
    both_halves = pltpu.VMEM((BLOCKS, 2, quarter // 2, width), LOW)
    hops = DMA((2, 3, BLOCKS))
    exchange = [both_halves, half_block, half_block, half_block]
    scratch = [
        pltpu.VMEM((2, seq_len, width), LOW),
        DMA((2,)),
        pltpu.VMEM((slots, width), LOW),
        pltpu.VMEM((slots, width), LOW),
        pltpu.VMEM((3, slots, local_width), LOW),
        pltpu.VMEM((slots, local_width), LOW),
        pltpu.VMEM((4, width, local_width), LOW),
        *exchange,
        both_halves,
        hops,
        hops,
        *exchange,
        both_halves,
        hops,
        *exchange,
        hops,
        pltpu.VMEM((slots, hidden), FULL),
        pltpu.VMEM((slots, width), LOW),
        pltpu.VMEM((slots, local_width), LOW),
        pltpu.VMEM((width, local_width), FULL),
        pltpu.VMEM((2, slots, local_width), FULL),
        pltpu.VMEM((3, slots, local_width), LOW),
        pltpu.VMEM((8, width), FULL),
    ]
    if joined:
        weights = shard
        vectors = jnp.pad(vec_master.astype(LOW), ((0, 13), (0, 128 - share)))
        scratch += [
            pltpu.VMEM((3, groups, share, width), LOW),
            pltpu.VMEM((8, width), FULL),
            pltpu.VMEM((groups, 16, 128), LOW),
            DMA((4, line - 1)),
            DMA((4, line - 1)),
            DMA((4, line - 1)),
            DMA((4, line - 1)),
            DMA((4, line)),
            DMA((4, line)),
            pltpu.VMEM((3, groups, share, width), LOW),
            pltpu.VMEM((3, line, share, width), LOW),
            pltpu.VMEM((3, line, share, width), LOW),
            pltpu.VMEM((3, line - 1, share, width), LOW),
            pltpu.VMEM((groups, 8, 128), FULL),
            pltpu.VMEM((groups - 1, 8, 128), FULL),
            DMA((3, line)),
            DMA((3, line)),
            DMA((3, line - 1)),
            DMA((3, line - 1)),
            DMA((groups - 1,)),
            DMA((groups - 1,)),
        ]
    else:
        weights = lax.all_gather(shard, "dp", axis=1, tiled=True)
        vectors = lax.all_gather(vec_master.astype(LOW), "dp", axis=1, tiled=True)
        vectors = jnp.pad(vectors.astype(FULL), ((0, 5), (0, 0)))
    y_rows, dx_rows, grad_sum, vec_sum = pl.pallas_call(
        functools.partial(main_kernel, groups, joined),
        out_shape=[
            shape((BLOCKS, 2, quarter // 2, width), LOW),
            shape((BLOCKS, 2, quarter // 2, width), LOW),
            shape((3, share if joined else width, width), FULL),
            shape((8, 128 if joined else width), FULL),
        ],
        in_specs=[IN_SMEM, IN_VMEM, IN_ANY, IN_ANY, IN_VMEM, IN_VMEM],
        out_specs=[IN_VMEM] * 4,
        scratch_shapes=scratch,
        compiler_params=params(0),
        name="main",
    )(capacity, sel_column, token_rows, cot_rows, weights, vectors)
    y_rows, dx_rows = (rows.reshape(slots, width) for rows in (y_rows, dx_rows))

    spot_rows = min(256, seq_len)
    by_spot = pl.BlockSpec((spot_rows, width), lambda i: (i, 0))
    block_out, input_grad = pl.pallas_call(
        place_kernel,
        grid=(seq_len // spot_rows,),
        out_shape=[shape((seq_len, width), LOW), shape((seq_len, width), FULL)],
        in_specs=[
            IN_SMEM,
            pl.BlockSpec((1, slots), lambda i: (0, 0)),
            by_spot,
            by_spot,
            pl.BlockSpec((slots, width), lambda i: (0, 0)),
            pl.BlockSpec((slots, width), lambda i: (0, 0)),
        ],
        out_specs=[by_spot, by_spot],
        compiler_params=params(),
        name="place",
    )(count, selected, token_rows, cot_rows, y_rows, dx_rows)

    if joined:
        vec_grad = vec_sum[:3, :share]
    else:
        grad_sum = lax.psum_scatter(grad_sum, "dp", scatter_dimension=1, tiled=True)
        vec_grad = lax.psum_scatter(vec_sum[:3], "dp", scatter_dimension=1, tiled=True)
    first_sum = grad_sum[0]
    qkv_sum = jnp.stack(
        [first_sum[:, t * local_width : (t + 1) * local_width] for t in range(3)]
    )
    out_sum = first_sum[:, 3 * local_width :].T
    qkv_res = adam_update(qkv_master, qkv_first, qkv_second, qkv_sum, RATE_MATRIX, WEIGHT_DECAY)
    out_res = adam_update(out_master, out_first, out_second, out_sum, RATE_MATRIX, WEIGHT_DECAY)
    up_res = adam_update(up_master, up_first, up_second, grad_sum[1], RATE_MATRIX, WEIGHT_DECAY)
    down_res = adam_update(
        down_master, down_first, down_second, grad_sum[2].T, RATE_MATRIX, WEIGHT_DECAY
    )
    vec_res = adam_update(vec_master, vec_first, vec_second, vec_grad, RATE_VECTOR, 0.0)
    results = (qkv_res, out_res, up_res, down_res, vec_res)
    return (
        block_out[None],
        input_grad[None],
        *(res[0] for res in results),
        *(res[1] for res in results),
        *(res[2] for res in results),
    )


def solution(mesh):
    weights = (
        P(None, "dp", "mp"),
        P("mp", "dp"),
        P("dp", "mp"),
        P("mp", "dp"),
        P(None, "dp"),
    )
    rows = (P("dp", None, None), P("dp", None, None))
    return jax.shard_map(
        local,
        mesh=mesh,
        in_specs=(*rows, P(), P("dp", None), *weights * 3),
        out_specs=(*rows, *weights * 3),
        check_vma=False,
    )
```

```python
import functools

import jax
import jax.numpy as jnp
from jax import lax
from jax.experimental import pallas as pl
from jax.experimental.pallas import tpu as pltpu
from jax.sharding import PartitionSpec as P

HEAD_DIM = 64
STEP = 10
NORM_EPS = 1e-05
MASKED_SCORE = -1000000000.0
MOMENT_DECAY = 0.9
SQUARE_DECAY = 0.95
ADAM_EPS = 1e-08
WEIGHT_DECAY = 0.1
RATE_MATRIX = 0.06
RATE_VECTOR = 0.2

LOW = jnp.bfloat16
FULL = jnp.float32
MESH = pl.DeviceIdType.MESH
BLOCKS = 4
AROUND = (2,)
SPOT_ROWS = 512
VMEM_BYTES = 60 * 2**20


def nn(a, b):
    return lax.dot_general(a, b, (((1,), (0,)), ((), ())), preferred_element_type=FULL)


def nt(a, b):
    return lax.dot_general(a, b, (((1,), (1,)), ((), ())), preferred_element_type=FULL)


def tn(a, b):
    return lax.dot_general(a, b, (((0,), (0,)), ((), ())), preferred_element_type=FULL)


def mean_square_inverse(values):
    return lax.rsqrt(jnp.mean(values * values, axis=-1, keepdims=True) + NORM_EPS)


def gate_of(rows, router_row):
    width = rows.shape[-1]
    logit = jnp.sum(rows * router_row, axis=-1, keepdims=True) * width ** (-0.5)
    return jax.nn.sigmoid(logit)


def greet(partners):
    barrier = pltpu.get_barrier_semaphore()
    for partner in partners:
        pl.semaphore_signal(barrier, inc=1, device_id=partner, device_id_type=MESH)
    pl.semaphore_wait(barrier, len(partners))


def remote(src, dst, send_sem, recv_sem, device):
    return pltpu.make_async_remote_copy(
        src_ref=src,
        dst_ref=dst,
        send_sem=send_sem,
        recv_sem=recv_sem,
        device_id=device,
        device_id_type=MESH,
    )


class Exchange:
    def __init__(self, parts, near, pair, far, total, sems):
        self.parts, self.near, self.pair, self.far, self.total = parts, near, pair, far, total
        self.sems = sems
        self.me, self.part = lax.axis_index("dp"), lax.axis_index("mp")
        self.half = self.part % 2
        self.near_device = (self.me, self.part + 1 - 2 * self.half)
        self.far_device = (self.me, (self.part + 2) % 4)

    def copy(self, which, block, src, dst):
        device = self.far_device if which == 1 else self.near_device
        return remote(src, dst, self.sems.at[0, which, block], self.sems.at[1, which, block], device)

    def out(self, which, block):
        if which == 0:
            return self.copy(0, block, self.parts.at[block, 1 - self.half], self.near.at[block])
        if which == 1:
            return self.copy(1, block, self.pair.at[block], self.far.at[block])
        spot = self.total.at[block, self.half]
        return self.copy(2, block, spot, spot)

    def into(self, which, block):
        spot = (self.near.at[block], self.far.at[block], self.total.at[block, 1 - self.half])[which]
        return self.copy(which, block, spot, spot)

    def put(self, block, value):
        rows, width = value.shape
        self.parts[block] = value.astype(LOW).reshape(2, rows // 2, width)
        self.send(block)

    def send(self, block):
        self.out(0, block).start()

    def cross(self, block):
        self.into(0, block).wait_recv()
        self.pair[block] = (
            self.parts[block, self.half].astype(FULL) + self.near[block].astype(FULL)
        ).astype(LOW)
        self.out(1, block).start()

    def finish(self, block):
        self.into(1, block).wait_recv()
        self.total[block, self.half] = (
            self.pair[block].astype(FULL) + self.far[block].astype(FULL)
        ).astype(LOW)
        self.out(2, block).start()

    def arrived(self, block):
        self.into(2, block).wait_recv()

    def drain(self, block):
        for which in range(3):
            self.out(which, block).wait_send()


def head_lanes(width, head):
    lanes = lax.broadcasted_iota(jnp.int32, (1, width), 1)
    return (lanes // HEAD_DIM == head).astype(FULL).astype(LOW)


def main_kernel(groups, joined, *refs):
    (cap_ref, sel_ref, tok_any, cot_any), refs = refs[:4], refs[4:]
    if joined:
        masters, refs = refs[:5], refs[5:]
    else:
        (wg, gains), refs = refs[:2], refs[2:]
    (m_total, d_total, gsum_ref, vsum_ref), refs = refs[:4], refs[4:]
    (table, table_sems, x_ref, dy_ref, qkv_ref, o_ref, w4), refs = refs[:7], refs[7:]
    (parts, near, pair, far, a_total, a_sems, d_sems), refs = refs[:7], refs[7:]
    (h_parts, h_near, h_pair, h_far, h_total, h_sems), refs = refs[:6], refs[6:]
    (m_parts, m_near, m_pair, m_far, m_sems), refs = refs[:5], refs[5:]
    (slope_ref, dz_ref, out_acc, dkv, dlow, vacc), refs = refs[:6], refs[6:]

    slots, width = x_ref.shape
    seq_len = tok_any.shape[0]
    local_width = o_ref.shape[1]
    heads = local_width // HEAD_DIM
    size = slots // BLOCKS
    me, part = lax.axis_index("dp"), lax.axis_index("mp")
    count = cap_ref[me]
    downward = tuple(reversed(range(BLOCKS)))

    def rows_at(number):
        return slice(number * size, (number + 1) * size)

    def table_copy(which, source):
        return pltpu.make_async_copy(source, table.at[which], table_sems.at[which])

    table_copy(0, tok_any).start()
    table_copy(1, cot_any).start()

    heads_sum = Exchange(parts, near, pair, far, a_total, a_sems)
    hidden_sum = Exchange(h_parts, h_near, h_pair, h_far, h_total, h_sems)
    branch_sum = Exchange(m_parts, m_near, m_pair, m_far, m_total, m_sems)
    input_sum = Exchange(parts, near, pair, far, d_total, d_sems)
    partners = [heads_sum.near_device, heads_sum.far_device]

    if joined:
        (wg, gains, vg, send_r, recv_r, send_l, recv_l, send_f, recv_f), refs = refs[:9], refs[9:]
        (send_e, recv_e), refs = refs[:2], refs[2:]
        (grads, ry, pairs, rz, vpad, vr), refs = refs[:6], refs[6:]
        send_y, recv_y, send_z, recv_z, send_v, recv_v = refs
        line, place, side = groups // 2, me // 2, me % 2
        other = (me + 1 - 2 * side, part)
        everyone = [(lax.rem(me + j, groups), part) for j in range(1, groups)]

        def slot(k, d):
            return vg.at[d] if k == 3 else wg.at[k, d]

        def chain(k, step, right):
            z = place - step + 1 if right else place + step - 1
            sems = (send_r, recv_r) if right else (send_l, recv_l)
            target = (me + 2 if right else me - 2, part)
            return remote(
                slot(k, z * 2 + side),
                slot(k, z * 2 + side),
                sems[0].at[k, step - 1],
                sems[1].at[k, step - 1],
                target,
            )

        def chain_in(k, step, right):
            z = place - step if right else place + step
            sems = (send_r, recv_r) if right else (send_l, recv_l)
            spot = slot(k, z * 2 + side)
            return remote(spot, spot, sems[0].at[k, step - 1], sems[1].at[k, step - 1], other)

        def can_send(step, right):
            if right:
                return (place + 1 < line) & (place - step + 1 >= 0)
            return (place >= 1) & (place + step - 1 < line)

        def across(k, z):
            spot = slot(k, z * 2 + side)
            return remote(spot, spot, send_f.at[k, z], recv_f.at[k, z], other)

        def across_in(k, z):
            spot = slot(k, z * 2 + 1 - side)
            return remote(spot, spot, send_f.at[k, z], recv_f.at[k, z], other)

        def begin_line(k):
            for right in (True, False):

                @pl.when(can_send(1, right))
                def _():
                    chain(k, 1, right).start()

        def begin_across(k):
            across(k, place).start()

        def round_about(k, z):
            if k not in AROUND:
                return False
            return ((place == 0) & (z == 1)) | ((place == line - 1) & (z == line - 2))

        def around(k, right):
            spot = slot(k, me + 1 - 2 * side)
            target = (me + 2 if right else me - 2, part)
            return remote(spot, spot, send_e.at[k], recv_e.at[k], target)

        def around_in(k, right):
            spot = slot(k, (me - 2 if right else me + 2) + 1 - 2 * side)
            return remote(spot, spot, send_e.at[k], recv_e.at[k], other)

        def turn(k):
            across_in(k, place).wait_recv()

            @pl.when(place == 1)
            def _():
                around(k, False).start()

            @pl.when(place == line - 2)
            def _():
                around(k, True).start()

        def pump(k, step):
            for right in (True, False):
                z = place - step if right else place + step

                @pl.when((z >= 0) & (z < line))
                def _():
                    chain_in(k, step, right).wait_recv()

                    if k in AROUND:

                        @pl.when(jnp.logical_not(round_about(k, z)))
                        def _():
                            across(k, z).start()

                    else:
                        across(k, z).start()

                if step + 1 < line:

                    @pl.when(can_send(step + 1, right))
                    def _():
                        chain(k, step + 1, right).start()

        def arrive(k):
            for z in range(line):
                if k in AROUND:

                    @pl.when(jnp.logical_not(round_about(k, z)) & (place != z))
                    def _():
                        across_in(k, z).wait_recv()

                else:
                    across_in(k, z).wait_recv()
            if k in AROUND:

                @pl.when(place == 0)
                def _():
                    around_in(k, False).wait_recv()

                @pl.when(place == line - 1)
                def _():
                    around_in(k, True).wait_recv()

        def drain_weights(k):
            for right in (True, False):
                for step in range(1, line):

                    @pl.when(can_send(step, right))
                    def _():
                        chain(k, step, right).wait_send()

            for z in range(line):
                if k in AROUND:

                    @pl.when(jnp.logical_not(round_about(k, z)))
                    def _():
                        across(k, z).wait_send()

                else:
                    across(k, z).wait_send()
            if k in AROUND:

                @pl.when(place == 1)
                def _():
                    around(k, False).wait_send()

                @pl.when(place == line - 2)
                def _():
                    around(k, True).wait_send()

        def plane(j):
            return lax.rem(place + j, line)

        def to_pair(k, j):
            spot = plane(j) * 2 + 1 - side
            return remote(
                grads.at[k, spot], ry.at[k, j - 1], send_y.at[k, j - 1], recv_y.at[k, j - 1], other
            )

        def to_line(k, j):
            return remote(
                pairs.at[k, j - 1],
                rz.at[k, j - 1],
                send_z.at[k, j - 1],
                recv_z.at[k, j - 1],
                (plane(j) * 2 + side, part),
            )

        def keep(k, value):
            grads[k] = value.astype(LOW).reshape(groups, width // groups, width)

        def give(k):
            for j in range(1, line + 1):
                to_pair(k, j).start()

        def relay(k, *which):
            for j in which:
                to_pair(k, j).wait_recv()
                own = grads[k, plane(j) * 2 + side].astype(FULL)
                pairs[k, j - 1] = (own + ry[k, j - 1].astype(FULL)).astype(LOW)
                if j < line:
                    to_line(k, j).start()

        def collect(k):
            total = pairs[k, line - 1].astype(FULL)
            for j in range(1, line):
                to_line(k, j).wait_recv()
                total = total + rz[k, j - 1].astype(FULL)
            gsum_ref[k] = total

        def to_all(j):
            target = lax.rem(me + j, groups)
            return remote(
                vpad.at[target], vr.at[j - 1], send_v.at[j - 1], recv_v.at[j - 1], (target, part)
            )

        qkv_m, out_m, up_m, down_m, vec_m = masters
        share = width // groups
        vg[me] = jnp.zeros((8, 128), FULL)
        vg[me, 0:3, :share] = vec_m[...].astype(LOW).astype(FULL)
        columns = [qkv_m[t] for t in range(3)] + [out_m[...].T]
        wg[0, me] = jnp.concatenate(columns, axis=1).astype(LOW)
        greet(partners + everyone)
        for k in (3, 0):
            begin_line(k)
            begin_across(k)
        wg[1, me] = up_m[...].astype(LOW)
        begin_across(1)
        wg[2, me] = down_m[...].astype(LOW)
        steps = [(k, step) for k in (0, 1, 2) for step in range(1, line)]
    else:
        greet(partners)
        steps = []

        def keep(k, value):
            gsum_ref[k] = value

        def give(k):
            pass

        def relay(k, *which):
            pass

    def advance(number):
        for _ in range(number):
            if steps:
                k, step = steps.pop(0)
                pump(k, step)
                if k == 0:
                    pump(3, step)
                if step == 1 and k < 2:
                    begin_line(k + 1)
                if step == line - 1 and k == 0:
                    begin_across(2)
                if step == 1 and k in AROUND:
                    turn(k)

    def pick(number, which, dead_zero, out_ref):
        block = 2 * size
        rows = slice(number * block, (number + 1) * block)
        spots = lax.broadcasted_iota(jnp.int32, (block, seq_len), 1)
        hot = (spots == sel_column[rows, :]).astype(FULL).astype(LOW)
        got = nn(hot, table[which])
        if dead_zero:
            ids = number * block + lax.broadcasted_iota(jnp.int32, (block, 1), 0)
            got = jnp.where(ids < count, got, 0.0)
        out_ref[rows, :] = got.astype(LOW)

    sel_column = jnp.broadcast_to(sel_ref[...].astype(FULL), (8, slots)).T[:, 0:1].astype(jnp.int32)
    table_copy(0, tok_any).wait()
    pick(0, 0, False, x_ref)
    pick(1, 0, False, x_ref)
    advance(1)
    table_copy(1, cot_any).wait()
    pick(0, 1, True, dy_ref)
    pick(1, 1, True, dy_ref)
    advance(2)

    if joined:
        arrive(3)
        arrive(0)
        gains[...] = jnp.concatenate([vg[d][:, :share] for d in range(groups)], axis=1)

    first_gain, gain_row, router_row = gains[0:1, :], gains[1:2, :], gains[2:3, :]

    def weight(k):
        return wg[k].reshape(width, wg.shape[-1])

    w_first = weight(0)
    for t in range(4):
        w4[t] = w_first[:, t * local_width : (t + 1) * local_width]

    def first_norm(number):
        x_rows = x_ref[rows_at(number), :].astype(FULL)
        inverse = mean_square_inverse(x_rows)
        return x_rows, x_rows * inverse, inverse

    for number in downward:
        normed = (first_norm(number)[1] * first_gain).astype(LOW)
        for t in range(3):
            qkv_ref[t, rows_at(number), :] = nn(normed, w4[t]).astype(LOW)
    advance(1)


    for number in downward:
        start, stop = number * size, (number + 1) * size
        own = start + lax.broadcasted_iota(jnp.int32, (size, 1), 0)
        keys = lax.broadcasted_iota(jnp.int32, (size, stop), 1)
        allowed = keys <= jnp.minimum(own, count - 1)
        def forward_head(head, mixed):
            lanes = head_lanes(local_width, head)
            query = qkv_ref[0, start:stop, :] * (lanes * HEAD_DIM ** (-0.5))
            scores = nt(query, qkv_ref[1, :stop, :])
            scores = jnp.where(allowed, scores, MASKED_SCORE)
            terms = jnp.exp(scores - jnp.max(scores, axis=-1, keepdims=True))
            inverse = 1.0 / jnp.sum(terms, axis=-1, keepdims=True)
            probs = (terms * inverse).astype(LOW)
            return mixed + nn(probs, qkv_ref[2, :stop, :] * lanes)

        mixed = jnp.zeros((size, local_width), FULL)
        mixed = lax.fori_loop(0, heads, forward_head, mixed).astype(LOW)
        o_ref[start:stop, :] = mixed
        heads_sum.put(number, nt(mixed, w4[3]))
        if number + 1 < BLOCKS:
            heads_sum.cross(number + 1)
        advance(1)
    heads_sum.cross(0)

    def summed(number):
        attended = a_total[number].reshape(size, width).astype(FULL)
        x_rows = x_ref[rows_at(number), :].astype(FULL)
        summed_rows = (x_rows + attended).astype(LOW).astype(FULL)
        inverse = mean_square_inverse(summed_rows)
        return summed_rows * inverse, inverse

    def kept(which, number):
        return which // 2, slice((which % 2) * slots + number * size, (which % 2) * slots + (number + 1) * size)

    def kept_all(which):
        return table[which // 2, (which % 2) * slots : (which % 2 + 1) * slots, :]

    def up_phase(number):
        heads_sum.arrived(number)
        inner = (summed(number)[0] * gain_row).astype(LOW)
        up = nn(inner, weight(1))
        square = up * up
        bent = jnp.tanh(0.7978845608028654 * (up + 0.044715 * square * up))
        half = 0.5 * (1.0 + bent)
        which, spot = kept(0, number)
        table[which, spot, :] = (up * half).astype(LOW)
        which, spot = kept(1, number)
        table[which, spot, :] = inner
        slope_ref[rows_at(number), :] = half + 0.5 * up * (1.0 - bent * bent) * (
            0.7978845608028654 * (1.0 + 3.0 * 0.044715 * square)
        )

    def back_phase(number):
        rows = rows_at(number)
        gate = gate_of(x_ref[rows, :].astype(FULL), router_row)
        branch = (gate * dy_ref[rows, :].astype(FULL)).astype(LOW)
        up_low = (nn(branch, weight(2)) * slope_ref[rows, :]).astype(LOW)
        hidden_sum.put(number, nt(up_low, weight(1)))
        which, spot = kept(2, number)
        table[which, spot, :] = branch
        which, spot = kept(3, number)
        table[which, spot, :] = up_low
        if number + 1 < BLOCKS:
            hidden_sum.cross(number + 1)

    heads_sum.finish(3)
    advance(len(steps))
    if joined:
        arrive(1)
    heads_sum.finish(2)
    up_phase(3)
    heads_sum.finish(1)
    up_phase(2)
    up_phase(1)
    if joined:
        arrive(2)
    back_phase(3)
    heads_sum.finish(0)
    back_phase(2)
    up_phase(0)
    back_phase(1)
    back_phase(0)
    hidden_sum.cross(0)
    keep(2, tn(kept_all(2), kept_all(0)))
    give(2)
    keep(1, tn(kept_all(1), kept_all(3)))

    which, spot = kept(0, 3)
    branch_sum.put(3, nt(table[which, spot, :], weight(2)))
    out_acc[...] = jnp.zeros_like(out_acc)
    dkv[...] = jnp.zeros_like(dkv)
    vacc[...] = jnp.zeros_like(vacc)
    hidden_sum.finish(BLOCKS - 1)

    for number in downward:
        rows = rows_at(number)
        start, stop = number * size, (number + 1) * size
        if number > 0:
            hidden_sum.finish(number - 1)
        if number < 3:
            which, spot = kept(0, number)
            branch_sum.put(number, nt(table[which, spot, :], weight(2)))
        hidden_sum.arrived(number)
        normed, inverse = summed(number)
        grad = h_total[number].reshape(size, width).astype(FULL)
        vacc[1:2, :] += jnp.sum(grad * normed, axis=0, keepdims=True)
        scaled = grad * gain_row
        back = inverse * (scaled - normed * jnp.mean(scaled * normed, axis=-1, keepdims=True))
        back_low = back.astype(LOW)
        dz_ref[rows, :] = back_low
        gate = gate_of(x_ref[rows, :].astype(FULL), router_row)
        attn = (gate * dy_ref[rows, :].astype(FULL) + back_low.astype(FULL)).astype(LOW)
        do_rows = nn(attn, w4[3]).astype(LOW)
        out_acc[...] += tn(attn, o_ref[rows, :])
        if number + 1 < BLOCKS:
            input_sum.cross(number + 1)
        branch_sum.cross(number)

        own = start + lax.broadcasted_iota(jnp.int32, (1, size), 1)
        keys = lax.broadcasted_iota(jnp.int32, (stop, size), 0)
        allowed = keys <= jnp.minimum(own, count - 1)
        def backward_head(head, dq):
            lanes = head_lanes(local_width, head)
            query = qkv_ref[0, start:stop, :] * (lanes * HEAD_DIM ** (-0.5))
            mixed_grad = do_rows * lanes
            scores = nt(qkv_ref[1, :stop, :], query)
            scores = jnp.where(allowed, scores, MASKED_SCORE)
            terms = jnp.exp(scores - jnp.max(scores, axis=0, keepdims=True))
            total = 1.0 / jnp.sum(terms, axis=0, keepdims=True)
            probs = terms * total
            prob_grad = nt(qkv_ref[2, :stop, :], mixed_grad)
            dots = jnp.sum(prob_grad * probs, axis=0, keepdims=True)
            score_grad = (probs * (prob_grad - dots)).astype(LOW)
            dkv[1, :stop, :] += nn(probs.astype(LOW), mixed_grad)
            dkv[0, :stop, :] += nn(score_grad, query)
            return dq + tn(score_grad, qkv_ref[1, :stop, :] * lanes)

        dq = jnp.zeros((size, local_width), FULL)
        dq = lax.fori_loop(0, heads, backward_head, dq)
        dlow[0, rows, :] = (dq * HEAD_DIM ** (-0.5)).astype(LOW)
        dlow[1, rows, :] = dkv[0, rows, :].astype(LOW)
        dlow[2, rows, :] = dkv[1, rows, :].astype(LOW)
        part_sum = nt(dlow[0, rows, :], w4[0])
        part_sum += nt(dlow[1, rows, :], w4[1])
        part_sum += nt(dlow[2, rows, :], w4[2])
        heads_sum.drain(number)
        input_sum.put(number, part_sum)
        if joined:
            if number == 3:
                relay(2, 1, 2)
            elif number == 2:
                relay(2, *range(3, line + 1))
                give(1)
            elif number == 1:
                relay(1, 1)
            else:
                relay(1, 2)
    input_sum.cross(0)

    for number in range(BLOCKS):
        which, spot = kept(0, number)
        table[which, spot, :] = (first_norm(number)[1] * first_gain).astype(LOW)
    blocks = [tn(kept_all(0), dlow[t]) for t in range(3)]
    blocks.append(out_acc[...])
    keep(0, jnp.concatenate(blocks, axis=1))
    give(0)

    branch_sum.finish(BLOCKS - 1)
    input_sum.finish(BLOCKS - 1)
    for number in downward:
        rows = rows_at(number)
        if number > 0:
            branch_sum.finish(number - 1)
            input_sum.finish(number - 1)
        if joined:
            if number == 2:
                relay(1, *range(3, line + 1))
            elif number == 1:
                relay(0, 1, 2)
            elif number == 0:
                relay(0, *range(3, line + 1))
        branch_sum.arrived(number)
        x_rows, normed, inverse = first_norm(number)
        dy_rows = dy_ref[rows, :].astype(FULL)
        added = a_total[number].reshape(size, width).astype(FULL)
        added = added + m_total[number].reshape(size, width).astype(FULL)
        gate = gate_of(x_rows, router_row)
        gate_grad = jnp.sum(dy_rows * added, axis=-1, keepdims=True)
        logit_grad = gate_grad * gate * (1.0 - gate) * width ** (-0.5)
        branch_sum.drain(number)
        m_total[number] = (x_rows + gate * added).astype(LOW).reshape(2, size // 2, width)
        input_sum.arrived(number)
        grad = d_total[number].reshape(size, width).astype(FULL)
        vacc[0:1, :] += jnp.sum(grad * normed, axis=0, keepdims=True)
        vacc[2:3, :] += jnp.sum(logit_grad * x_rows, axis=0, keepdims=True)
        scaled = grad * first_gain
        back = inverse * (scaled - normed * jnp.mean(scaled * normed, axis=-1, keepdims=True))
        dx_rows = dy_rows + dz_ref[rows, :].astype(FULL) + back + logit_grad * router_row
        input_sum.drain(number)
        d_total[number] = dx_rows.astype(LOW).reshape(2, size // 2, width)

    if joined:
        for d in range(groups):
            vpad[d, :, :share] = vacc[:, d * share : (d + 1) * share]
        for j in range(1, groups):
            to_all(j).start()
        for k in (2, 1, 0):
            collect(k)
        total = vpad[me]
        for j in range(1, groups):
            to_all(j).wait_recv()
            total = total + vr[j - 1]
        vsum_ref[...] = total
        for k in range(3):
            drain_weights(k)
            for j in range(1, line + 1):
                to_pair(k, j).wait_send()
            for j in range(1, line):
                to_line(k, j).wait_send()
        drain_weights(3)
        for j in range(1, groups):
            to_all(j).wait_send()
    else:
        vsum_ref[...] = vacc[...]
    for number in range(BLOCKS):
        hidden_sum.drain(number)


def adam_update(master, first_moment, second_moment, gradient, step_rate, decay_rate):
    first_new = MOMENT_DECAY * first_moment + (1.0 - MOMENT_DECAY) * gradient
    second_new = SQUARE_DECAY * second_moment + (1.0 - SQUARE_DECAY) * gradient * gradient
    first_hat = first_new / (1.0 - MOMENT_DECAY**STEP)
    second_hat = second_new / (1.0 - SQUARE_DECAY**STEP)
    master_new = master - step_rate * (
        first_hat / (jnp.sqrt(second_hat) + ADAM_EPS) + decay_rate * master
    )
    return (master_new, first_new, second_new)


def last_kernel(cap_ref, sel_ref, tok_ref, cot_ref, y_ref, dx_ref, sum_ref, vsum_ref, *refs):
    olds, (out_ref, grad_ref), news = refs[:15], refs[15:17], refs[17:]
    rows, width = tok_ref.shape
    slots = y_ref.shape[0]
    spots = pl.program_id(0) * rows + lax.broadcasted_iota(jnp.int32, (rows, slots), 0)
    ids = lax.broadcasted_iota(jnp.int32, (1, slots), 1)
    chosen = jnp.where(ids < cap_ref[lax.axis_index("dp")], sel_ref[...], -1)
    hot = (spots == chosen).astype(FULL)
    hit = jnp.max(hot, axis=-1, keepdims=True) > 0.5
    hot = hot.astype(LOW)
    out_ref[...] = jnp.where(hit, nn(hot, y_ref[...]), tok_ref[...].astype(FULL)).astype(LOW)
    grad_ref[...] = jnp.where(hit, nn(hot, dx_ref[...]), cot_ref[...].astype(FULL))

    @pl.when(pl.program_id(0) == 0)
    def _():
        local_width = olds[0].shape[-1]
        share = olds[4].shape[1]
        first = sum_ref[0]
        parts = [first[:, t * local_width : (t + 1) * local_width] for t in range(4)]

        def step(number, gradient, rate, decay, t=None):
            old = [olds[number + 5 * i] for i in range(3)]
            new = [news[number + 5 * i] for i in range(3)]
            values = [ref[...] if t is None else ref[t] for ref in old]
            for ref, value in zip(new, adam_update(*values, gradient, rate, decay)):
                if t is None:
                    ref[...] = value
                else:
                    ref[t] = value

        for t in range(3):
            step(0, parts[t], RATE_MATRIX, WEIGHT_DECAY, t)
        step(1, parts[3].T, RATE_MATRIX, WEIGHT_DECAY)
        step(2, sum_ref[1], RATE_MATRIX, WEIGHT_DECAY)
        step(3, sum_ref[2], RATE_MATRIX, WEIGHT_DECAY)
        step(4, vsum_ref[0:3, :share], RATE_VECTOR, 0.0)


def shape(dims, kind):
    return jax.ShapeDtypeStruct(dims, kind)


IN_VMEM = pl.BlockSpec(memory_space=pltpu.VMEM)
IN_SMEM = pl.BlockSpec(memory_space=pltpu.SMEM)
IN_ANY = pl.BlockSpec(memory_space=pl.ANY)
DMA = pltpu.SemaphoreType.DMA


def params(number=None):
    if number is None:
        return pltpu.CompilerParams(vmem_limit_bytes=VMEM_BYTES)
    return pltpu.CompilerParams(
        vmem_limit_bytes=VMEM_BYTES, collective_id=number, has_side_effects=True
    )


def local(
    tokens,
    cotangent,
    capacity,
    selected,
    qkv_master,
    out_master,
    up_master,
    down_master,
    vec_master,
    qkv_first,
    out_first,
    up_first,
    down_first,
    vec_first,
    qkv_second,
    out_second,
    up_second,
    down_second,
    vec_second,
):
    groups = lax.axis_size("dp")
    me = lax.axis_index("dp")
    share, local_width = qkv_master.shape[1:]
    hidden = up_master.shape[1]
    width = tokens.shape[2]
    seq_len = tokens.shape[1]
    slots = selected.shape[1]
    joined = share % 16 == 0 and groups % 2 == 0 and groups >= 8
    token_rows, cot_rows = tokens[0], cotangent[0]
    line = groups // 2

    quarter = slots // BLOCKS
    half_block = pltpu.VMEM((BLOCKS, quarter // 2, width), LOW)
    both_halves = pltpu.VMEM((BLOCKS, 2, quarter // 2, width), LOW)
    hops = DMA((2, 3, BLOCKS))
    exchange = [both_halves, half_block, half_block, half_block]
    scratch = [
        pltpu.VMEM((2, seq_len, width), LOW),
        DMA((2,)),
        pltpu.VMEM((slots, width), LOW),
        pltpu.VMEM((slots, width), LOW),
        pltpu.VMEM((3, slots, local_width), LOW),
        pltpu.VMEM((slots, local_width), LOW),
        pltpu.VMEM((4, width, local_width), LOW),
        *exchange,
        both_halves,
        hops,
        hops,
        *exchange,
        both_halves,
        hops,
        *exchange,
        hops,
        pltpu.VMEM((slots, hidden), FULL),
        pltpu.VMEM((slots, width), LOW),
        pltpu.VMEM((width, local_width), FULL),
        pltpu.VMEM((2, slots, local_width), FULL),
        pltpu.VMEM((3, slots, local_width), LOW),
        pltpu.VMEM((8, width), FULL),
    ]
    if joined:
        weights = (qkv_master, out_master, up_master, down_master.T, vec_master)
        scratch += [
            pltpu.VMEM((3, groups, share, width), LOW),
            pltpu.VMEM((8, width), FULL),
            pltpu.VMEM((groups, 8, 128), FULL),
            DMA((4, line - 1)),
            DMA((4, line - 1)),
            DMA((4, line - 1)),
            DMA((4, line - 1)),
            DMA((4, line)),
            DMA((4, line)),
            DMA((3,)),
            DMA((3,)),
            pltpu.VMEM((3, groups, share, width), LOW),
            pltpu.VMEM((3, line, share, width), LOW),
            pltpu.VMEM((3, line, share, width), LOW),
            pltpu.VMEM((3, line - 1, share, width), LOW),
            pltpu.VMEM((groups, 8, 128), FULL),
            pltpu.VMEM((groups - 1, 8, 128), FULL),
            DMA((3, line)),
            DMA((3, line)),
            DMA((3, line - 1)),
            DMA((3, line - 1)),
            DMA((groups - 1,)),
            DMA((groups - 1,)),
        ]
    else:
        first_shard = jnp.concatenate(
            [qkv_master[0], qkv_master[1], qkv_master[2], out_master.T], axis=1
        )
        shard = jnp.stack([first_shard, up_master, down_master.T]).astype(LOW)
        vectors = lax.all_gather(vec_master.astype(LOW), "dp", axis=1, tiled=True)
        weights = (
            lax.all_gather(shard, "dp", axis=1, tiled=True),
            jnp.pad(vectors.astype(FULL), ((0, 5), (0, 0))),
        )
    y_rows, dx_rows, grad_sum, vec_sum = pl.pallas_call(
        functools.partial(main_kernel, groups, joined),
        out_shape=[
            shape((BLOCKS, 2, quarter // 2, width), LOW),
            shape((BLOCKS, 2, quarter // 2, width), LOW),
            shape((3, share if joined else width, width), FULL),
            shape((8, 128 if joined else width), FULL),
        ],
        in_specs=[IN_SMEM, IN_VMEM, IN_ANY, IN_ANY] + [IN_VMEM] * len(weights),
        out_specs=[IN_VMEM] * 4,
        scratch_shapes=scratch,
        compiler_params=params(0),
        name="main",
    )(capacity, selected, token_rows, cot_rows, *weights)
    y_rows, dx_rows = (rows.reshape(slots, width) for rows in (y_rows, dx_rows))

    if not joined:
        grad_sum = lax.psum_scatter(grad_sum, "dp", scatter_dimension=1, tiled=True)
        vec_sum = lax.psum_scatter(vec_sum, "dp", scatter_dimension=1, tiled=True)
    olds = (
        qkv_master, out_master, up_master, down_master.T, vec_master,
        qkv_first, out_first, up_first, down_first.T, vec_first,
        qkv_second, out_second, up_second, down_second.T, vec_second,
    )
    spot_rows = min(SPOT_ROWS, seq_len)
    by_spot = pl.BlockSpec((spot_rows, width), lambda i: (i, 0))

    def whole(array):
        return pl.BlockSpec(array.shape, lambda i: (0,) * array.ndim)

    block_out, input_grad, *news = pl.pallas_call(
        last_kernel,
        grid=(seq_len // spot_rows,),
        out_shape=[shape((seq_len, width), LOW), shape((seq_len, width), FULL)]
        + [shape(old.shape, FULL) for old in olds],
        in_specs=[IN_SMEM, whole(selected), by_spot, by_spot]
        + [whole(array) for array in (y_rows, dx_rows, grad_sum, vec_sum, *olds)],
        out_specs=[by_spot, by_spot] + [whole(old) for old in olds],
        compiler_params=params(),
        name="last",
    )(capacity, selected, token_rows, cot_rows, y_rows, dx_rows, grad_sum, vec_sum, *olds)
    for number in (3, 8, 13):
        news[number] = news[number].T
    return (block_out[None], input_grad[None], *news)


def solution(mesh):
    weights = (
        P(None, "dp", "mp"),
        P("mp", "dp"),
        P("dp", "mp"),
        P("mp", "dp"),
        P(None, "dp"),
    )
    rows = (P("dp", None, None), P("dp", None, None))
    return jax.shard_map(
        local,
        mesh=mesh,
        in_specs=(*rows, P(), P("dp", None), *weights * 3),
        out_specs=(*rows, *weights * 3),
        check_vma=False,
    )
```

```python
import functools

import jax
import jax.numpy as jnp
from jax import lax
from jax.experimental import pallas as pl
from jax.experimental.pallas import tpu as pltpu
from jax.sharding import PartitionSpec as P

HEAD_DIM = 64
STEP = 10
NORM_EPS = 1e-05
MASKED_SCORE = -1000000000.0
MOMENT_DECAY = 0.9
SQUARE_DECAY = 0.95
ADAM_EPS = 1e-08
WEIGHT_DECAY = 0.1
RATE_MATRIX = 0.06
RATE_VECTOR = 0.2

LOW = jnp.bfloat16
FULL = jnp.float32
MESH = pl.DeviceIdType.MESH
BLOCKS = 4
AROUND = (3,)
SPOT_ROWS = 512
VMEM_BYTES = 60 * 2**20


def nn(a, b):
    return lax.dot_general(a, b, (((1,), (0,)), ((), ())), preferred_element_type=FULL)


def nt(a, b):
    return lax.dot_general(a, b, (((1,), (1,)), ((), ())), preferred_element_type=FULL)


def tn(a, b):
    return lax.dot_general(a, b, (((0,), (0,)), ((), ())), preferred_element_type=FULL)


def mean_square_inverse(values):
    return lax.rsqrt(jnp.mean(values * values, axis=-1, keepdims=True) + NORM_EPS)


def gate_of(rows, router_row):
    width = rows.shape[-1]
    logit = jnp.sum(rows * router_row, axis=-1, keepdims=True) * width ** (-0.5)
    return jax.nn.sigmoid(logit)


def greet(partners):
    barrier = pltpu.get_barrier_semaphore()
    for partner in partners:
        pl.semaphore_signal(barrier, inc=1, device_id=partner, device_id_type=MESH)


def met(partners):
    pl.semaphore_wait(pltpu.get_barrier_semaphore(), len(partners))


def remote(src, dst, send_sem, recv_sem, device):
    return pltpu.make_async_remote_copy(
        src_ref=src,
        dst_ref=dst,
        send_sem=send_sem,
        recv_sem=recv_sem,
        device_id=device,
        device_id_type=MESH,
    )


class Exchange:
    def __init__(self, parts, near, pair, far, total, sems):
        self.parts, self.near, self.pair, self.far, self.total = parts, near, pair, far, total
        self.sems = sems
        self.me, self.part = lax.axis_index("dp"), lax.axis_index("mp")
        self.half = self.part % 2
        self.near_device = (self.me, self.part + 1 - 2 * self.half)
        self.far_device = (self.me, (self.part + 2) % 4)

    def copy(self, which, block, src, dst):
        device = self.far_device if which == 1 else self.near_device
        return remote(src, dst, self.sems.at[0, which, block], self.sems.at[1, which, block], device)

    def out(self, which, block):
        if which == 0:
            return self.copy(0, block, self.parts.at[block, 1 - self.half], self.near.at[block])
        if which == 1:
            return self.copy(1, block, self.pair.at[block], self.far.at[block])
        spot = self.total.at[block, self.half]
        return self.copy(2, block, spot, spot)

    def into(self, which, block):
        spot = (self.near.at[block], self.far.at[block], self.total.at[block, 1 - self.half])[which]
        return self.copy(which, block, spot, spot)

    def put(self, block, value):
        rows, width = value.shape
        self.parts[block] = value.astype(LOW).reshape(2, rows // 2, width)
        self.send(block)

    def send(self, block):
        self.out(0, block).start()

    def cross(self, block):
        self.into(0, block).wait_recv()
        self.pair[block] = (
            self.parts[block, self.half].astype(FULL) + self.near[block].astype(FULL)
        ).astype(LOW)
        self.out(1, block).start()

    def finish(self, block):
        self.into(1, block).wait_recv()
        self.total[block, self.half] = (
            self.pair[block].astype(FULL) + self.far[block].astype(FULL)
        ).astype(LOW)
        self.out(2, block).start()

    def arrived(self, block):
        self.into(2, block).wait_recv()

    def drain(self, block):
        for which in range(3):
            self.out(which, block).wait_send()


def head_lanes(width, head):
    lanes = lax.broadcasted_iota(jnp.int32, (1, width), 1)
    return (lanes // HEAD_DIM == head).astype(FULL).astype(LOW)


def main_kernel(groups, joined, *refs):
    (cap_ref, sel_ref, tok_any, cot_any), refs = refs[:4], refs[4:]
    if joined:
        masters, refs = refs[:5], refs[5:]
    else:
        (wg, gains), refs = refs[:2], refs[2:]
    (m_total, d_total, gsum_ref, vsum_ref), refs = refs[:4], refs[4:]
    (table, table_sems, x_ref, dy_ref, qkv_ref, o_ref, w4), refs = refs[:7], refs[7:]
    (parts, near, pair, far, a_total, a_sems, d_sems), refs = refs[:7], refs[7:]
    (h_parts, h_near, h_pair, h_far, h_total, h_sems), refs = refs[:6], refs[6:]
    (m_parts, m_near, m_pair, m_far, m_sems), refs = refs[:5], refs[5:]
    (slope_ref, dz_ref, out_acc, dkv, dlow, vacc, spot_ref, do_ref), refs = refs[:8], refs[8:]

    slots, width = x_ref.shape
    seq_len = tok_any.shape[0]
    local_width = o_ref.shape[1]
    heads = local_width // HEAD_DIM
    size = slots // BLOCKS
    me, part = lax.axis_index("dp"), lax.axis_index("mp")
    count = cap_ref[me]
    top = BLOCKS - 1

    def span(start):
        return pl.ds(pl.multiple_of(start, size), size)

    def rows_at(number):
        return span(number * size)

    def table_copy(which, source):
        return pltpu.make_async_copy(source, table.at[which], table_sems.at[which])

    table_copy(0, tok_any).start()
    table_copy(1, cot_any).start()

    heads_sum = Exchange(parts, near, pair, far, a_total, a_sems)
    hidden_sum = Exchange(h_parts, h_near, h_pair, h_far, h_total, h_sems)
    branch_sum = Exchange(m_parts, m_near, m_pair, m_far, m_total, m_sems)
    input_sum = Exchange(parts, near, pair, far, d_total, d_sems)
    partners = [heads_sum.near_device, heads_sum.far_device]

    if joined:
        (wg, gains, vg, send_r, recv_r, send_l, recv_l, send_f, recv_f), refs = refs[:9], refs[9:]
        (send_e, recv_e), refs = refs[:2], refs[2:]
        (grads, ry, pairs, rz, vpad, vr), refs = refs[:6], refs[6:]
        send_y, recv_y, send_z, recv_z, send_v, recv_v = refs
        line, place, side = groups // 2, me // 2, me % 2
        other = (me + 1 - 2 * side, part)
        everyone = [(lax.rem(me + j, groups), part) for j in range(1, groups)]

        half_share = width // groups // 2

        def slot(k, d):
            if k < 2:
                return wg.at[0, d, pl.ds(k * half_share, half_share)]
            return vg.at[d] if k == 4 else wg.at[k - 1, d]

        def chain(k, step, right):
            z = place - step + 1 if right else place + step - 1
            sems = (send_r, recv_r) if right else (send_l, recv_l)
            target = (me + 2 if right else me - 2, part)
            return remote(
                slot(k, z * 2 + side),
                slot(k, z * 2 + side),
                sems[0].at[k, step - 1],
                sems[1].at[k, step - 1],
                target,
            )

        def chain_in(k, step, right):
            z = place - step if right else place + step
            sems = (send_r, recv_r) if right else (send_l, recv_l)
            spot = slot(k, z * 2 + side)
            return remote(spot, spot, sems[0].at[k, step - 1], sems[1].at[k, step - 1], other)

        def can_send(step, right):
            if right:
                return (place + 1 < line) & (place - step + 1 >= 0)
            return (place >= 1) & (place + step - 1 < line)

        def across(k, z):
            spot = slot(k, z * 2 + side)
            return remote(spot, spot, send_f.at[k, z], recv_f.at[k, z], other)

        def across_in(k, z):
            spot = slot(k, z * 2 + 1 - side)
            return remote(spot, spot, send_f.at[k, z], recv_f.at[k, z], other)

        def begin_line(k):
            for right in (True, False):

                @pl.when(can_send(1, right))
                def _():
                    chain(k, 1, right).start()

        def begin_across(k):
            across(k, place).start()

        def round_about(k, z):
            if k not in AROUND:
                return False
            return ((place == 0) & (z == 1)) | ((place == line - 1) & (z == line - 2))

        def around(k, right):
            spot = slot(k, me + 1 - 2 * side)
            target = (me + 2 if right else me - 2, part)
            return remote(spot, spot, send_e.at[k], recv_e.at[k], target)

        def around_in(k, right):
            spot = slot(k, (me - 2 if right else me + 2) + 1 - 2 * side)
            return remote(spot, spot, send_e.at[k], recv_e.at[k], other)

        def turn(k):
            across_in(k, place).wait_recv()

            @pl.when(place == 1)
            def _():
                around(k, False).start()

            @pl.when(place == line - 2)
            def _():
                around(k, True).start()

        def pump(k, step):
            for right in (True, False):
                z = place - step if right else place + step

                @pl.when((z >= 0) & (z < line))
                def _():
                    chain_in(k, step, right).wait_recv()

                    if k in AROUND:

                        @pl.when(jnp.logical_not(round_about(k, z)))
                        def _():
                            across(k, z).start()

                    else:
                        across(k, z).start()

                if step + 1 < line:

                    @pl.when(can_send(step + 1, right))
                    def _():
                        chain(k, step + 1, right).start()

        def arrive(k):
            for z in range(line):
                if k in AROUND:

                    @pl.when(jnp.logical_not(round_about(k, z)) & (place != z))
                    def _():
                        across_in(k, z).wait_recv()

                else:
                    across_in(k, z).wait_recv()
            if k in AROUND:

                @pl.when(place == 0)
                def _():
                    around_in(k, False).wait_recv()

                @pl.when(place == line - 1)
                def _():
                    around_in(k, True).wait_recv()

        def drain_weights(k):
            for right in (True, False):
                for step in range(1, line):

                    @pl.when(can_send(step, right))
                    def _():
                        chain(k, step, right).wait_send()

            for z in range(line):
                if k in AROUND:

                    @pl.when(jnp.logical_not(round_about(k, z)))
                    def _():
                        across(k, z).wait_send()

                else:
                    across(k, z).wait_send()
            if k in AROUND:

                @pl.when(place == 1)
                def _():
                    around(k, False).wait_send()

                @pl.when(place == line - 2)
                def _():
                    around(k, True).wait_send()

        def plane(j):
            return lax.rem(place + j, line)

        def to_pair(k, j):
            spot = plane(j) * 2 + 1 - side
            return remote(
                grads.at[k, spot], ry.at[k, j - 1], send_y.at[k, j - 1], recv_y.at[k, j - 1], other
            )

        def to_line(k, j):
            return remote(
                pairs.at[k, j - 1],
                rz.at[k, j - 1],
                send_z.at[k, j - 1],
                recv_z.at[k, j - 1],
                (plane(j) * 2 + side, part),
            )

        def keep(k, value):
            grads[k] = value.astype(LOW).reshape(groups, width // groups, width)

        def give(k):
            for j in range(1, line + 1):
                to_pair(k, j).start()

        def relay(k, *which):
            for j in which:
                to_pair(k, j).wait_recv()
                own = grads[k, plane(j) * 2 + side].astype(FULL)
                pairs[k, j - 1] = (own + ry[k, j - 1].astype(FULL)).astype(LOW)
                if j < line:
                    to_line(k, j).start()

        def collect(k):
            total = pairs[k, line - 1].astype(FULL)
            for j in range(1, line):
                to_line(k, j).wait_recv()
                total = total + rz[k, j - 1].astype(FULL)
            gsum_ref[k] = total

        def to_all(j):
            target = lax.rem(me + j, groups)
            return remote(
                vpad.at[target], vr.at[j - 1], send_v.at[j - 1], recv_v.at[j - 1], (target, part)
            )

        greet(partners + everyone)
        qkv_m, out_m, up_m, down_m, vec_m = masters
        share = width // groups
        vg[me] = jnp.zeros((8, 128), FULL)
        vg[me, 0:3, :share] = vec_m[...].astype(LOW).astype(FULL)
        columns = [qkv_m[t] for t in range(3)] + [out_m[...].T]
        wg[0, me] = jnp.concatenate(columns, axis=1).astype(LOW)
        met(partners + everyone)
        for k in (0, 4, 1):
            begin_line(k)
            begin_across(k)
        wg[1, me] = up_m[...].astype(LOW)
        wg[2, me] = down_m[...].astype(LOW)
    else:
        greet(partners)
        met(partners)

        def keep(k, value):
            gsum_ref[k] = value

        def give(k):
            pass

        def relay(k, *which):
            pass

    def advance(*steps):
        if not joined:
            return
        for k, number in steps:
            last = line - 1
            for step in range(number, last + 1 if number == 3 else number + 1):
                pump(k, step)
                if k == 0:
                    pump(4, step)
                if k == 0 and step == 2:
                    begin_line(2)
                if k == 0 and step == last:
                    begin_across(2)
                if k == 1 and step == last:
                    begin_across(3)
                if k == 2 and step == 1:
                    begin_line(3)
                if step == 1 and k in AROUND:
                    turn(k)

    sel_column = jnp.broadcast_to(sel_ref[...].astype(FULL), (8, slots)).T[:, 0:1].astype(jnp.int32)
    spot_ref[...] = sel_column

    def pick(number, which, dead_zero, out_ref):
        block = 2 * size
        rows = pl.ds(pl.multiple_of(number * block, block), block)
        spots = lax.broadcasted_iota(jnp.int32, (block, seq_len), 1)
        hot = (spots == spot_ref[rows, :]).astype(FULL).astype(LOW)
        got = nn(hot, table[which])
        if dead_zero:
            ids = number * block + lax.broadcasted_iota(jnp.int32, (block, 1), 0)
            got = jnp.where(ids < count, got, 0.0)
        out_ref[rows, :] = got.astype(LOW)

    table_copy(0, tok_any).wait()

    @pl.loop(0, 2)
    def _(number):
        pick(number, 0, False, x_ref)

    advance((0, 1))
    table_copy(1, cot_any).wait()

    @pl.loop(0, 2)
    def _(number):
        pick(number, 1, True, dy_ref)

        @pl.when(number == 0)
        def _():
            advance((1, 1))

    advance((0, 2), (1, 2), (0, 3), (1, 3), (2, 1))

    if joined:
        arrive(4)
        arrive(0)
        arrive(1)
        gains[...] = jnp.concatenate([vg[d][:, :share] for d in range(groups)], axis=1)

    first_gain, gain_row, router_row = gains[0:1, :], gains[1:2, :], gains[2:3, :]

    def weight(k):
        return wg[k].reshape(width, wg.shape[-1])

    w_first = weight(0)
    for t in range(4):
        w4[t] = w_first[:, t * local_width : (t + 1) * local_width]
    def first_norm(number):
        x_rows = x_ref[rows_at(number), :].astype(FULL)
        inverse = mean_square_inverse(x_rows)
        return x_rows, x_rows * inverse, inverse

    for number in range(BLOCKS):
        table[0, number * size : (number + 1) * size, :] = (
            first_norm(number)[1] * first_gain
        ).astype(LOW)
    for t in range(3):
        qkv_ref[t] = nn(table[0, :slots, :], w4[t]).astype(LOW)

    def forward_rows(block):
        start, stop = block * size, (block + 1) * size
        own = start + lax.broadcasted_iota(jnp.int32, (size, 1), 0)
        keys = lax.broadcasted_iota(jnp.int32, (size, stop), 1)
        allowed = keys <= jnp.minimum(own, count - 1)

        def forward_head(head, mixed):
            lanes = head_lanes(local_width, head)
            query = qkv_ref[0, start:stop, :] * (lanes * HEAD_DIM ** (-0.5))
            scores = nt(query, qkv_ref[1, :stop, :])
            scores = jnp.where(allowed, scores, MASKED_SCORE)
            terms = jnp.exp(scores - jnp.max(scores, axis=-1, keepdims=True))
            inverse = 1.0 / jnp.sum(terms, axis=-1, keepdims=True)
            probs = (terms * inverse).astype(LOW)
            return mixed + nn(probs, qkv_ref[2, :stop, :] * lanes)

        mixed = jnp.zeros((size, local_width), FULL)
        for head in range(heads):
            mixed = forward_head(head, mixed)
        o_ref[start:stop, :] = mixed.astype(LOW)

    @pl.loop(0, BLOCKS)
    def _(turn_number):
        number = top - turn_number

        @pl.when(turn_number > 0)
        def _():
            heads_sum.cross(number + 1)

        for block in range(BLOCKS):

            @pl.when(number == block)
            def _():
                forward_rows(block)

        heads_sum.put(number, nt(o_ref[rows_at(number), :], w4[3]))

        @pl.when(turn_number == 0)
        def _():
            advance((2, 2), (3, 1))

    heads_sum.cross(0)
    advance((2, 3), (3, 2), (3, 3))

    def summed(number):
        attended = a_total[number].reshape(size, width).astype(FULL)
        x_rows = x_ref[rows_at(number), :].astype(FULL)
        summed_rows = (x_rows + attended).astype(LOW).astype(FULL)
        inverse = mean_square_inverse(summed_rows)
        return summed_rows * inverse, inverse

    def kept(which, number):
        return which // 2, span((which % 2) * slots + number * size)

    def kept_all(which):
        return table[which // 2, (which % 2) * slots : (which % 2 + 1) * slots, :]

    def up_phase(number):
        heads_sum.arrived(number)
        inner = (summed(number)[0] * gain_row).astype(LOW)
        up = nn(inner, weight(1))
        square = up * up
        bent = jnp.tanh(0.7978845608028654 * (up + 0.044715 * square * up))
        half = 0.5 * (1.0 + bent)
        which, spot = kept(0, number)
        table[which, spot, :] = (up * half).astype(LOW)
        which, spot = kept(1, number)
        table[which, spot, :] = inner
        slope = half + 0.5 * up * (1.0 - bent * bent) * (
            0.7978845608028654 * (1.0 + 3.0 * 0.044715 * square)
        )
        slope_ref[rows_at(number), :] = slope.astype(LOW)
        rows = rows_at(number)
        gate = gate_of(x_ref[rows, :].astype(FULL), router_row)
        which, spot = kept(2, number)
        table[which, spot, :] = (gate * dy_ref[rows, :].astype(FULL)).astype(LOW)

    def back_phase(number):
        rows = rows_at(number)
        which, spot = kept(2, number)
        up_low = (nn(table[which, spot, :], weight(2)) * slope_ref[rows, :].astype(FULL)).astype(LOW)
        which, spot = kept(3, number)
        table[which, spot, :] = up_low
        hidden_sum.put(number, nt(table[which, spot, :], weight(1)))

    heads_sum.finish(top)
    if joined:
        arrive(2)

    @pl.loop(0, BLOCKS + 1)
    def _(turn_number):
        number = top - turn_number

        @pl.when(turn_number > 1)
        def _():
            hidden_sum.cross(number + 2)
            branch_sum.cross(number + 2)

        @pl.when(turn_number < BLOCKS)
        def _():
            up_phase(number)

            @pl.when(number > 0)
            def _():
                heads_sum.finish(number - 1)

        if joined:

            @pl.when(turn_number == 1)
            def _():
                arrive(3)

        @pl.when(turn_number == BLOCKS)
        def _():
            keep(2, tn(kept_all(2), kept_all(0)))
            give(2)

        @pl.when(turn_number > 0)
        def _():
            back_phase(number + 1)
            which, spot = kept(0, number + 1)
            branch_sum.put(number + 1, nt(table[which, spot, :], weight(2)))

    hidden_sum.cross(0)
    branch_sum.cross(0)
    keep(1, tn(kept_all(1), kept_all(3)))
    give(1)

    out_acc[...] = jnp.zeros_like(out_acc)
    dkv[...] = jnp.zeros_like(dkv)
    vacc[...] = jnp.zeros_like(vacc)
    hidden_sum.finish(top)

    def backward_rows(block):
        start, stop = block * size, (block + 1) * size
        own = start + lax.broadcasted_iota(jnp.int32, (1, size), 1)
        keys = lax.broadcasted_iota(jnp.int32, (stop, size), 0)
        allowed = keys <= jnp.minimum(own, count - 1)

        def backward_head(head, dq):
            lanes = head_lanes(local_width, head)
            query = qkv_ref[0, start:stop, :] * (lanes * HEAD_DIM ** (-0.5))
            mixed_grad = do_ref[...] * lanes
            scores = nt(qkv_ref[1, :stop, :], query)
            scores = jnp.where(allowed, scores, MASKED_SCORE)
            terms = jnp.exp(scores - jnp.max(scores, axis=0, keepdims=True))
            total = 1.0 / jnp.sum(terms, axis=0, keepdims=True)
            probs = terms * total
            prob_grad = nt(qkv_ref[2, :stop, :], mixed_grad)
            dots = jnp.sum(prob_grad * probs, axis=0, keepdims=True)
            score_grad = (probs * (prob_grad - dots)).astype(LOW)
            dkv[1, :stop, :] += nn(probs.astype(LOW), mixed_grad)
            dkv[0, :stop, :] += nn(score_grad, query)
            return dq + tn(score_grad, qkv_ref[1, :stop, :] * lanes)

        dq = jnp.zeros((size, local_width), FULL)
        dq = lax.fori_loop(0, heads, backward_head, dq)
        dlow[0, start:stop, :] = (dq * HEAD_DIM ** (-0.5)).astype(LOW)

    @pl.loop(0, BLOCKS)
    def _(turn_number):
        number = top - turn_number
        rows = rows_at(number)

        @pl.when(number > 0)
        def _():
            hidden_sum.finish(number - 1)

        hidden_sum.arrived(number)
        normed, inverse = summed(number)
        grad = h_total[number].reshape(size, width).astype(FULL)
        vacc[1:2, :] += jnp.sum(grad * normed, axis=0, keepdims=True)
        scaled = grad * gain_row
        back = inverse * (scaled - normed * jnp.mean(scaled * normed, axis=-1, keepdims=True))
        back_low = back.astype(LOW)
        dz_ref[rows, :] = back_low
        gate = gate_of(x_ref[rows, :].astype(FULL), router_row)
        attn = (gate * dy_ref[rows, :].astype(FULL) + back_low.astype(FULL)).astype(LOW)
        do_ref[...] = nn(attn, w4[3]).astype(LOW)
        out_acc[...] += tn(attn, o_ref[rows, :])

        @pl.when(turn_number > 0)
        def _():
            input_sum.cross(number + 1)

        for block in range(BLOCKS):

            @pl.when(number == block)
            def _():
                backward_rows(block)

        dlow[1, rows, :] = dkv[0, rows, :].astype(LOW)
        dlow[2, rows, :] = dkv[1, rows, :].astype(LOW)
        part_sum = nt(dlow[0, rows, :], w4[0])
        part_sum += nt(dlow[1, rows, :], w4[1])
        part_sum += nt(dlow[2, rows, :], w4[2])
        heads_sum.drain(number)
        input_sum.put(number, part_sum)
        if joined:
            for when, k, which in ((0, 2, (1, 2)), (1, 2, range(3, line + 1)), (2, 1, (1, 2)), (3, 1, (3,))):

                @pl.when(turn_number == when)
                def _():
                    relay(k, *which)

    input_sum.cross(0)

    @pl.loop(0, BLOCKS)
    def _(number):
        which, spot = kept(0, number)
        table[which, spot, :] = (first_norm(number)[1] * first_gain).astype(LOW)

    blocks = [tn(kept_all(0), dlow[t]) for t in range(3)]
    blocks.append(out_acc[...])
    keep(0, jnp.concatenate(blocks, axis=1))
    give(0)

    branch_sum.finish(top)
    input_sum.finish(top)

    @pl.loop(0, BLOCKS)
    def _(turn_number):
        number = top - turn_number
        rows = rows_at(number)

        @pl.when(number > 0)
        def _():
            branch_sum.finish(number - 1)
            input_sum.finish(number - 1)

        if joined:
            for when, k, which in ((1, 1, range(4, line + 1)), (2, 0, (1, 2)), (3, 0, range(3, line + 1))):

                @pl.when(turn_number == when)
                def _():
                    relay(k, *which)

        branch_sum.arrived(number)
        x_rows, normed, inverse = first_norm(number)
        dy_rows = dy_ref[rows, :].astype(FULL)
        added = a_total[number].reshape(size, width).astype(FULL)
        added = added + m_total[number].reshape(size, width).astype(FULL)
        gate = gate_of(x_rows, router_row)
        gate_grad = jnp.sum(dy_rows * added, axis=-1, keepdims=True)
        logit_grad = gate_grad * gate * (1.0 - gate) * width ** (-0.5)
        branch_sum.drain(number)
        m_total[number] = (x_rows + gate * added).astype(LOW).reshape(2, size // 2, width)
        input_sum.arrived(number)
        grad = d_total[number].reshape(size, width).astype(FULL)
        vacc[0:1, :] += jnp.sum(grad * normed, axis=0, keepdims=True)
        vacc[2:3, :] += jnp.sum(logit_grad * x_rows, axis=0, keepdims=True)
        scaled = grad * first_gain
        back = inverse * (scaled - normed * jnp.mean(scaled * normed, axis=-1, keepdims=True))
        dx_rows = dy_rows + dz_ref[rows, :].astype(FULL) + back + logit_grad * router_row
        input_sum.drain(number)
        d_total[number] = dx_rows.astype(LOW).reshape(2, size // 2, width)

    if joined:
        for d in range(groups):
            vpad[d, :, :share] = vacc[:, d * share : (d + 1) * share]
        for j in range(1, groups):
            to_all(j).start()
        for k in (2, 1, 0):
            collect(k)
        total = vpad[me]
        for j in range(1, groups):
            to_all(j).wait_recv()
            total = total + vr[j - 1]
        vsum_ref[...] = total
        for k in range(5):
            drain_weights(k)
        for k in range(3):
            for j in range(1, line + 1):
                to_pair(k, j).wait_send()
            for j in range(1, line):
                to_line(k, j).wait_send()
        for j in range(1, groups):
            to_all(j).wait_send()
    else:
        vsum_ref[...] = vacc[...]

    @pl.loop(0, BLOCKS)
    def _(number):
        hidden_sum.drain(number)


def adam_update(master, first_moment, second_moment, gradient, step_rate, decay_rate):
    first_new = MOMENT_DECAY * first_moment + (1.0 - MOMENT_DECAY) * gradient
    second_new = SQUARE_DECAY * second_moment + (1.0 - SQUARE_DECAY) * gradient * gradient
    first_hat = first_new / (1.0 - MOMENT_DECAY**STEP)
    second_hat = second_new / (1.0 - SQUARE_DECAY**STEP)
    master_new = master - step_rate * (
        first_hat / (jnp.sqrt(second_hat) + ADAM_EPS) + decay_rate * master
    )
    return (master_new, first_new, second_new)


def last_kernel(cap_ref, sel_ref, vsum_ref, *refs):
    vec_old, (tok, cot, y, dx, gsum), olds, refs = refs[:3], refs[3:8], refs[8:20], refs[20:]
    vec_new, (out, grad), news, refs = refs[:3], refs[3:5], refs[5:17], refs[17:]
    (tok_b, cot_b, y_b, dx_b, gsum_b), olds_b, (out_b, grad_b), news_b = (
        refs[:5],
        refs[5:17],
        refs[17:19],
        refs[19:31],
    )
    row_sems, in_sems, out_sems, done_sems = refs[31:]
    slots, width = y_b.shape
    seq_len = tok_b.shape[0]
    rows = min(SPOT_ROWS, seq_len)
    chunks = seq_len // rows

    small = [pltpu.make_async_copy(gsum, gsum_b, in_sems.at[0])]
    small += [
        pltpu.make_async_copy(old, old_b, in_sems.at[3 + i])
        for i, (old, old_b) in enumerate(zip(olds, olds_b))
    ]
    placed = [
        pltpu.make_async_copy(y, y_b, in_sems.at[1]),
        pltpu.make_async_copy(dx, dx_b, in_sems.at[2]),
    ]
    finished = [
        pltpu.make_async_copy(new_b, new, done_sems.at[i])
        for i, (new, new_b) in enumerate(zip(news, news_b))
    ]

    def part(number):
        return pl.ds(pl.multiple_of(number * rows, rows), rows)

    def load(which, number):
        source, target = ((tok, tok_b), (cot, cot_b))[which]
        return pltpu.make_async_copy(
            source.at[part(number)], target.at[part(number)], row_sems.at[which, number]
        )

    def store(which, number):
        source, target = ((out_b, out), (grad_b, grad))[which]
        return pltpu.make_async_copy(
            source.at[part(number)], target.at[part(number)], out_sems.at[which, number]
        )

    for copy in small[:1] + small[1:] + placed:
        copy.start()

    @pl.loop(0, chunks)
    def _(number):
        load(0, number).start()
        load(1, number).start()

    for copy in small:
        copy.wait()
    local_width = olds_b[0].shape[-1]
    share = vec_old[0].shape[1]
    first = gsum_b[0]
    parts = [first[:, t * local_width : (t + 1) * local_width] for t in range(4)]
    for t in range(3):
        old = [olds_b[4 * i][t] for i in range(3)]
        for i, value in enumerate(adam_update(*old, parts[t], RATE_MATRIX, WEIGHT_DECAY)):
            news_b[4 * i][t] = value
    for number, gradient in ((1, parts[3].T), (2, gsum_b[1]), (3, gsum_b[2])):
        old = [olds_b[number + 4 * i][...] for i in range(3)]
        for i, value in enumerate(adam_update(*old, gradient, RATE_MATRIX, WEIGHT_DECAY)):
            news_b[number + 4 * i][...] = value
    for copy in finished:
        copy.start()
    values = adam_update(*[ref[...] for ref in vec_old], vsum_ref[0:3, :share], RATE_VECTOR, 0.0)
    for ref, value in zip(vec_new, values):
        ref[...] = value

    for copy in placed:
        copy.wait()
    ids = lax.broadcasted_iota(jnp.int32, (1, slots), 1)
    chosen = jnp.where(ids < cap_ref[lax.axis_index("dp")], sel_ref[...], -1)

    @pl.loop(0, chunks)
    def _(number):
        load(0, number).wait()
        load(1, number).wait()
        spots = number * rows + lax.broadcasted_iota(jnp.int32, (rows, slots), 0)
        hot = (spots == chosen).astype(FULL)
        hit = jnp.max(hot, axis=-1, keepdims=True) > 0.5
        hot = hot.astype(LOW)
        kept_rows = tok_b[part(number), :].astype(FULL)
        out_b[part(number), :] = jnp.where(hit, nn(hot, y_b[...]), kept_rows).astype(LOW)
        store(0, number).start()
        kept_rows = cot_b[part(number), :].astype(FULL)
        grad_b[part(number), :] = jnp.where(hit, nn(hot, dx_b[...]), kept_rows)
        store(1, number).start()

    for copy in finished:
        copy.wait()

    @pl.loop(0, chunks)
    def _(number):
        store(0, number).wait()
        store(1, number).wait()


def shape(dims, kind):
    return jax.ShapeDtypeStruct(dims, kind)


IN_VMEM = pl.BlockSpec(memory_space=pltpu.VMEM)
IN_SMEM = pl.BlockSpec(memory_space=pltpu.SMEM)
IN_ANY = pl.BlockSpec(memory_space=pl.ANY)
DMA = pltpu.SemaphoreType.DMA


def params(number=None):
    if number is None:
        return pltpu.CompilerParams(vmem_limit_bytes=VMEM_BYTES)
    return pltpu.CompilerParams(
        vmem_limit_bytes=VMEM_BYTES, collective_id=number, has_side_effects=True
    )


def local(
    tokens,
    cotangent,
    capacity,
    selected,
    qkv_master,
    out_master,
    up_master,
    down_master,
    vec_master,
    qkv_first,
    out_first,
    up_first,
    down_first,
    vec_first,
    qkv_second,
    out_second,
    up_second,
    down_second,
    vec_second,
):
    groups = lax.axis_size("dp")
    me = lax.axis_index("dp")
    share, local_width = qkv_master.shape[1:]
    hidden = up_master.shape[1]
    width = tokens.shape[2]
    seq_len = tokens.shape[1]
    slots = selected.shape[1]
    joined = share % 32 == 0 and groups % 2 == 0 and groups >= 8
    token_rows, cot_rows = tokens[0], cotangent[0]
    line = groups // 2

    quarter = slots // BLOCKS
    half_block = pltpu.VMEM((BLOCKS, quarter // 2, width), LOW)
    both_halves = pltpu.VMEM((BLOCKS, 2, quarter // 2, width), LOW)
    hops = DMA((2, 3, BLOCKS))
    exchange = [both_halves, half_block, half_block, half_block]
    scratch = [
        pltpu.VMEM((2, seq_len, width), LOW),
        DMA((2,)),
        pltpu.VMEM((slots, width), LOW),
        pltpu.VMEM((slots, width), LOW),
        pltpu.VMEM((3, slots, local_width), LOW),
        pltpu.VMEM((slots, local_width), LOW),
        pltpu.VMEM((4, width, local_width), LOW),
        *exchange,
        both_halves,
        hops,
        hops,
        *exchange,
        both_halves,
        hops,
        *exchange,
        hops,
        pltpu.VMEM((slots, hidden), LOW),
        pltpu.VMEM((slots, width), LOW),
        pltpu.VMEM((width, local_width), FULL),
        pltpu.VMEM((2, slots, local_width), FULL),
        pltpu.VMEM((3, slots, local_width), LOW),
        pltpu.VMEM((8, width), FULL),
        pltpu.VMEM((slots, 1), jnp.int32),
        pltpu.VMEM((quarter, local_width), LOW),
    ]
    if joined:
        weights = (qkv_master, out_master, up_master, down_master.T, vec_master)
        scratch += [
            pltpu.VMEM((3, groups, share, width), LOW),
            pltpu.VMEM((8, width), FULL),
            pltpu.VMEM((groups, 8, 128), FULL),
            DMA((5, line - 1)),
            DMA((5, line - 1)),
            DMA((5, line - 1)),
            DMA((5, line - 1)),
            DMA((5, line)),
            DMA((5, line)),
            DMA((5,)),
            DMA((5,)),
            pltpu.VMEM((3, groups, share, width), LOW),
            pltpu.VMEM((3, line, share, width), LOW),
            pltpu.VMEM((3, line, share, width), LOW),
            pltpu.VMEM((3, line - 1, share, width), LOW),
            pltpu.VMEM((groups, 8, 128), FULL),
            pltpu.VMEM((groups - 1, 8, 128), FULL),
            DMA((3, line)),
            DMA((3, line)),
            DMA((3, line - 1)),
            DMA((3, line - 1)),
            DMA((groups - 1,)),
            DMA((groups - 1,)),
        ]
    else:
        first_shard = jnp.concatenate(
            [qkv_master[0], qkv_master[1], qkv_master[2], out_master.T], axis=1
        )
        shard = jnp.stack([first_shard, up_master, down_master.T]).astype(LOW)
        vectors = lax.all_gather(vec_master.astype(LOW), "dp", axis=1, tiled=True)
        weights = (
            lax.all_gather(shard, "dp", axis=1, tiled=True),
            jnp.pad(vectors.astype(FULL), ((0, 5), (0, 0))),
        )
    y_rows, dx_rows, grad_sum, vec_sum = pl.pallas_call(
        functools.partial(main_kernel, groups, joined),
        out_shape=[
            shape((BLOCKS, 2, quarter // 2, width), LOW),
            shape((BLOCKS, 2, quarter // 2, width), LOW),
            shape((3, share if joined else width, width), FULL),
            shape((8, 128 if joined else width), FULL),
        ],
        in_specs=[IN_SMEM, IN_VMEM, IN_ANY, IN_ANY] + [IN_VMEM] * len(weights),
        out_specs=[IN_VMEM] * 4,
        scratch_shapes=scratch,
        compiler_params=params(0),
        name="main",
    )(capacity, selected, token_rows, cot_rows, *weights)
    y_rows, dx_rows = (rows.reshape(slots, width) for rows in (y_rows, dx_rows))

    if not joined:
        grad_sum = lax.psum_scatter(grad_sum, "dp", scatter_dimension=1, tiled=True)
        vec_sum = lax.psum_scatter(vec_sum, "dp", scatter_dimension=1, tiled=True)
    olds = (
        qkv_master, out_master, up_master, down_master.T,
        qkv_first, out_first, up_first, down_first.T,
        qkv_second, out_second, up_second, down_second.T,
    )
    vec_olds = (vec_master, vec_first, vec_second)
    ones = (token_rows, cot_rows, y_rows, dx_rows, grad_sum)
    made = [shape((seq_len, width), LOW), shape((seq_len, width), FULL)]
    made += [shape(old.shape, FULL) for old in olds]
    chunks = seq_len // min(SPOT_ROWS, seq_len)
    *vec_news, block_out, input_grad, q0, o0, u0, d0, q1, o1, u1, d1, q2, o2, u2, d2 = pl.pallas_call(
        last_kernel,
        out_shape=[shape(old.shape, FULL) for old in vec_olds] + made,
        in_specs=[IN_SMEM] + [IN_VMEM] * 5 + [IN_ANY] * 17,
        out_specs=[IN_VMEM] * 3 + [IN_ANY] * 14,
        scratch_shapes=[pltpu.VMEM(array.shape, array.dtype) for array in (*ones, *olds, *made)]
        + [DMA((2, chunks)), DMA((15,)), DMA((2, chunks)), DMA((12,))],
        compiler_params=params(),
        name="last",
    )(capacity, selected, vec_sum, *vec_olds, *ones, *olds)
    v0, v1, v2 = vec_news
    return (
        block_out[None], input_grad[None],
        q0, o0, u0, d0.T, v0, q1, o1, u1, d1.T, v1, q2, o2, u2, d2.T, v2,
    )


def solution(mesh):
    weights = (
        P(None, "dp", "mp"),
        P("mp", "dp"),
        P("dp", "mp"),
        P("mp", "dp"),
        P(None, "dp"),
    )
    rows = (P("dp", None, None), P("dp", None, None))
    return jax.shard_map(
        local,
        mesh=mesh,
        in_specs=(*rows, P(), P("dp", None), *weights * 3),
        out_specs=(*rows, *weights * 3),
        check_vma=False,
    )
```

```python
import functools

import jax
import jax.numpy as jnp
from jax import lax
from jax.experimental import pallas as pl
from jax.experimental.pallas import tpu as pltpu
from jax.sharding import PartitionSpec as P

HEAD_DIM = 64
STEP = 10
NORM_EPS = 1e-05
MASKED_SCORE = -1000000000.0
MOMENT_DECAY = 0.9
SQUARE_DECAY = 0.95
ADAM_EPS = 1e-08
WEIGHT_DECAY = 0.1
RATE_MATRIX = 0.06
RATE_VECTOR = 0.2

LOW = jnp.bfloat16
FULL = jnp.float32
MESH = pl.DeviceIdType.MESH
BLOCKS = 4
AROUND = (3,)
SPOT_ROWS = 512
VMEM_BYTES = 60 * 2**20


def nn(a, b):
    return lax.dot_general(a, b, (((1,), (0,)), ((), ())), preferred_element_type=FULL)


def nt(a, b):
    return lax.dot_general(a, b, (((1,), (1,)), ((), ())), preferred_element_type=FULL)


def tn(a, b):
    return lax.dot_general(a, b, (((0,), (0,)), ((), ())), preferred_element_type=FULL)


def mean_square_inverse(values):
    return lax.rsqrt(jnp.mean(values * values, axis=-1, keepdims=True) + NORM_EPS)


def gate_of(rows, router_row):
    width = rows.shape[-1]
    logit = jnp.sum(rows * router_row, axis=-1, keepdims=True) * width ** (-0.5)
    return jax.nn.sigmoid(logit)


def greet(partners):
    barrier = pltpu.get_barrier_semaphore()
    for partner in partners:
        pl.semaphore_signal(barrier, inc=1, device_id=partner, device_id_type=MESH)


def met(partners):
    pl.semaphore_wait(pltpu.get_barrier_semaphore(), len(partners))


def remote(src, dst, send_sem, recv_sem, device):
    return pltpu.make_async_remote_copy(
        src_ref=src,
        dst_ref=dst,
        send_sem=send_sem,
        recv_sem=recv_sem,
        device_id=device,
        device_id_type=MESH,
    )


class Exchange:
    def __init__(self, parts, near, pair, far, total, sems):
        self.parts, self.near, self.pair, self.far, self.total = parts, near, pair, far, total
        self.sems = sems
        self.me, self.part = lax.axis_index("dp"), lax.axis_index("mp")
        self.half = self.part % 2
        self.near_device = (self.me, self.part + 1 - 2 * self.half)
        self.far_device = (self.me, (self.part + 2) % 4)

    def copy(self, which, block, src, dst):
        device = self.far_device if which == 1 else self.near_device
        return remote(src, dst, self.sems.at[0, which, block], self.sems.at[1, which, block], device)

    def out(self, which, block):
        if which == 0:
            return self.copy(0, block, self.parts.at[block, 1 - self.half], self.near.at[block])
        if which == 1:
            return self.copy(1, block, self.pair.at[block], self.far.at[block])
        spot = self.total.at[block, self.half]
        return self.copy(2, block, spot, spot)

    def into(self, which, block):
        spot = (self.near.at[block], self.far.at[block], self.total.at[block, 1 - self.half])[which]
        return self.copy(which, block, spot, spot)

    def put(self, block, value):
        rows, width = value.shape
        self.parts[block] = value.astype(LOW).reshape(2, rows // 2, width)
        self.send(block)

    def send(self, block):
        self.out(0, block).start()

    def cross(self, block):
        self.into(0, block).wait_recv()
        self.pair[block] = (
            self.parts[block, self.half].astype(FULL) + self.near[block].astype(FULL)
        ).astype(LOW)
        self.out(1, block).start()

    def finish(self, block):
        self.into(1, block).wait_recv()
        self.total[block, self.half] = (
            self.pair[block].astype(FULL) + self.far[block].astype(FULL)
        ).astype(LOW)
        self.out(2, block).start()

    def arrived(self, block):
        self.into(2, block).wait_recv()

    def drain(self, block):
        for which in range(3):
            self.out(which, block).wait_send()


def head_lanes(width, head):
    lanes = lax.broadcasted_iota(jnp.int32, (1, width), 1)
    return (lanes // HEAD_DIM == head).astype(FULL).astype(LOW)


def main_kernel(groups, joined, *refs):
    (cap_ref, sel_ref, tok_any, cot_any), refs = refs[:4], refs[4:]
    if joined:
        masters, refs = refs[:5], refs[5:]
    else:
        (wg, gains), refs = refs[:2], refs[2:]
    (y_any, dx_any, gsum_ref, vsum_ref), refs = refs[:4], refs[4:]
    (m_total, d_total, row_sems), refs = refs[:3], refs[3:]
    (table, table_sems, x_ref, dy_ref, qkv_ref, o_ref, w4), refs = refs[:7], refs[7:]
    (parts, near, pair, far, a_total, a_sems, d_sems), refs = refs[:7], refs[7:]
    (h_parts, h_near, h_pair, h_far, h_total, h_sems), refs = refs[:6], refs[6:]
    (m_parts, m_near, m_pair, m_far, m_sems), refs = refs[:5], refs[5:]
    (slope_ref, dz_ref, out_acc, dkv, dlow, vacc, spot_ref, do_ref), refs = refs[:8], refs[8:]

    slots, width = x_ref.shape
    seq_len = tok_any.shape[0]
    local_width = o_ref.shape[1]
    heads = local_width // HEAD_DIM
    size = slots // BLOCKS
    me, part = lax.axis_index("dp"), lax.axis_index("mp")
    count = cap_ref[me]
    top = BLOCKS - 1

    def span(start):
        return pl.ds(pl.multiple_of(start, size), size)

    def rows_at(number):
        return span(number * size)

    def table_copy(which, source):
        return pltpu.make_async_copy(source, table.at[which], table_sems.at[which])

    table_copy(0, tok_any).start()
    table_copy(1, cot_any).start()

    heads_sum = Exchange(parts, near, pair, far, a_total, a_sems)
    hidden_sum = Exchange(h_parts, h_near, h_pair, h_far, h_total, h_sems)
    branch_sum = Exchange(m_parts, m_near, m_pair, m_far, m_total, m_sems)
    input_sum = Exchange(parts, near, pair, far, d_total, d_sems)
    partners = [heads_sum.near_device, heads_sum.far_device]

    if joined:
        (wg, gains, vg, send_r, recv_r, send_l, recv_l, send_f, recv_f), refs = refs[:9], refs[9:]
        (send_e, recv_e), refs = refs[:2], refs[2:]
        (grads, ry, pairs, rz, vpad, vr), refs = refs[:6], refs[6:]
        send_y, recv_y, send_z, recv_z, send_v, recv_v = refs
        line, place, side = groups // 2, me // 2, me % 2
        other = (me + 1 - 2 * side, part)
        everyone = [(lax.rem(me + j, groups), part) for j in range(1, groups)]

        half_share = width // groups // 2

        def slot(k, d):
            if k < 2:
                return wg.at[0, d, pl.ds(k * half_share, half_share)]
            return vg.at[d] if k == 4 else wg.at[k - 1, d]

        def chain(k, step, right):
            z = place - step + 1 if right else place + step - 1
            sems = (send_r, recv_r) if right else (send_l, recv_l)
            target = (me + 2 if right else me - 2, part)
            return remote(
                slot(k, z * 2 + side),
                slot(k, z * 2 + side),
                sems[0].at[k, step - 1],
                sems[1].at[k, step - 1],
                target,
            )

        def chain_in(k, step, right):
            z = place - step if right else place + step
            sems = (send_r, recv_r) if right else (send_l, recv_l)
            spot = slot(k, z * 2 + side)
            return remote(spot, spot, sems[0].at[k, step - 1], sems[1].at[k, step - 1], other)

        def can_send(step, right):
            if right:
                return (place + 1 < line) & (place - step + 1 >= 0)
            return (place >= 1) & (place + step - 1 < line)

        def across(k, z):
            spot = slot(k, z * 2 + side)
            return remote(spot, spot, send_f.at[k, z], recv_f.at[k, z], other)

        def across_in(k, z):
            spot = slot(k, z * 2 + 1 - side)
            return remote(spot, spot, send_f.at[k, z], recv_f.at[k, z], other)

        def begin_line(k):
            for right in (True, False):

                @pl.when(can_send(1, right))
                def _():
                    chain(k, 1, right).start()

        def begin_across(k):
            across(k, place).start()

        def round_about(k, z):
            if k not in AROUND:
                return False
            return ((place == 0) & (z == 1)) | ((place == line - 1) & (z == line - 2))

        def around(k, right):
            spot = slot(k, me + 1 - 2 * side)
            target = (me + 2 if right else me - 2, part)
            return remote(spot, spot, send_e.at[k], recv_e.at[k], target)

        def around_in(k, right):
            spot = slot(k, (me - 2 if right else me + 2) + 1 - 2 * side)
            return remote(spot, spot, send_e.at[k], recv_e.at[k], other)

        def turn(k):
            across_in(k, place).wait_recv()

            @pl.when(place == 1)
            def _():
                around(k, False).start()

            @pl.when(place == line - 2)
            def _():
                around(k, True).start()

        def pump(k, step):
            for right in (True, False):
                z = place - step if right else place + step

                @pl.when((z >= 0) & (z < line))
                def _():
                    chain_in(k, step, right).wait_recv()

                    if k in AROUND:

                        @pl.when(jnp.logical_not(round_about(k, z)))
                        def _():
                            across(k, z).start()

                    else:
                        across(k, z).start()

                if step + 1 < line:

                    @pl.when(can_send(step + 1, right))
                    def _():
                        chain(k, step + 1, right).start()

        def arrive(k):
            for z in range(line):
                if k in AROUND:

                    @pl.when(jnp.logical_not(round_about(k, z)) & (place != z))
                    def _():
                        across_in(k, z).wait_recv()

                else:
                    across_in(k, z).wait_recv()
            if k in AROUND:

                @pl.when(place == 0)
                def _():
                    around_in(k, False).wait_recv()

                @pl.when(place == line - 1)
                def _():
                    around_in(k, True).wait_recv()

        def drain_weights(k):
            for right in (True, False):
                for step in range(1, line):

                    @pl.when(can_send(step, right))
                    def _():
                        chain(k, step, right).wait_send()

            for z in range(line):
                if k in AROUND:

                    @pl.when(jnp.logical_not(round_about(k, z)))
                    def _():
                        across(k, z).wait_send()

                else:
                    across(k, z).wait_send()
            if k in AROUND:

                @pl.when(place == 1)
                def _():
                    around(k, False).wait_send()

                @pl.when(place == line - 2)
                def _():
                    around(k, True).wait_send()

        def plane(j):
            return lax.rem(place + j, line)

        def to_pair(k, j):
            spot = plane(j) * 2 + 1 - side
            return remote(
                grads.at[k, spot], ry.at[k, j - 1], send_y.at[k, j - 1], recv_y.at[k, j - 1], other
            )

        def to_line(k, j):
            return remote(
                pairs.at[k, j - 1],
                rz.at[k, j - 1],
                send_z.at[k, j - 1],
                recv_z.at[k, j - 1],
                (plane(j) * 2 + side, part),
            )

        def keep(k, value):
            grads[k] = value.astype(LOW).reshape(groups, width // groups, width)

        def give(k):
            for j in range(1, line + 1):
                to_pair(k, j).start()

        def relay(k, *which):
            for j in which:
                to_pair(k, j).wait_recv()
                own = grads[k, plane(j) * 2 + side].astype(FULL)
                pairs[k, j - 1] = (own + ry[k, j - 1].astype(FULL)).astype(LOW)
                if j < line:
                    to_line(k, j).start()

        def collect(k):
            total = pairs[k, line - 1].astype(FULL)
            for j in range(1, line):
                to_line(k, j).wait_recv()
                total = total + rz[k, j - 1].astype(FULL)
            gsum_ref[k] = total

        def to_all(j):
            target = lax.rem(me + j, groups)
            return remote(
                vpad.at[target], vr.at[j - 1], send_v.at[j - 1], recv_v.at[j - 1], (target, part)
            )

        greet(partners + everyone)
        qkv_m, out_m, up_m, down_m, vec_m = masters
        share = width // groups
        vg[me] = jnp.zeros((8, 128), FULL)
        vg[me, 0:3, :share] = vec_m[...].astype(LOW).astype(FULL)
        columns = [qkv_m[t] for t in range(3)] + [out_m[...].T]
        wg[0, me] = jnp.concatenate(columns, axis=1).astype(LOW)
        met(partners + everyone)
        for k in (0, 4, 1):
            begin_line(k)
            begin_across(k)
        wg[1, me] = up_m[...].astype(LOW)
        wg[2, me] = down_m[...].astype(LOW)
    else:
        greet(partners)
        met(partners)

        def keep(k, value):
            gsum_ref[k] = value

        def give(k):
            pass

        def relay(k, *which):
            pass

    def advance(*steps):
        if not joined:
            return
        for k, number in steps:
            last = line - 1
            for step in range(number, last + 1 if number == 3 else number + 1):
                pump(k, step)
                if k == 0:
                    pump(4, step)
                if k == 0 and step == 2:
                    begin_line(2)
                if k == 0 and step == last:
                    begin_across(2)
                if k == 1 and step == last:
                    begin_across(3)
                if k == 2 and step == 1:
                    begin_line(3)
                if step == 1 and k in AROUND:
                    turn(k)

    sel_column = jnp.broadcast_to(sel_ref[...].astype(FULL), (8, slots)).T[:, 0:1].astype(jnp.int32)
    spot_ref[...] = sel_column

    def pick(number, which, dead_zero, out_ref):
        block = 2 * size
        rows = pl.ds(pl.multiple_of(number * block, block), block)
        spots = lax.broadcasted_iota(jnp.int32, (block, seq_len), 1)
        hot = (spots == spot_ref[rows, :]).astype(FULL).astype(LOW)
        got = nn(hot, table[which])
        if dead_zero:
            ids = number * block + lax.broadcasted_iota(jnp.int32, (block, 1), 0)
            got = jnp.where(ids < count, got, 0.0)
        out_ref[rows, :] = got.astype(LOW)

    table_copy(0, tok_any).wait()

    @pl.loop(0, 2)
    def _(number):
        pick(number, 0, False, x_ref)

    advance((0, 1))
    table_copy(1, cot_any).wait()

    @pl.loop(0, 2)
    def _(number):
        pick(number, 1, True, dy_ref)

        @pl.when(number == 0)
        def _():
            advance((1, 1))

    advance((0, 2), (1, 2), (0, 3), (1, 3), (2, 1))

    if joined:
        arrive(4)
        gains[...] = jnp.concatenate([vg[d][:, :share] for d in range(groups)], axis=1)

    first_gain, gain_row, router_row = gains[0:1, :], gains[1:2, :], gains[2:3, :]

    def weight(k):
        return wg[k].reshape(width, wg.shape[-1])

    def first_norm(number):
        x_rows = x_ref[rows_at(number), :].astype(FULL)
        inverse = mean_square_inverse(x_rows)
        return x_rows, x_rows * inverse, inverse

    for number in range(BLOCKS):
        table[0, number * size : (number + 1) * size, :] = (
            first_norm(number)[1] * first_gain
        ).astype(LOW)
    if joined:
        arrive(0)
        arrive(1)
        advance((2, 2))
    w_first = weight(0)
    for t in range(4):
        w4[t] = w_first[:, t * local_width : (t + 1) * local_width]
    for t in range(3):
        qkv_ref[t] = nn(table[0, :slots, :], w4[t]).astype(LOW)

    def forward_rows(block):
        start, stop = block * size, (block + 1) * size
        own = start + lax.broadcasted_iota(jnp.int32, (size, 1), 0)
        keys = lax.broadcasted_iota(jnp.int32, (size, stop), 1)
        allowed = keys <= jnp.minimum(own, count - 1)

        def forward_head(head, mixed):
            lanes = head_lanes(local_width, head)
            query = qkv_ref[0, start:stop, :] * (lanes * HEAD_DIM ** (-0.5))
            scores = nt(query, qkv_ref[1, :stop, :])
            scores = jnp.where(allowed, scores, MASKED_SCORE)
            terms = jnp.exp(scores - jnp.max(scores, axis=-1, keepdims=True))
            inverse = 1.0 / jnp.sum(terms, axis=-1, keepdims=True)
            probs = (terms * inverse).astype(LOW)
            return mixed + nn(probs, qkv_ref[2, :stop, :] * lanes)

        mixed = jnp.zeros((size, local_width), FULL)
        for head in range(heads):
            mixed = forward_head(head, mixed)
        o_ref[start:stop, :] = mixed.astype(LOW)

    @pl.loop(0, BLOCKS)
    def _(turn_number):
        number = top - turn_number

        @pl.when(turn_number > 0)
        def _():
            heads_sum.cross(number + 1)

        @pl.when(turn_number == 1)
        def _():
            advance((3, 1), (2, 3))

        @pl.when(turn_number == 2)
        def _():
            advance((3, 2))

        for block in range(BLOCKS):

            @pl.when(number == block)
            def _():
                forward_rows(block)

        heads_sum.put(number, nt(o_ref[rows_at(number), :], w4[3]))

    heads_sum.cross(0)
    advance((3, 3))

    def summed(number):
        attended = a_total[number].reshape(size, width).astype(FULL)
        x_rows = x_ref[rows_at(number), :].astype(FULL)
        summed_rows = (x_rows + attended).astype(LOW).astype(FULL)
        inverse = mean_square_inverse(summed_rows)
        return summed_rows * inverse, inverse

    def kept(which, number):
        return which // 2, span((which % 2) * slots + number * size)

    def kept_all(which):
        return table[which // 2, (which % 2) * slots : (which % 2 + 1) * slots, :]

    def up_phase(number):
        heads_sum.arrived(number)
        inner = (summed(number)[0] * gain_row).astype(LOW)
        up = nn(inner, weight(1))
        square = up * up
        bent = jnp.tanh(0.7978845608028654 * (up + 0.044715 * square * up))
        half = 0.5 * (1.0 + bent)
        which, spot = kept(0, number)
        table[which, spot, :] = (up * half).astype(LOW)
        which, spot = kept(1, number)
        table[which, spot, :] = inner
        slope = half + 0.5 * up * (1.0 - bent * bent) * (
            0.7978845608028654 * (1.0 + 3.0 * 0.044715 * square)
        )
        slope_ref[rows_at(number), :] = slope.astype(LOW)
        rows = rows_at(number)
        gate = gate_of(x_ref[rows, :].astype(FULL), router_row)
        which, spot = kept(2, number)
        table[which, spot, :] = (gate * dy_ref[rows, :].astype(FULL)).astype(LOW)

    def back_phase(number):
        rows = rows_at(number)
        which, spot = kept(2, number)
        up_low = (nn(table[which, spot, :], weight(2)) * slope_ref[rows, :].astype(FULL)).astype(LOW)
        which, spot = kept(3, number)
        table[which, spot, :] = up_low
        hidden_sum.put(number, nt(table[which, spot, :], weight(1)))

    def put_branch(number):
        which, spot = kept(0, number)
        branch_sum.put(number, nt(table[which, spot, :], weight(2)))

    heads_sum.finish(top)
    if joined:
        arrive(2)

    @pl.loop(0, BLOCKS + 1)
    def _(turn_number):
        number = top - turn_number

        @pl.when(turn_number > 1)
        def _():
            hidden_sum.cross(number + 2)

        @pl.when(turn_number == 2)
        def _():
            branch_sum.cross(top)

        @pl.when(turn_number < BLOCKS)
        def _():
            up_phase(number)

            @pl.when(number > 0)
            def _():
                heads_sum.finish(number - 1)

        if joined:

            @pl.when(turn_number == 1)
            def _():
                arrive(3)

        @pl.when(turn_number == BLOCKS)
        def _():
            keep(2, tn(kept_all(2), kept_all(0)))
            give(2)

        @pl.when(turn_number > 0)
        def _():
            back_phase(number + 1)

        @pl.when((turn_number > 0) & (turn_number < 3))
        def _():
            put_branch(number + 1)

    hidden_sum.cross(0)
    branch_sum.cross(top - 1)
    keep(1, tn(kept_all(1), kept_all(3)))
    give(1)
    for number in range(top - 1):
        put_branch(top - 2 - number)
    for number in range(top - 1):
        branch_sum.cross(top - 2 - number)

    @pl.loop(0, BLOCKS)
    def _(number):
        which, spot = kept(0, number)
        table[which, spot, :] = (first_norm(number)[1] * first_gain).astype(LOW)

    out_acc[...] = jnp.zeros_like(out_acc)
    dkv[...] = jnp.zeros_like(dkv)
    vacc[...] = jnp.zeros_like(vacc)
    hidden_sum.finish(top)

    def backward_rows(block):
        start, stop = block * size, (block + 1) * size
        own = start + lax.broadcasted_iota(jnp.int32, (1, size), 1)
        keys = lax.broadcasted_iota(jnp.int32, (stop, size), 0)
        allowed = keys <= jnp.minimum(own, count - 1)

        def backward_head(head, dq):
            lanes = head_lanes(local_width, head)
            query = qkv_ref[0, start:stop, :] * (lanes * HEAD_DIM ** (-0.5))
            mixed_grad = do_ref[...] * lanes
            scores = nt(qkv_ref[1, :stop, :], query)
            scores = jnp.where(allowed, scores, MASKED_SCORE)
            terms = jnp.exp(scores - jnp.max(scores, axis=0, keepdims=True))
            total = 1.0 / jnp.sum(terms, axis=0, keepdims=True)
            probs = terms * total
            prob_grad = nt(qkv_ref[2, :stop, :], mixed_grad)
            dots = jnp.sum(prob_grad * probs, axis=0, keepdims=True)
            score_grad = (probs * (prob_grad - dots)).astype(LOW)
            dkv[1, :stop, :] += nn(probs.astype(LOW), mixed_grad)
            dkv[0, :stop, :] += nn(score_grad, query)
            return dq + tn(score_grad, qkv_ref[1, :stop, :] * lanes)

        dq = jnp.zeros((size, local_width), FULL)
        dq = lax.fori_loop(0, heads, backward_head, dq)
        dlow[0, start:stop, :] = (dq * HEAD_DIM ** (-0.5)).astype(LOW)

    @pl.loop(0, BLOCKS)
    def _(turn_number):
        number = top - turn_number
        rows = rows_at(number)

        @pl.when(number > 0)
        def _():
            hidden_sum.finish(number - 1)

        hidden_sum.arrived(number)
        normed, inverse = summed(number)
        grad = h_total[number].reshape(size, width).astype(FULL)
        vacc[1:2, :] += jnp.sum(grad * normed, axis=0, keepdims=True)
        scaled = grad * gain_row
        back = inverse * (scaled - normed * jnp.mean(scaled * normed, axis=-1, keepdims=True))
        back_low = back.astype(LOW)
        dz_ref[rows, :] = back_low
        gate = gate_of(x_ref[rows, :].astype(FULL), router_row)
        attn = (gate * dy_ref[rows, :].astype(FULL) + back_low.astype(FULL)).astype(LOW)
        do_ref[...] = nn(attn, w4[3]).astype(LOW)
        out_acc[...] += tn(attn, o_ref[rows, :])

        @pl.when(turn_number > 0)
        def _():
            input_sum.cross(number + 1)

        for block in range(BLOCKS):

            @pl.when(number == block)
            def _():
                backward_rows(block)

        dlow[1, rows, :] = dkv[0, rows, :].astype(LOW)
        dlow[2, rows, :] = dkv[1, rows, :].astype(LOW)
        part_sum = nt(dlow[0, rows, :], w4[0])
        part_sum += nt(dlow[1, rows, :], w4[1])
        part_sum += nt(dlow[2, rows, :], w4[2])
        heads_sum.drain(number)
        input_sum.put(number, part_sum)
        if joined:
            for when, k, which in ((0, 2, (1, 2)), (1, 2, range(3, line + 1)), (2, 1, (1, 2)), (3, 1, (3,))):

                @pl.when(turn_number == when)
                def _():
                    relay(k, *which)

    input_sum.cross(0)

    blocks = [tn(kept_all(0), dlow[t]) for t in range(3)]
    blocks.append(out_acc[...])
    keep(0, jnp.concatenate(blocks, axis=1))
    give(0)

    def rows_out(which, number):
        held, target = ((m_total, y_any), (d_total, dx_any))[which]
        return pltpu.make_async_copy(
            held.at[number], target.at[number], row_sems.at[which, number]
        )

    branch_sum.finish(top)
    input_sum.finish(top)

    @pl.loop(0, BLOCKS)
    def _(turn_number):
        number = top - turn_number
        rows = rows_at(number)

        @pl.when(number > 0)
        def _():
            branch_sum.finish(number - 1)
            input_sum.finish(number - 1)

        if joined:
            for when, k, which in (
                (0, 1, range(4, line + 1)),
                (1, 0, (1,)),
                (2, 0, range(2, line)),
                (3, 0, (line,)),
            ):

                @pl.when(turn_number == when)
                def _():
                    relay(k, *which)
                    if k == 0 and 0 < when < 3:
                        collect(3 - when)

        branch_sum.arrived(number)
        x_rows, normed, inverse = first_norm(number)
        dy_rows = dy_ref[rows, :].astype(FULL)
        added = a_total[number].reshape(size, width).astype(FULL)
        added = added + m_total[number].reshape(size, width).astype(FULL)
        gate = gate_of(x_rows, router_row)
        gate_grad = jnp.sum(dy_rows * added, axis=-1, keepdims=True)
        logit_grad = gate_grad * gate * (1.0 - gate) * width ** (-0.5)
        branch_sum.drain(number)
        m_total[number] = (x_rows + gate * added).astype(LOW).reshape(2, size // 2, width)
        rows_out(0, number).start()
        input_sum.arrived(number)
        grad = d_total[number].reshape(size, width).astype(FULL)
        vacc[0:1, :] += jnp.sum(grad * normed, axis=0, keepdims=True)
        vacc[2:3, :] += jnp.sum(logit_grad * x_rows, axis=0, keepdims=True)
        scaled = grad * first_gain
        back = inverse * (scaled - normed * jnp.mean(scaled * normed, axis=-1, keepdims=True))
        dx_rows = dy_rows + dz_ref[rows, :].astype(FULL) + back + logit_grad * router_row
        input_sum.drain(number)
        d_total[number] = dx_rows.astype(LOW).reshape(2, size // 2, width)
        rows_out(1, number).start()

    if joined:
        for d in range(groups):
            vpad[d, :, :share] = vacc[:, d * share : (d + 1) * share]
        for j in range(1, groups):
            to_all(j).start()
        collect(0)
        total = vpad[me]
        for j in range(1, groups):
            to_all(j).wait_recv()
            total = total + vr[j - 1]
        vsum_ref[...] = total
        for k in range(5):
            drain_weights(k)
        for k in range(3):
            for j in range(1, line + 1):
                to_pair(k, j).wait_send()
            for j in range(1, line):
                to_line(k, j).wait_send()
        for j in range(1, groups):
            to_all(j).wait_send()
    else:
        vsum_ref[...] = vacc[...]

    @pl.loop(0, BLOCKS)
    def _(number):
        hidden_sum.drain(number)
        rows_out(0, number).wait()
        rows_out(1, number).wait()


def adam_update(master, first_moment, second_moment, gradient, step_rate, decay_rate):
    first_new = MOMENT_DECAY * first_moment + (1.0 - MOMENT_DECAY) * gradient
    second_new = SQUARE_DECAY * second_moment + (1.0 - SQUARE_DECAY) * gradient * gradient
    first_hat = first_new / (1.0 - MOMENT_DECAY**STEP)
    second_hat = second_new / (1.0 - SQUARE_DECAY**STEP)
    master_new = master - step_rate * (
        first_hat / (jnp.sqrt(second_hat) + ADAM_EPS) + decay_rate * master
    )
    return (master_new, first_new, second_new)


def last_kernel(cap_ref, sel_ref, vsum_ref, *refs):
    vec_old, (tok, cot, y, dx, gsum), olds, refs = refs[:3], refs[3:8], refs[8:20], refs[20:]
    vec_new, (out, grad), news, refs = refs[:3], refs[3:5], refs[5:17], refs[17:]
    (tok_b, cot_b, y_b, dx_b, gsum_b), olds_b, (out_b, grad_b), news_b = (
        refs[:5],
        refs[5:17],
        refs[17:19],
        refs[19:31],
    )
    row_sems, in_sems, out_sems, done_sems = refs[31:]
    slots, width = y_b.shape
    seq_len = tok_b.shape[0]
    rows = min(SPOT_ROWS, seq_len)
    chunks = seq_len // rows

    small = [pltpu.make_async_copy(gsum, gsum_b, in_sems.at[0])]
    small += [
        pltpu.make_async_copy(old, old_b, in_sems.at[3 + i])
        for i, (old, old_b) in enumerate(zip(olds, olds_b))
    ]
    placed = [
        pltpu.make_async_copy(y, y_b, in_sems.at[1]),
        pltpu.make_async_copy(dx, dx_b, in_sems.at[2]),
    ]
    finished = [
        pltpu.make_async_copy(new_b, new, done_sems.at[i])
        for i, (new, new_b) in enumerate(zip(news, news_b))
    ]

    def part(number):
        return pl.ds(pl.multiple_of(number * rows, rows), rows)

    def load(which, number):
        source, target = ((tok, tok_b), (cot, cot_b))[which]
        return pltpu.make_async_copy(
            source.at[part(number)], target.at[part(number)], row_sems.at[which, number]
        )

    def store(which, number):
        source, target = ((out_b, out), (grad_b, grad))[which]
        return pltpu.make_async_copy(
            source.at[part(number)], target.at[part(number)], out_sems.at[which, number]
        )

    for copy in small[:1] + small[1:] + placed:
        copy.start()

    @pl.loop(0, chunks)
    def _(number):
        load(0, number).start()
        load(1, number).start()

    for copy in small:
        copy.wait()
    local_width = olds_b[0].shape[-1]
    share = vec_old[0].shape[1]
    first = gsum_b[0]
    parts = [first[:, t * local_width : (t + 1) * local_width] for t in range(4)]
    for t in range(3):
        old = [olds_b[4 * i][t] for i in range(3)]
        for i, value in enumerate(adam_update(*old, parts[t], RATE_MATRIX, WEIGHT_DECAY)):
            news_b[4 * i][t] = value
    for number, gradient in ((1, parts[3].T), (2, gsum_b[1]), (3, gsum_b[2])):
        old = [olds_b[number + 4 * i][...] for i in range(3)]
        for i, value in enumerate(adam_update(*old, gradient, RATE_MATRIX, WEIGHT_DECAY)):
            news_b[number + 4 * i][...] = value
    for copy in finished:
        copy.start()
    values = adam_update(*[ref[...] for ref in vec_old], vsum_ref[0:3, :share], RATE_VECTOR, 0.0)
    for ref, value in zip(vec_new, values):
        ref[...] = value

    for copy in placed:
        copy.wait()
    ids = lax.broadcasted_iota(jnp.int32, (1, slots), 1)
    chosen = jnp.where(ids < cap_ref[lax.axis_index("dp")], sel_ref[...], -1)

    @pl.loop(0, chunks)
    def _(number):
        load(0, number).wait()
        load(1, number).wait()
        spots = number * rows + lax.broadcasted_iota(jnp.int32, (rows, slots), 0)
        hot = (spots == chosen).astype(FULL)
        hit = jnp.max(hot, axis=-1, keepdims=True) > 0.5
        hot = hot.astype(LOW)
        kept_rows = tok_b[part(number), :].astype(FULL)
        out_b[part(number), :] = jnp.where(hit, nn(hot, y_b[...]), kept_rows).astype(LOW)
        store(0, number).start()
        kept_rows = cot_b[part(number), :].astype(FULL)
        grad_b[part(number), :] = jnp.where(hit, nn(hot, dx_b[...]), kept_rows)
        store(1, number).start()

    for copy in finished:
        copy.wait()

    @pl.loop(0, chunks)
    def _(number):
        store(0, number).wait()
        store(1, number).wait()


def shape(dims, kind):
    return jax.ShapeDtypeStruct(dims, kind)


IN_VMEM = pl.BlockSpec(memory_space=pltpu.VMEM)
IN_SMEM = pl.BlockSpec(memory_space=pltpu.SMEM)
IN_ANY = pl.BlockSpec(memory_space=pl.ANY)
DMA = pltpu.SemaphoreType.DMA


def params(number=None):
    if number is None:
        return pltpu.CompilerParams(vmem_limit_bytes=VMEM_BYTES)
    return pltpu.CompilerParams(
        vmem_limit_bytes=VMEM_BYTES, collective_id=number, has_side_effects=True
    )


def local(
    tokens,
    cotangent,
    capacity,
    selected,
    qkv_master,
    out_master,
    up_master,
    down_master,
    vec_master,
    qkv_first,
    out_first,
    up_first,
    down_first,
    vec_first,
    qkv_second,
    out_second,
    up_second,
    down_second,
    vec_second,
):
    groups = lax.axis_size("dp")
    me = lax.axis_index("dp")
    share, local_width = qkv_master.shape[1:]
    hidden = up_master.shape[1]
    width = tokens.shape[2]
    seq_len = tokens.shape[1]
    slots = selected.shape[1]
    joined = share % 32 == 0 and groups % 2 == 0 and groups >= 8
    token_rows, cot_rows = tokens[0], cotangent[0]
    line = groups // 2

    quarter = slots // BLOCKS
    half_block = pltpu.VMEM((BLOCKS, quarter // 2, width), LOW)
    both_halves = pltpu.VMEM((BLOCKS, 2, quarter // 2, width), LOW)
    hops = DMA((2, 3, BLOCKS))
    exchange = [both_halves, half_block, half_block, half_block]
    scratch = [
        both_halves,
        both_halves,
        DMA((2, BLOCKS)),
        pltpu.VMEM((2, seq_len, width), LOW),
        DMA((2,)),
        pltpu.VMEM((slots, width), LOW),
        pltpu.VMEM((slots, width), LOW),
        pltpu.VMEM((3, slots, local_width), LOW),
        pltpu.VMEM((slots, local_width), LOW),
        pltpu.VMEM((4, width, local_width), LOW),
        *exchange,
        both_halves,
        hops,
        hops,
        *exchange,
        both_halves,
        hops,
        *exchange,
        hops,
        pltpu.VMEM((slots, hidden), LOW),
        pltpu.VMEM((slots, width), LOW),
        pltpu.VMEM((width, local_width), FULL),
        pltpu.VMEM((2, slots, local_width), FULL),
        pltpu.VMEM((3, slots, local_width), LOW),
        pltpu.VMEM((8, width), FULL),
        pltpu.VMEM((slots, 1), jnp.int32),
        pltpu.VMEM((quarter, local_width), LOW),
    ]
    if joined:
        weights = (qkv_master, out_master, up_master, down_master.T, vec_master)
        scratch += [
            pltpu.VMEM((3, groups, share, width), LOW),
            pltpu.VMEM((8, width), FULL),
            pltpu.VMEM((groups, 8, 128), FULL),
            DMA((5, line - 1)),
            DMA((5, line - 1)),
            DMA((5, line - 1)),
            DMA((5, line - 1)),
            DMA((5, line)),
            DMA((5, line)),
            DMA((5,)),
            DMA((5,)),
            pltpu.VMEM((3, groups, share, width), LOW),
            pltpu.VMEM((3, line, share, width), LOW),
            pltpu.VMEM((3, line, share, width), LOW),
            pltpu.VMEM((3, line - 1, share, width), LOW),
            pltpu.VMEM((groups, 8, 128), FULL),
            pltpu.VMEM((groups - 1, 8, 128), FULL),
            DMA((3, line)),
            DMA((3, line)),
            DMA((3, line - 1)),
            DMA((3, line - 1)),
            DMA((groups - 1,)),
            DMA((groups - 1,)),
        ]
    else:
        first_shard = jnp.concatenate(
            [qkv_master[0], qkv_master[1], qkv_master[2], out_master.T], axis=1
        )
        shard = jnp.stack([first_shard, up_master, down_master.T]).astype(LOW)
        vectors = lax.all_gather(vec_master.astype(LOW), "dp", axis=1, tiled=True)
        weights = (
            lax.all_gather(shard, "dp", axis=1, tiled=True),
            jnp.pad(vectors.astype(FULL), ((0, 5), (0, 0))),
        )
    y_rows, dx_rows, grad_sum, vec_sum = pl.pallas_call(
        functools.partial(main_kernel, groups, joined),
        out_shape=[
            shape((BLOCKS, 2, quarter // 2, width), LOW),
            shape((BLOCKS, 2, quarter // 2, width), LOW),
            shape((3, share if joined else width, width), FULL),
            shape((8, 128 if joined else width), FULL),
        ],
        in_specs=[IN_SMEM, IN_VMEM, IN_ANY, IN_ANY] + [IN_VMEM] * len(weights),
        out_specs=[IN_ANY] * 2 + [IN_VMEM] * 2,
        scratch_shapes=scratch,
        compiler_params=params(0),
        name="main",
    )(capacity, selected, token_rows, cot_rows, *weights)
    y_rows, dx_rows = (rows.reshape(slots, width) for rows in (y_rows, dx_rows))

    if not joined:
        grad_sum = lax.psum_scatter(grad_sum, "dp", scatter_dimension=1, tiled=True)
        vec_sum = lax.psum_scatter(vec_sum, "dp", scatter_dimension=1, tiled=True)
    olds = (
        qkv_master, out_master, up_master, down_master.T,
        qkv_first, out_first, up_first, down_first.T,
        qkv_second, out_second, up_second, down_second.T,
    )
    vec_olds = (vec_master, vec_first, vec_second)
    ones = (token_rows, cot_rows, y_rows, dx_rows, grad_sum)
    made = [shape((seq_len, width), LOW), shape((seq_len, width), FULL)]
    made += [shape(old.shape, FULL) for old in olds]
    chunks = seq_len // min(SPOT_ROWS, seq_len)
    *vec_news, block_out, input_grad, q0, o0, u0, d0, q1, o1, u1, d1, q2, o2, u2, d2 = pl.pallas_call(
        last_kernel,
        out_shape=[shape(old.shape, FULL) for old in vec_olds] + made,
        in_specs=[IN_SMEM] + [IN_VMEM] * 5 + [IN_ANY] * 17,
        out_specs=[IN_VMEM] * 3 + [IN_ANY] * 14,
        scratch_shapes=[pltpu.VMEM(array.shape, array.dtype) for array in (*ones, *olds, *made)]
        + [DMA((2, chunks)), DMA((15,)), DMA((2, chunks)), DMA((12,))],
        compiler_params=params(),
        name="last",
    )(capacity, selected, vec_sum, *vec_olds, *ones, *olds)
    v0, v1, v2 = vec_news
    return (
        block_out[None], input_grad[None],
        q0, o0, u0, d0.T, v0, q1, o1, u1, d1.T, v1, q2, o2, u2, d2.T, v2,
    )


def solution(mesh):
    weights = (
        P(None, "dp", "mp"),
        P("mp", "dp"),
        P("dp", "mp"),
        P("mp", "dp"),
        P(None, "dp"),
    )
    rows = (P("dp", None, None), P("dp", None, None))
    return jax.shard_map(
        local,
        mesh=mesh,
        in_specs=(*rows, P(), P("dp", None), *weights * 3),
        out_specs=(*rows, *weights * 3),
        check_vma=False,
    )
```

```python
import functools

import jax
import jax.numpy as jnp
from jax import lax
from jax.experimental import pallas as pl
from jax.experimental.pallas import tpu as pltpu
from jax.sharding import PartitionSpec as P

HEAD_DIM = 64
STEP = 10
NORM_EPS = 1e-05
MASKED_SCORE = -1000000000.0
MOMENT_DECAY = 0.9
SQUARE_DECAY = 0.95
ADAM_EPS = 1e-08
WEIGHT_DECAY = 0.1
RATE_MATRIX = 0.06
RATE_VECTOR = 0.2

LOW = jnp.bfloat16
FULL = jnp.float32
MESH = pl.DeviceIdType.MESH
BLOCKS = 4
AROUND = (3,)
SPOT_ROWS = 512
VMEM_BYTES = 60 * 2**20


def nn(a, b):
    return lax.dot_general(a, b, (((1,), (0,)), ((), ())), preferred_element_type=FULL)


def nt(a, b):
    return lax.dot_general(a, b, (((1,), (1,)), ((), ())), preferred_element_type=FULL)


def tn(a, b):
    return lax.dot_general(a, b, (((0,), (0,)), ((), ())), preferred_element_type=FULL)


def mean_square_inverse(values):
    return lax.rsqrt(jnp.mean(values * values, axis=-1, keepdims=True) + NORM_EPS)


def gate_of(rows, router_row):
    width = rows.shape[-1]
    logit = jnp.sum(rows * router_row, axis=-1, keepdims=True) * width ** (-0.5)
    return jax.nn.sigmoid(logit)


def greet(partners):
    barrier = pltpu.get_barrier_semaphore()
    for partner in partners:
        pl.semaphore_signal(barrier, inc=1, device_id=partner, device_id_type=MESH)


def met(partners):
    pl.semaphore_wait(pltpu.get_barrier_semaphore(), len(partners))


def remote(src, dst, send_sem, recv_sem, device):
    return pltpu.make_async_remote_copy(
        src_ref=src,
        dst_ref=dst,
        send_sem=send_sem,
        recv_sem=recv_sem,
        device_id=device,
        device_id_type=MESH,
    )


class Exchange:
    def __init__(self, parts, near, pair, far, total, sems):
        self.parts, self.near, self.pair, self.far, self.total = parts, near, pair, far, total
        self.sems = sems
        self.me, self.part = lax.axis_index("dp"), lax.axis_index("mp")
        self.half = self.part % 2
        self.near_device = (self.me, self.part + 1 - 2 * self.half)
        self.far_device = (self.me, (self.part + 2) % 4)

    def copy(self, which, block, src, dst):
        device = self.far_device if which == 1 else self.near_device
        return remote(src, dst, self.sems.at[0, which, block], self.sems.at[1, which, block], device)

    def out(self, which, block):
        if which == 0:
            return self.copy(0, block, self.parts.at[block, 1 - self.half], self.near.at[block])
        if which == 1:
            return self.copy(1, block, self.pair.at[block], self.far.at[block])
        spot = self.total.at[block, self.half]
        return self.copy(2, block, spot, spot)

    def into(self, which, block):
        spot = (self.near.at[block], self.far.at[block], self.total.at[block, 1 - self.half])[which]
        return self.copy(which, block, spot, spot)

    def put(self, block, value):
        rows, width = value.shape
        self.parts[block] = value.astype(LOW).reshape(2, rows // 2, width)
        self.send(block)

    def send(self, block):
        self.out(0, block).start()

    def cross(self, block):
        self.into(0, block).wait_recv()
        self.pair[block] = (
            self.parts[block, self.half].astype(FULL) + self.near[block].astype(FULL)
        ).astype(LOW)
        self.out(1, block).start()

    def finish(self, block):
        self.into(1, block).wait_recv()
        self.total[block, self.half] = (
            self.pair[block].astype(FULL) + self.far[block].astype(FULL)
        ).astype(LOW)
        self.out(2, block).start()

    def arrived(self, block):
        self.into(2, block).wait_recv()

    def drain(self, block):
        for which in range(3):
            self.out(which, block).wait_send()


def head_lanes(width, head):
    lanes = lax.broadcasted_iota(jnp.int32, (1, width), 1)
    return (lanes // HEAD_DIM == head).astype(FULL).astype(LOW)


def main_kernel(groups, joined, *refs):
    (cap_ref, sel_ref, tok_any, cot_any), refs = refs[:4], refs[4:]
    if joined:
        masters, refs = refs[:5], refs[5:]
    else:
        (wg, gains), refs = refs[:2], refs[2:]
    (y_any, dx_any, gsum_ref, vsum_ref), refs = refs[:4], refs[4:]
    (m_total, d_total, row_sems), refs = refs[:3], refs[3:]
    (table, table_sems, x_ref, dy_ref, qkv_ref, o_ref, w4), refs = refs[:7], refs[7:]
    (parts, near, pair, far, a_total, a_sems, d_sems), refs = refs[:7], refs[7:]
    (h_parts, h_near, h_pair, h_far, h_total, h_sems), refs = refs[:6], refs[6:]
    (m_parts, m_near, m_pair, m_far, m_sems), refs = refs[:5], refs[5:]
    (slope_ref, dz_ref, out_acc, dkv, dlow, vacc, spot_ref, do_ref), refs = refs[:8], refs[8:]

    slots, width = x_ref.shape
    seq_len = tok_any.shape[0]
    local_width = o_ref.shape[1]
    heads = local_width // HEAD_DIM
    size = slots // BLOCKS
    me, part = lax.axis_index("dp"), lax.axis_index("mp")
    count = cap_ref[me]
    top = BLOCKS - 1

    def span(start):
        return pl.ds(pl.multiple_of(start, size), size)

    def rows_at(number):
        return span(number * size)

    def table_copy(which, source):
        return pltpu.make_async_copy(source, table.at[which], table_sems.at[which])

    table_copy(0, tok_any).start()
    table_copy(1, cot_any).start()

    heads_sum = Exchange(parts, near, pair, far, a_total, a_sems)
    hidden_sum = Exchange(h_parts, h_near, h_pair, h_far, h_total, h_sems)
    branch_sum = Exchange(m_parts, m_near, m_pair, m_far, m_total, m_sems)
    input_sum = Exchange(parts, near, pair, far, d_total, d_sems)
    partners = [heads_sum.near_device, heads_sum.far_device]

    if joined:
        (wg, gains, vg, send_r, recv_r, send_l, recv_l, send_f, recv_f), refs = refs[:9], refs[9:]
        (send_e, recv_e), refs = refs[:2], refs[2:]
        (grads, ry, pairs, rz, vpad, vr), refs = refs[:6], refs[6:]
        send_y, recv_y, send_z, recv_z, send_v, recv_v = refs
        line, place, side = groups // 2, me // 2, me % 2
        other = (me + 1 - 2 * side, part)
        everyone = [(lax.rem(me + j, groups), part) for j in range(1, groups)]

        half_share = width // groups // 2

        def slot(k, d):
            if k < 2:
                return wg.at[0, d, pl.ds(k * half_share, half_share)]
            return vg.at[d] if k == 4 else wg.at[k - 1, d]

        def chain(k, step, right):
            z = place - step + 1 if right else place + step - 1
            sems = (send_r, recv_r) if right else (send_l, recv_l)
            target = (me + 2 if right else me - 2, part)
            return remote(
                slot(k, z * 2 + side),
                slot(k, z * 2 + side),
                sems[0].at[k, step - 1],
                sems[1].at[k, step - 1],
                target,
            )

        def chain_in(k, step, right):
            z = place - step if right else place + step
            sems = (send_r, recv_r) if right else (send_l, recv_l)
            spot = slot(k, z * 2 + side)
            return remote(spot, spot, sems[0].at[k, step - 1], sems[1].at[k, step - 1], other)

        def can_send(step, right):
            if right:
                return (place + 1 < line) & (place - step + 1 >= 0)
            return (place >= 1) & (place + step - 1 < line)

        def across(k, z):
            spot = slot(k, z * 2 + side)
            return remote(spot, spot, send_f.at[k, z], recv_f.at[k, z], other)

        def across_in(k, z):
            spot = slot(k, z * 2 + 1 - side)
            return remote(spot, spot, send_f.at[k, z], recv_f.at[k, z], other)

        def begin_line(k):
            for right in (True, False):

                @pl.when(can_send(1, right))
                def _():
                    chain(k, 1, right).start()

        def begin_across(k):
            across(k, place).start()

        def round_about(k, z):
            if k not in AROUND:
                return False
            return ((place == 0) & (z == 1)) | ((place == line - 1) & (z == line - 2))

        def around(k, right):
            spot = slot(k, me + 1 - 2 * side)
            target = (me + 2 if right else me - 2, part)
            return remote(spot, spot, send_e.at[k], recv_e.at[k], target)

        def around_in(k, right):
            spot = slot(k, (me - 2 if right else me + 2) + 1 - 2 * side)
            return remote(spot, spot, send_e.at[k], recv_e.at[k], other)

        def turn(k):
            across_in(k, place).wait_recv()

            @pl.when(place == 1)
            def _():
                around(k, False).start()

            @pl.when(place == line - 2)
            def _():
                around(k, True).start()

        def pump(k, step):
            for right in (True, False):
                z = place - step if right else place + step

                @pl.when((z >= 0) & (z < line))
                def _():
                    chain_in(k, step, right).wait_recv()

                    if k in AROUND:

                        @pl.when(jnp.logical_not(round_about(k, z)))
                        def _():
                            across(k, z).start()

                    else:
                        across(k, z).start()

                if step + 1 < line:

                    @pl.when(can_send(step + 1, right))
                    def _():
                        chain(k, step + 1, right).start()

        def arrive(k):
            for z in range(line):
                if k in AROUND:

                    @pl.when(jnp.logical_not(round_about(k, z)) & (place != z))
                    def _():
                        across_in(k, z).wait_recv()

                else:
                    across_in(k, z).wait_recv()
            if k in AROUND:

                @pl.when(place == 0)
                def _():
                    around_in(k, False).wait_recv()

                @pl.when(place == line - 1)
                def _():
                    around_in(k, True).wait_recv()

        def drain_weights(k):
            for right in (True, False):
                for step in range(1, line):

                    @pl.when(can_send(step, right))
                    def _():
                        chain(k, step, right).wait_send()

            for z in range(line):
                if k in AROUND:

                    @pl.when(jnp.logical_not(round_about(k, z)))
                    def _():
                        across(k, z).wait_send()

                else:
                    across(k, z).wait_send()
            if k in AROUND:

                @pl.when(place == 1)
                def _():
                    around(k, False).wait_send()

                @pl.when(place == line - 2)
                def _():
                    around(k, True).wait_send()

        def plane(j):
            return lax.rem(place + j, line)

        def to_pair(k, j):
            spot = plane(j) * 2 + 1 - side
            return remote(
                grads.at[k, spot], ry.at[k, j - 1], send_y.at[k, j - 1], recv_y.at[k, j - 1], other
            )

        def to_line(k, j):
            return remote(
                pairs.at[k, j - 1],
                rz.at[k, j - 1],
                send_z.at[k, j - 1],
                recv_z.at[k, j - 1],
                (plane(j) * 2 + side, part),
            )

        def keep(k, value):
            grads[k] = value.astype(LOW).reshape(groups, width // groups, width)

        def give(k):
            for j in range(1, line + 1):
                to_pair(k, j).start()

        def relay(k, *which):
            for j in which:
                to_pair(k, j).wait_recv()
                own = grads[k, plane(j) * 2 + side].astype(FULL)
                pairs[k, j - 1] = (own + ry[k, j - 1].astype(FULL)).astype(LOW)
                if j < line:
                    to_line(k, j).start()

        def collect(k):
            total = pairs[k, line - 1].astype(FULL)
            for j in range(1, line):
                to_line(k, j).wait_recv()
                total = total + rz[k, j - 1].astype(FULL)
            gsum_ref[k] = total

        def to_all(j):
            target = lax.rem(me + j, groups)
            return remote(
                vpad.at[target], vr.at[j - 1], send_v.at[j - 1], recv_v.at[j - 1], (target, part)
            )

        greet(partners + everyone)
        qkv_m, out_m, up_m, down_m, vec_m = masters
        share = width // groups
        vg[me] = jnp.zeros((8, 128), FULL)
        vg[me, 0:3, :share] = vec_m[...].astype(LOW).astype(FULL)
        columns = [qkv_m[t] for t in range(3)] + [out_m[...].T]
        wg[0, me] = jnp.concatenate(columns, axis=1).astype(LOW)
        met(partners + everyone)
        for k in (0, 4, 1):
            begin_line(k)
            begin_across(k)
        wg[1, me] = up_m[...].astype(LOW)
        wg[2, me] = down_m[...].astype(LOW)
    else:
        greet(partners)
        met(partners)

        def keep(k, value):
            gsum_ref[k] = value

        def give(k):
            pass

        def relay(k, *which):
            pass

    def advance(*steps):
        if not joined:
            return
        for k, number in steps:
            last = line - 1
            for step in range(number, last + 1 if number == 3 else number + 1):
                pump(k, step)
                if k == 0:
                    pump(4, step)
                if k == 0 and step == 2:
                    begin_line(2)
                if k == 0 and step == last:
                    begin_across(2)
                if k == 1 and step == last:
                    begin_across(3)
                if k == 2 and step == 1:
                    begin_line(3)
                if step == 1 and k in AROUND:
                    turn(k)

    sel_column = jnp.broadcast_to(sel_ref[...].astype(FULL), (8, slots)).T[:, 0:1].astype(jnp.int32)
    spot_ref[...] = sel_column

    def pick(number, which, dead_zero, out_ref):
        block = 2 * size
        rows = pl.ds(pl.multiple_of(number * block, block), block)
        spots = lax.broadcasted_iota(jnp.int32, (block, seq_len), 1)
        hot = (spots == spot_ref[rows, :]).astype(FULL).astype(LOW)
        got = nn(hot, table[which])
        if dead_zero:
            ids = number * block + lax.broadcasted_iota(jnp.int32, (block, 1), 0)
            got = jnp.where(ids < count, got, 0.0)
        out_ref[rows, :] = got.astype(LOW)

    table_copy(0, tok_any).wait()

    @pl.loop(0, 2)
    def _(number):
        pick(number, 0, False, x_ref)

    advance((0, 1))
    table_copy(1, cot_any).wait()

    @pl.loop(0, 2)
    def _(number):
        pick(number, 1, True, dy_ref)

        @pl.when(number == 0)
        def _():
            advance((1, 1))

    advance((0, 2), (1, 2), (0, 3), (1, 3), (2, 1))

    if joined:
        arrive(4)
        gains[...] = jnp.concatenate([vg[d][:, :share] for d in range(groups)], axis=1)

    first_gain, gain_row, router_row = gains[0:1, :], gains[1:2, :], gains[2:3, :]

    def weight(k):
        return wg[k].reshape(width, wg.shape[-1])

    def first_norm(number):
        x_rows = x_ref[rows_at(number), :].astype(FULL)
        inverse = mean_square_inverse(x_rows)
        return x_rows, x_rows * inverse, inverse

    for number in range(BLOCKS):
        table[0, number * size : (number + 1) * size, :] = (
            first_norm(number)[1] * first_gain
        ).astype(LOW)
    if joined:
        arrive(0)
        arrive(1)
        advance((2, 2))
    w_first = weight(0)
    for t in range(4):
        w4[t] = w_first[:, t * local_width : (t + 1) * local_width]
    for t in range(3):
        qkv_ref[t] = nn(table[0, :slots, :], w4[t]).astype(LOW)

    def forward_rows(block):
        start, stop = block * size, (block + 1) * size
        own = start + lax.broadcasted_iota(jnp.int32, (size, 1), 0)
        keys = lax.broadcasted_iota(jnp.int32, (size, stop), 1)
        allowed = keys <= jnp.minimum(own, count - 1)

        def forward_head(head, mixed):
            lanes = head_lanes(local_width, head)
            query = qkv_ref[0, start:stop, :] * (lanes * HEAD_DIM ** (-0.5))
            scores = nt(query, qkv_ref[1, :stop, :])
            scores = jnp.where(allowed, scores, MASKED_SCORE)
            terms = jnp.exp(scores - jnp.max(scores, axis=-1, keepdims=True))
            inverse = 1.0 / jnp.sum(terms, axis=-1, keepdims=True)
            probs = (terms * inverse).astype(LOW)
            return mixed + nn(probs, qkv_ref[2, :stop, :] * lanes)

        mixed = jnp.zeros((size, local_width), FULL)
        for head in range(heads):
            mixed = forward_head(head, mixed)
        o_ref[start:stop, :] = mixed.astype(LOW)

    @pl.loop(0, BLOCKS)
    def _(turn_number):
        number = top - turn_number

        @pl.when(turn_number > 0)
        def _():
            heads_sum.cross(number + 1)

        @pl.when(turn_number == 1)
        def _():
            advance((3, 1), (2, 3))

        @pl.when(turn_number == 2)
        def _():
            advance((3, 2))

        for block in range(BLOCKS):

            @pl.when(number == block)
            def _():
                forward_rows(block)

        heads_sum.put(number, nt(o_ref[rows_at(number), :], w4[3]))

    heads_sum.cross(0)
    advance((3, 3))

    def summed(number):
        attended = a_total[number].reshape(size, width).astype(FULL)
        x_rows = x_ref[rows_at(number), :].astype(FULL)
        summed_rows = (x_rows + attended).astype(LOW).astype(FULL)
        inverse = mean_square_inverse(summed_rows)
        return summed_rows * inverse, inverse

    def kept(which, number):
        return which // 2, span((which % 2) * slots + number * size)

    def kept_all(which):
        return table[which // 2, (which % 2) * slots : (which % 2 + 1) * slots, :]

    def up_phase(number):
        heads_sum.arrived(number)
        inner = (summed(number)[0] * gain_row).astype(LOW)
        up = nn(inner, weight(1))
        square = up * up
        bent = jnp.tanh(0.7978845608028654 * (up + 0.044715 * square * up))
        half = 0.5 * (1.0 + bent)
        which, spot = kept(0, number)
        table[which, spot, :] = (up * half).astype(LOW)
        which, spot = kept(1, number)
        table[which, spot, :] = inner
        slope = half + 0.5 * up * (1.0 - bent * bent) * (
            0.7978845608028654 * (1.0 + 3.0 * 0.044715 * square)
        )
        slope_ref[rows_at(number), :] = slope.astype(LOW)
        rows = rows_at(number)
        gate = gate_of(x_ref[rows, :].astype(FULL), router_row)
        which, spot = kept(2, number)
        table[which, spot, :] = (gate * dy_ref[rows, :].astype(FULL)).astype(LOW)

    def back_phase(number):
        rows = rows_at(number)
        which, spot = kept(2, number)
        up_low = (nn(table[which, spot, :], weight(2)) * slope_ref[rows, :].astype(FULL)).astype(LOW)
        which, spot = kept(3, number)
        table[which, spot, :] = up_low
        hidden_sum.put(number, nt(table[which, spot, :], weight(1)))

    def put_branch(number):
        which, spot = kept(0, number)
        branch_sum.put(number, nt(table[which, spot, :], weight(2)))

    heads_sum.finish(top)
    if joined:
        arrive(2)

    @pl.loop(0, BLOCKS + 1)
    def _(turn_number):
        number = top - turn_number

        @pl.when(turn_number > 1)
        def _():
            hidden_sum.cross(number + 2)

        @pl.when(turn_number == 2)
        def _():
            branch_sum.cross(top)

        @pl.when(turn_number < BLOCKS)
        def _():
            up_phase(number)

            @pl.when(number > 0)
            def _():
                heads_sum.finish(number - 1)

        if joined:

            @pl.when(turn_number == 1)
            def _():
                arrive(3)

        @pl.when(turn_number == BLOCKS)
        def _():
            keep(2, tn(kept_all(2), kept_all(0)))
            give(2)

        @pl.when(turn_number > 0)
        def _():
            back_phase(number + 1)

        @pl.when((turn_number > 0) & (turn_number < 3))
        def _():
            put_branch(number + 1)

    hidden_sum.cross(0)
    branch_sum.cross(top - 1)
    keep(1, tn(kept_all(1), kept_all(3)))
    give(1)
    for number in range(top - 1):
        put_branch(top - 2 - number)
    for number in range(top - 1):
        branch_sum.cross(top - 2 - number)

    @pl.loop(0, BLOCKS)
    def _(number):
        which, spot = kept(0, number)
        table[which, spot, :] = (first_norm(number)[1] * first_gain).astype(LOW)

    out_acc[...] = jnp.zeros_like(out_acc)
    dkv[...] = jnp.zeros_like(dkv)
    vacc[...] = jnp.zeros_like(vacc)
    hidden_sum.finish(top)

    def backward_rows(block):
        start, stop = block * size, (block + 1) * size
        own = start + lax.broadcasted_iota(jnp.int32, (1, size), 1)
        keys = lax.broadcasted_iota(jnp.int32, (stop, size), 0)
        allowed = keys <= jnp.minimum(own, count - 1)

        def backward_head(head, dq):
            lanes = head_lanes(local_width, head)
            query = qkv_ref[0, start:stop, :] * (lanes * HEAD_DIM ** (-0.5))
            mixed_grad = do_ref[...] * lanes
            scores = nt(qkv_ref[1, :stop, :], query)
            scores = jnp.where(allowed, scores, MASKED_SCORE)
            terms = jnp.exp(scores - jnp.max(scores, axis=0, keepdims=True))
            total = 1.0 / jnp.sum(terms, axis=0, keepdims=True)
            probs = terms * total
            prob_grad = nt(qkv_ref[2, :stop, :], mixed_grad)
            dots = jnp.sum(prob_grad * probs, axis=0, keepdims=True)
            score_grad = (probs * (prob_grad - dots)).astype(LOW)
            dkv[1, :stop, :] += nn(probs.astype(LOW), mixed_grad)
            dkv[0, :stop, :] += nn(score_grad, query)
            return dq + tn(score_grad, qkv_ref[1, :stop, :] * lanes)

        dq = jnp.zeros((size, local_width), FULL)
        dq = lax.fori_loop(0, heads, backward_head, dq)
        dlow[0, start:stop, :] = (dq * HEAD_DIM ** (-0.5)).astype(LOW)

    @pl.loop(0, BLOCKS)
    def _(turn_number):
        number = top - turn_number
        rows = rows_at(number)

        @pl.when(number > 0)
        def _():
            hidden_sum.finish(number - 1)

        hidden_sum.arrived(number)
        normed, inverse = summed(number)
        grad = h_total[number].reshape(size, width).astype(FULL)
        vacc[1:2, :] += jnp.sum(grad * normed, axis=0, keepdims=True)
        scaled = grad * gain_row
        back = inverse * (scaled - normed * jnp.mean(scaled * normed, axis=-1, keepdims=True))
        back_low = back.astype(LOW)
        dz_ref[rows, :] = back_low
        gate = gate_of(x_ref[rows, :].astype(FULL), router_row)
        attn = (gate * dy_ref[rows, :].astype(FULL) + back_low.astype(FULL)).astype(LOW)
        do_ref[...] = nn(attn, w4[3]).astype(LOW)
        out_acc[...] += tn(attn, o_ref[rows, :])

        @pl.when(turn_number > 0)
        def _():
            input_sum.cross(number + 1)

        for block in range(BLOCKS):

            @pl.when(number == block)
            def _():
                backward_rows(block)

        dlow[1, rows, :] = dkv[0, rows, :].astype(LOW)
        dlow[2, rows, :] = dkv[1, rows, :].astype(LOW)
        part_sum = nt(dlow[0, rows, :], w4[0])
        part_sum += nt(dlow[1, rows, :], w4[1])
        part_sum += nt(dlow[2, rows, :], w4[2])
        heads_sum.drain(number)
        input_sum.put(number, part_sum)
        if joined:
            for when, k, which in ((0, 2, (1, 2)), (1, 2, range(3, line + 1)), (2, 1, (1, 2)), (3, 1, (3,))):

                @pl.when(turn_number == when)
                def _():
                    relay(k, *which)

    input_sum.cross(0)

    blocks = [tn(kept_all(0), dlow[t]) for t in range(3)]
    blocks.append(out_acc[...])
    keep(0, jnp.concatenate(blocks, axis=1))
    give(0)

    def rows_out(which, number):
        held, target = ((m_total, y_any), (d_total, dx_any))[which]
        return pltpu.make_async_copy(
            held.at[number], target.at[number], row_sems.at[which, number]
        )

    branch_sum.finish(top)
    input_sum.finish(top)

    @pl.loop(0, BLOCKS)
    def _(turn_number):
        number = top - turn_number
        rows = rows_at(number)

        @pl.when(number > 0)
        def _():
            branch_sum.finish(number - 1)
            input_sum.finish(number - 1)

        if joined:
            for when, k, which in (
                (0, 1, range(4, line + 1)),
                (1, 0, (1,)),
                (2, 0, range(2, line)),
                (3, 0, (line,)),
            ):

                @pl.when(turn_number == when)
                def _():
                    relay(k, *which)
                    if k == 0 and 0 < when < 3:
                        collect(3 - when)

        branch_sum.arrived(number)
        x_rows, normed, inverse = first_norm(number)
        dy_rows = dy_ref[rows, :].astype(FULL)
        added = a_total[number].reshape(size, width).astype(FULL)
        added = added + m_total[number].reshape(size, width).astype(FULL)
        gate = gate_of(x_rows, router_row)
        gate_grad = jnp.sum(dy_rows * added, axis=-1, keepdims=True)
        logit_grad = gate_grad * gate * (1.0 - gate) * width ** (-0.5)
        branch_sum.drain(number)
        m_total[number] = (x_rows + gate * added).astype(LOW).reshape(2, size // 2, width)
        rows_out(0, number).start()
        input_sum.arrived(number)
        grad = d_total[number].reshape(size, width).astype(FULL)
        vacc[0:1, :] += jnp.sum(grad * normed, axis=0, keepdims=True)
        vacc[2:3, :] += jnp.sum(logit_grad * x_rows, axis=0, keepdims=True)
        scaled = grad * first_gain
        back = inverse * (scaled - normed * jnp.mean(scaled * normed, axis=-1, keepdims=True))
        dx_rows = dy_rows + dz_ref[rows, :].astype(FULL) + back + logit_grad * router_row
        input_sum.drain(number)
        d_total[number] = dx_rows.astype(LOW).reshape(2, size // 2, width)
        rows_out(1, number).start()

    if joined:
        for d in range(groups):
            vpad[d, :, :share] = vacc[:, d * share : (d + 1) * share]
        for j in range(1, groups):
            to_all(j).start()
        collect(0)
        total = vpad[me]
        for j in range(1, groups):
            to_all(j).wait_recv()
            total = total + vr[j - 1]
        vsum_ref[...] = total
        for k in range(5):
            drain_weights(k)
        for k in range(3):
            for j in range(1, line + 1):
                to_pair(k, j).wait_send()
            for j in range(1, line):
                to_line(k, j).wait_send()
        for j in range(1, groups):
            to_all(j).wait_send()
    else:
        vsum_ref[...] = vacc[...]

    @pl.loop(0, BLOCKS)
    def _(number):
        hidden_sum.drain(number)
        rows_out(0, number).wait()
        rows_out(1, number).wait()


def adam_update(master, first_moment, second_moment, gradient, step_rate, decay_rate):
    first_new = MOMENT_DECAY * first_moment + (1.0 - MOMENT_DECAY) * gradient
    second_new = SQUARE_DECAY * second_moment + (1.0 - SQUARE_DECAY) * gradient * gradient
    first_hat = first_new / (1.0 - MOMENT_DECAY**STEP)
    second_hat = second_new / (1.0 - SQUARE_DECAY**STEP)
    master_new = master - step_rate * (
        first_hat / (jnp.sqrt(second_hat) + ADAM_EPS) + decay_rate * master
    )
    return (master_new, first_new, second_new)


def last_kernel(cap_ref, sel_ref, vsum_ref, *refs):
    vec_old, (tok, cot, y, dx, gsum), olds, refs = refs[:3], refs[3:8], refs[8:20], refs[20:]
    vec_new, (out, grad), news, refs = refs[:3], refs[3:5], refs[5:17], refs[17:]
    (tok_b, cot_b, y_b, dx_b, gsum_b), olds_b, (out_b, grad_b), news_b = (
        refs[:5],
        refs[5:17],
        refs[17:19],
        refs[19:31],
    )
    row_sems, in_sems, out_sems, done_sems = refs[31:]
    slots, width = y_b.shape
    seq_len = tok_b.shape[0]
    rows = min(SPOT_ROWS, seq_len)
    chunks = seq_len // rows

    small = [pltpu.make_async_copy(gsum, gsum_b, in_sems.at[0])]
    small += [
        pltpu.make_async_copy(old, old_b, in_sems.at[3 + i])
        for i, (old, old_b) in enumerate(zip(olds, olds_b))
    ]
    placed = [
        pltpu.make_async_copy(y, y_b, in_sems.at[1]),
        pltpu.make_async_copy(dx, dx_b, in_sems.at[2]),
    ]
    finished = [
        pltpu.make_async_copy(new_b, new, done_sems.at[i])
        for i, (new, new_b) in enumerate(zip(news, news_b))
    ]

    def part(number):
        return pl.ds(pl.multiple_of(number * rows, rows), rows)

    def load(which, number):
        source, target = ((tok, tok_b), (cot, cot_b))[which]
        return pltpu.make_async_copy(
            source.at[part(number)], target.at[part(number)], row_sems.at[which, number]
        )

    def store(which, number):
        source, target = ((out_b, out), (grad_b, grad))[which]
        return pltpu.make_async_copy(
            source.at[part(number)], target.at[part(number)], out_sems.at[which, number]
        )

    for copy in placed:
        copy.start()

    @pl.loop(0, chunks)
    def _(number):
        load(0, number).start()
        load(1, number).start()

        @pl.when(number == 0)
        def _():
            for copy in small:
                copy.start()

    def update():
        for copy in small:
            copy.wait()
        local_width = olds_b[0].shape[-1]
        share = vec_old[0].shape[1]
        first = gsum_b[0]
        parts = [first[:, t * local_width : (t + 1) * local_width] for t in range(4)]
        for t in range(3):
            old = [olds_b[4 * i][t] for i in range(3)]
            for i, value in enumerate(adam_update(*old, parts[t], RATE_MATRIX, WEIGHT_DECAY)):
                news_b[4 * i][t] = value
        for number, gradient in ((1, parts[3].T), (2, gsum_b[1]), (3, gsum_b[2])):
            old = [olds_b[number + 4 * i][...] for i in range(3)]
            for i, value in enumerate(adam_update(*old, gradient, RATE_MATRIX, WEIGHT_DECAY)):
                news_b[number + 4 * i][...] = value
        for copy in finished:
            copy.start()
        values = adam_update(*[ref[...] for ref in vec_old], vsum_ref[0:3, :share], RATE_VECTOR, 0.0)
        for ref, value in zip(vec_new, values):
            ref[...] = value

    for copy in placed:
        copy.wait()
    ids = lax.broadcasted_iota(jnp.int32, (1, slots), 1)
    chosen = jnp.where(ids < cap_ref[lax.axis_index("dp")], sel_ref[...], -1)

    @pl.loop(0, chunks)
    def _(number):
        load(0, number).wait()
        load(1, number).wait()
        spots = number * rows + lax.broadcasted_iota(jnp.int32, (rows, slots), 0)
        hot = (spots == chosen).astype(FULL)
        hit = jnp.max(hot, axis=-1, keepdims=True) > 0.5
        hot = hot.astype(LOW)
        kept_rows = tok_b[part(number), :].astype(FULL)
        out_b[part(number), :] = jnp.where(hit, nn(hot, y_b[...]), kept_rows).astype(LOW)
        store(0, number).start()
        kept_rows = cot_b[part(number), :].astype(FULL)
        grad_b[part(number), :] = jnp.where(hit, nn(hot, dx_b[...]), kept_rows)
        store(1, number).start()

        @pl.when(number == 0)
        def _():
            update()

    for copy in finished:
        copy.wait()

    @pl.loop(0, chunks)
    def _(number):
        store(0, number).wait()
        store(1, number).wait()


def shape(dims, kind):
    return jax.ShapeDtypeStruct(dims, kind)


IN_VMEM = pl.BlockSpec(memory_space=pltpu.VMEM)
IN_SMEM = pl.BlockSpec(memory_space=pltpu.SMEM)
IN_ANY = pl.BlockSpec(memory_space=pl.ANY)
DMA = pltpu.SemaphoreType.DMA


def params(number=None):
    if number is None:
        return pltpu.CompilerParams(vmem_limit_bytes=VMEM_BYTES)
    return pltpu.CompilerParams(
        vmem_limit_bytes=VMEM_BYTES, collective_id=number, has_side_effects=True
    )


def local(
    tokens,
    cotangent,
    capacity,
    selected,
    qkv_master,
    out_master,
    up_master,
    down_master,
    vec_master,
    qkv_first,
    out_first,
    up_first,
    down_first,
    vec_first,
    qkv_second,
    out_second,
    up_second,
    down_second,
    vec_second,
):
    groups = lax.axis_size("dp")
    me = lax.axis_index("dp")
    share, local_width = qkv_master.shape[1:]
    hidden = up_master.shape[1]
    width = tokens.shape[2]
    seq_len = tokens.shape[1]
    slots = selected.shape[1]
    joined = share % 32 == 0 and groups % 2 == 0 and groups >= 8
    token_rows, cot_rows = tokens[0], cotangent[0]
    line = groups // 2

    quarter = slots // BLOCKS
    half_block = pltpu.VMEM((BLOCKS, quarter // 2, width), LOW)
    both_halves = pltpu.VMEM((BLOCKS, 2, quarter // 2, width), LOW)
    hops = DMA((2, 3, BLOCKS))
    exchange = [both_halves, half_block, half_block, half_block]
    scratch = [
        both_halves,
        both_halves,
        DMA((2, BLOCKS)),
        pltpu.VMEM((2, seq_len, width), LOW),
        DMA((2,)),
        pltpu.VMEM((slots, width), LOW),
        pltpu.VMEM((slots, width), LOW),
        pltpu.VMEM((3, slots, local_width), LOW),
        pltpu.VMEM((slots, local_width), LOW),
        pltpu.VMEM((4, width, local_width), LOW),
        *exchange,
        both_halves,
        hops,
        hops,
        *exchange,
        both_halves,
        hops,
        *exchange,
        hops,
        pltpu.VMEM((slots, hidden), LOW),
        pltpu.VMEM((slots, width), LOW),
        pltpu.VMEM((width, local_width), FULL),
        pltpu.VMEM((2, slots, local_width), FULL),
        pltpu.VMEM((3, slots, local_width), LOW),
        pltpu.VMEM((8, width), FULL),
        pltpu.VMEM((slots, 1), jnp.int32),
        pltpu.VMEM((quarter, local_width), LOW),
    ]
    if joined:
        weights = (qkv_master, out_master, up_master, down_master.T, vec_master)
        scratch += [
            pltpu.VMEM((3, groups, share, width), LOW),
            pltpu.VMEM((8, width), FULL),
            pltpu.VMEM((groups, 8, 128), FULL),
            DMA((5, line - 1)),
            DMA((5, line - 1)),
            DMA((5, line - 1)),
            DMA((5, line - 1)),
            DMA((5, line)),
            DMA((5, line)),
            DMA((5,)),
            DMA((5,)),
            pltpu.VMEM((3, groups, share, width), LOW),
            pltpu.VMEM((3, line, share, width), LOW),
            pltpu.VMEM((3, line, share, width), LOW),
            pltpu.VMEM((3, line - 1, share, width), LOW),
            pltpu.VMEM((groups, 8, 128), FULL),
            pltpu.VMEM((groups - 1, 8, 128), FULL),
            DMA((3, line)),
            DMA((3, line)),
            DMA((3, line - 1)),
            DMA((3, line - 1)),
            DMA((groups - 1,)),
            DMA((groups - 1,)),
        ]
    else:
        first_shard = jnp.concatenate(
            [qkv_master[0], qkv_master[1], qkv_master[2], out_master.T], axis=1
        )
        shard = jnp.stack([first_shard, up_master, down_master.T]).astype(LOW)
        vectors = lax.all_gather(vec_master.astype(LOW), "dp", axis=1, tiled=True)
        weights = (
            lax.all_gather(shard, "dp", axis=1, tiled=True),
            jnp.pad(vectors.astype(FULL), ((0, 5), (0, 0))),
        )
    y_rows, dx_rows, grad_sum, vec_sum = pl.pallas_call(
        functools.partial(main_kernel, groups, joined),
        out_shape=[
            shape((BLOCKS, 2, quarter // 2, width), LOW),
            shape((BLOCKS, 2, quarter // 2, width), LOW),
            shape((3, share if joined else width, width), FULL),
            shape((8, 128 if joined else width), FULL),
        ],
        in_specs=[IN_SMEM, IN_VMEM, IN_ANY, IN_ANY] + [IN_VMEM] * len(weights),
        out_specs=[IN_ANY] * 2 + [IN_VMEM] * 2,
        scratch_shapes=scratch,
        compiler_params=params(0),
        name="main",
    )(capacity, selected, token_rows, cot_rows, *weights)
    y_rows, dx_rows = (rows.reshape(slots, width) for rows in (y_rows, dx_rows))

    if not joined:
        grad_sum = lax.psum_scatter(grad_sum, "dp", scatter_dimension=1, tiled=True)
        vec_sum = lax.psum_scatter(vec_sum, "dp", scatter_dimension=1, tiled=True)
    olds = (
        qkv_master, out_master, up_master, down_master.T,
        qkv_first, out_first, up_first, down_first.T,
        qkv_second, out_second, up_second, down_second.T,
    )
    vec_olds = (vec_master, vec_first, vec_second)
    ones = (token_rows, cot_rows, y_rows, dx_rows, grad_sum)
    made = [shape((seq_len, width), LOW), shape((seq_len, width), FULL)]
    made += [shape(old.shape, FULL) for old in olds]
    chunks = seq_len // min(SPOT_ROWS, seq_len)
    *vec_news, block_out, input_grad, q0, o0, u0, d0, q1, o1, u1, d1, q2, o2, u2, d2 = pl.pallas_call(
        last_kernel,
        out_shape=[shape(old.shape, FULL) for old in vec_olds] + made,
        in_specs=[IN_SMEM] + [IN_VMEM] * 5 + [IN_ANY] * 17,
        out_specs=[IN_VMEM] * 3 + [IN_ANY] * 14,
        scratch_shapes=[pltpu.VMEM(array.shape, array.dtype) for array in (*ones, *olds, *made)]
        + [DMA((2, chunks)), DMA((15,)), DMA((2, chunks)), DMA((12,))],
        compiler_params=params(),
        name="last",
    )(capacity, selected, vec_sum, *vec_olds, *ones, *olds)
    v0, v1, v2 = vec_news
    return (
        block_out[None], input_grad[None],
        q0, o0, u0, d0.T, v0, q1, o1, u1, d1.T, v1, q2, o2, u2, d2.T, v2,
    )


def solution(mesh):
    weights = (
        P(None, "dp", "mp"),
        P("mp", "dp"),
        P("dp", "mp"),
        P("mp", "dp"),
        P(None, "dp"),
    )
    rows = (P("dp", None, None), P("dp", None, None))
    return jax.shard_map(
        local,
        mesh=mesh,
        in_specs=(*rows, P(), P("dp", None), *weights * 3),
        out_specs=(*rows, *weights * 3),
        check_vma=False,
    )
```
